32 devices in a mesh: dp: 8 (over y, x, core), seq: 4 (over z).
Axes of the slice: x: 2, y: 2, z: 4, core: 2. Of those that a mesh axis runs over, the one named last changes fastest.
Arguments:
- activations: bfloat16 [16, 2048, 512], P('dp', 'seq'), may hold values from -6 to 6
- qkv_weight: bfloat16 [512, 1536], P('dp'), may hold values from -0.25 to 0.25
- attn_weight: bfloat16 [512, 512], P('dp'), may hold values from -1 to 1
- router_weight: bfloat16 [512, 8], P('dp'), may hold values from -0.125 to 0.125
- gain_one: bfloat16 [512], P('dp'), may hold values from 0.099609375 to 1.8984375
- gain_two: bfloat16 [512], P('dp'), may hold values from 0.099609375 to 1.8984375
- expert_in: bfloat16 [2048, 8, 512], P(('dp', 'seq')), may hold values from -0.25 to 0.25
- expert_out: bfloat16 [2048, 8, 512], P(('dp', 'seq')), may hold values from -0.125 to 0.125
- segments: int32 [16, 2048], P('dp', 'seq'), may hold values from 0 to 15, as said below
- task_ids: int32 [16, 2048], P('dp', 'seq'), may hold values from 0 to 15, as said below
- task_experts: int32 [16, 2], replicated, may hold values from 0 to 7, all different within a row
- out_grad: float32 [16, 2048, 512], P('dp', 'seq'), may hold values from -6 to 6
Outputs:
- outputs: bfloat16 [16, 2048, 512], P('dp', 'seq')
- input_grad: float32 [16, 2048, 512], P('dp', 'seq')
- qkv_grad: float32 [512, 1536], P('dp')
- attn_grad: float32 [512, 512], P('dp')
- router_grad: float32 [512, 8], P('dp')
- gain_one_grad: float32 [512], P('dp')
- gain_two_grad: float32 [512], P('dp')
- expert_in_grad: float32 [2048, 8, 512], P(('dp', 'seq'))
- expert_out_grad: float32 [2048, 8, 512], P(('dp', 'seq'))
The draws below stay inside these ranges and needn't reach their ends.
Inputs may be any that keep to these rules, and one draw needn't show every extreme that they name: `segments`: segment numbers never fall along a pack and reach 15 in every draw; tokens attend only to tokens of their own pack with the same number; one pack of each index of dp is a single segment in every draw. `task_ids`: all tokens of a pack share one task; the 2 packs of one index of dp hold one or two tasks.
All inputs are finite; a program needn't handle non-finite values.
Results may differ from the reference program's by a relative error of at most 0.015.
Values may be sent and summed in bfloat16 or wider, within the bound.
A program may use at most 320 MiB of HBM per device.

```python
import jax
import jax.numpy as jnp
from jax import lax

D = 512
HEADS = 8
HEAD = 64
FF = 2048
EXPERTS = 8
TASKS = 16
PACKS_DEV = 2
PACK_LEN = 2048
PACKS = 16


def draw_segments(key, part):
    key = jax.random.fold_in(key, 11)
    cut_key, whole_key = jax.random.split(key)
    positions = jnp.arange(PACK_LEN)
    boundary = (jax.random.randint(cut_key, (PACKS, PACK_LEN), 0, PACK_LEN) < 3).astype(jnp.int32)
    boundary = boundary * (positions > 0).astype(jnp.int32)[None, :]
    groups = PACKS // PACKS_DEV
    chosen = jax.random.randint(whole_key, (groups,), 0, PACKS_DEV)
    pack_pos = jnp.arange(PACKS) % PACKS_DEV
    whole_pack = pack_pos == jnp.repeat(chosen, PACKS_DEV)
    boundary = jnp.where(whole_pack[:, None], 0, boundary)
    even_cuts = ((positions % (PACK_LEN // 16) == 0) & (positions > 0)).astype(jnp.int32)
    full_pack = jnp.arange(PACKS) == (chosen[0] + 1) % PACKS_DEV
    boundary = jnp.where(full_pack[:, None], even_cuts[None, :], boundary)
    return jnp.minimum(jnp.cumsum(boundary, axis=1), 15).astype(jnp.int32)


def draw_task_ids(key, part):
    key = jax.random.fold_in(key, 23)
    first_key, second_key, cut_key, pair_key = jax.random.split(key, 4)
    groups = PACKS // PACKS_DEV
    first_task = jax.random.randint(first_key, (groups,), 0, TASKS)
    second_task = (first_task + jax.random.randint(second_key, (groups,), 1, TASKS)) % TASKS
    cut_point = jax.random.randint(cut_key, (groups,), 1, PACKS_DEV)
    two_tasks = jax.random.randint(pair_key, (groups,), 0, 2)
    group_ids = jnp.arange(groups)
    two_tasks = jnp.where(group_ids == 0, 1, jnp.where(group_ids == 1, 0, two_tasks))
    slot_pos = jnp.arange(PACKS) % PACKS_DEV
    owner_group = jnp.arange(PACKS) // PACKS_DEV
    use_second = (slot_pos >= cut_point[owner_group]) & (two_tasks[owner_group] == 1)
    pack_task = jnp.where(use_second, second_task[owner_group], first_task[owner_group])
    return jnp.broadcast_to(pack_task[:, None], (PACKS, PACK_LEN)).astype(jnp.int32)


def steps_of(key, shape, shards, least, high):
    factor_of = 1.0
    for dim, parts in shards:
        draws = jax.random.uniform(jax.random.fold_in(jax.random.fold_in(key, 6), dim), (parts,), jnp.float32, least / len(shards), high / len(shards))
        factor_of = factor_of * jnp.repeat(jnp.exp(draws), shape[dim] // parts).reshape((-1,) + (1,) * (len(shape) - 1 - dim))
    return factor_of


def distinct(stream_key, rows, count, top, lift):
    sequence = jax.random.permutation(jax.random.fold_in(stream_key, 1), count)
    pull = sequence
    for power in range(3):
        pull = pull * pull // count
    pull = pull * lift // count
    tickets = jax.random.randint(jax.random.fold_in(stream_key, 2), (rows, count), 0, 4096) + pull
    holders = jax.random.permutation(jax.random.fold_in(stream_key, 3), rows)[jnp.arange(count) % rows]
    tickets = jnp.where(jnp.arange(rows)[:, None] == holders[None, :], 1 << 14, tickets)
    score = tickets * count + jnp.arange(count)
    return lax.top_k(score.astype(jnp.int32), top)[1].astype(jnp.int32)


def gaussian(own_key, dims, scale, bound, cuts=(), held_as=jnp.bfloat16):
    factor_of = steps_of(own_key, dims, cuts, -0.22, 0.18) if cuts else 1.0
    entries = jax.random.normal(own_key, dims, jnp.float32) * scale * factor_of
    return jnp.minimum(jnp.maximum(entries, -bound), bound).astype(held_as)


def setup_inputs(seed: int = 0) -> dict:
    arg_keys = jax.random.split(jax.random.key(seed), 13)
    activations = gaussian(arg_keys[0], (PACKS, PACK_LEN, D), 1.0, 6.0, ((0, 8), (1, 4)))
    qkv_weight = gaussian(arg_keys[1], (D, 3 * D), D ** -0.5, 0.25, ((0, 8),))
    attn_weight = gaussian(arg_keys[2], (D, D), (D // 16) ** -0.5, 1.0, ((0, 8),))
    router_weight = gaussian(arg_keys[3], (D, EXPERTS), (4 * D) ** -0.5, 0.125, ((0, 8),))
    gain_one = jnp.clip(1.0 + 0.18 * jax.random.normal(arg_keys[4], (D,), jnp.float32), 0.099609375, 1.8984375).astype(jnp.bfloat16)
    gain_two = jnp.clip(1.0 + 0.18 * jax.random.normal(arg_keys[5], (D,), jnp.float32), 0.099609375, 1.8984375).astype(jnp.bfloat16)
    expert_in = gaussian(arg_keys[6], (FF, EXPERTS, D), D ** -0.5, 0.25, ((0, 32),))
    expert_out = gaussian(arg_keys[7], (FF, EXPERTS, D), FF ** -0.5, 0.125, ((0, 32),))
    segments = draw_segments(jax.random.fold_in(arg_keys[12], 71), 0)
    task_ids = draw_task_ids(jax.random.fold_in(arg_keys[12], 71), 0)
    task_experts = distinct(arg_keys[10], TASKS, EXPERTS, 2, 2048)
    out_grad = gaussian(arg_keys[11], (PACKS, PACK_LEN, D), 1.0, 6.0, ((0, 8), (1, 4)), jnp.float32)
    return {"activations": activations, "qkv_weight": qkv_weight, "attn_weight": attn_weight, "router_weight": router_weight, "gain_one": gain_one, "gain_two": gain_two, "expert_in": expert_in, "expert_out": expert_out, "segments": segments, "task_ids": task_ids, "task_experts": task_experts, "out_grad": out_grad}


@jax.custom_vjp
def low(v):
    return lax.optimization_barrier(v.astype(jnp.bfloat16)).astype(jnp.float32)

@jax.custom_vjp
def low_back(v):
    return v

def low_keep(v):
    return (low(v), None)

def low_pass(kept, grad):
    return (grad,)

def back_keep(v):
    return (v, None)

def back_low(kept, grad):
    return (low(grad),)
low.defvjp(low_keep, low_pass)
low_back.defvjp(back_keep, back_low)

def product(left, right):
    return jnp.dot(left, right, precision=lax.Precision.HIGHEST)

def layer_norm(values, gain_vec):
    center = values - lax.optimization_barrier(jnp.mean(values, axis=-1, keepdims=True))
    variance = lax.optimization_barrier(jnp.mean(center * center, axis=-1, keepdims=True))
    return center * lax.rsqrt(variance + 1e-05) * gain_vec

def pack_layer(block_item, params, task_experts):
    inputs, seg_pack, task_pack = block_item
    qkv_weight, attn_weight, router_weight, gain_one, gain_two, expert_in, expert_out = params
    length = inputs.shape[0]
    normed_one = low(layer_norm(inputs, gain_one))
    qkv_rows = low(low_back(product(normed_one, qkv_weight))).reshape(length, 3, HEADS, HEAD)
    queries = qkv_rows[:, 0]
    key_rows = qkv_rows[:, 1]
    value_rows = qkv_rows[:, 2]
    raw_scores = jnp.einsum('ihc,jhc->hij', queries, key_rows, precision=lax.Precision.HIGHEST) * HEAD ** (-0.5)
    same_doc = seg_pack[:, None] == seg_pack[None, :]
    scores = jnp.where(same_doc[None], low_back(raw_scores), -1000000000.0)
    probs = low(jax.nn.softmax(scores, axis=-1))
    mixed_out = jnp.einsum('hij,jhc->ihc', probs, value_rows, precision=lax.Precision.HIGHEST).reshape(length, HEADS * HEAD)
    attended = low(low_back(mixed_out))
    residual = inputs + low_back(product(attended, attn_weight))
    normed_two = low(layer_norm(residual, gain_two))
    logits = product(normed_two, router_weight)
    pair_ids = task_experts[task_pack[0]]
    gate_vals = jax.nn.softmax(jnp.take(logits, pair_ids, axis=1), axis=-1)
    summed = residual
    for slot_pos in range(2):
        weight_in = jnp.take(expert_in, pair_ids[slot_pos], axis=1)
        weight_out = jnp.take(expert_out, pair_ids[slot_pos], axis=1)
        pre_act = low_back(jnp.dot(normed_two, weight_in.T, precision=lax.Precision.HIGHEST))
        hidden = low(jax.nn.gelu(pre_act, approximate=False))
        summed = summed + gate_vals[:, slot_pos:slot_pos + 1] * low_back(product(hidden, weight_out))
    return summed

def reference(activations, qkv_weight, attn_weight, router_weight, gain_one, gain_two, expert_in, expert_out, segments, task_ids, task_experts, out_grad):
    params = tuple((array_in.astype(jnp.float32) for array_in in (qkv_weight, attn_weight, router_weight, gain_one, gain_two, expert_in, expert_out)))
    inputs = activations.astype(jnp.float32)

    def forward(inputs, params):

        def single(block_item):
            return pack_layer(block_item, params, task_experts)
        return lax.map(jax.checkpoint(single), (inputs, segments, task_ids))
    outputs, pullback = jax.vjp(forward, inputs, params)
    input_grad, param_grads = pullback(out_grad)
    return (outputs.astype(jnp.bfloat16), input_grad, param_grads[0], param_grads[1], param_grads[2], param_grads[3], param_grads[4], param_grads[5], param_grads[6])
```

```python
import functools

import jax
import jax.numpy as jnp
from jax import lax
from jax.experimental import pallas as pl
from jax.experimental.pallas import tpu as pltpu
from jax.sharding import PartitionSpec as P

HEAD = 64
LANES = 128
SEG_COL = HEAD
LSE_COL = HEAD + 16
SEGMENTS = 16
FAR = 1e9
VMEM = 56 << 20
NT = (((1,), (1,)), ((), ()))
TN = (((0,), (0,)), ((), ()))
F32 = jnp.float32
LOW = jnp.bfloat16


def dot(a, b):
    return jnp.dot(a, b, preferred_element_type=F32)


def dot_nt(a, b):
    return lax.dot_general(a, b, NT, preferred_element_type=F32)


def dot_tn(a, b):
    return lax.dot_general(a, b, TN, preferred_element_type=F32)


def thirds(values):
    high = values.astype(LOW).astype(F32)
    rest = values - high
    mid = rest.astype(LOW).astype(F32)
    return high, mid, rest - mid


def lanes_of(shape):
    return lax.broadcasted_iota(jnp.int32, shape, len(shape) - 1)


def put_thirds(base, values, column):
    lane = lanes_of(base.shape)
    high, mid, last = thirds(values)
    base = jnp.where(lane == column, high, base)
    base = jnp.where(lane == column + 1, mid, base)
    return jnp.where(lane == column + 2, last, base)


def normalize(values):
    center = values - jnp.mean(values, axis=-1, keepdims=True)
    inverse = lax.rsqrt(jnp.mean(center * center, axis=-1, keepdims=True) + 1e-05)
    return center * inverse, inverse


def norm_backward(upstream, scaled, inverse, gain_vec):
    direct = upstream * gain_vec
    return inverse * (
        direct
        - jnp.mean(direct, axis=-1, keepdims=True)
        - scaled * jnp.mean(direct * scaled, axis=-1, keepdims=True)
    )


def params(limit=VMEM):
    return pltpu.CompilerParams(vmem_limit_bytes=limit)


def whole(*shape):
    return pl.BlockSpec(shape, lambda *_: (0,) * len(shape))


def select_kernel(ids, win, wout, out):
    def body(i, carry):
        out[i, 0] = win[ids[i]]
        out[i, 1] = wout[ids[i]]
        return carry

    lax.fori_loop(0, out.shape[0], body, 0)


def select_weights(ids, win, wout):
    experts, rows, width = win.shape
    count = ids.shape[0]
    return pl.pallas_call(
        select_kernel,
        grid_spec=pltpu.PrefetchScalarGridSpec(
            num_scalar_prefetch=1,
            grid=(1,),
            in_specs=[whole(experts, rows, width)] * 2,
            out_specs=whole(count, 2, rows, width),
        ),
        out_shape=jax.ShapeDtypeStruct((count, 2, rows, width), LOW),
        compiler_params=params(),
        name="select_weights",
    )(ids, win, wout)


def collect_kernel(ids, grads, out_in, out_out, acc_in, acc_out):
    acc_in[...] = jnp.zeros_like(acc_in)
    acc_out[...] = jnp.zeros_like(acc_out)

    def body(i, carry):
        acc_in[ids[i]] += grads[i, 0].astype(F32)
        acc_out[ids[i]] += grads[i, 1].astype(F32)
        return carry

    lax.fori_loop(0, grads.shape[0], body, 0)
    for e in range(acc_in.shape[0]):
        out_in[:, e, :] = acc_in[e]
        out_out[:, e, :] = acc_out[e]


def collect_grads(ids, grads, experts):
    count, _, rows, width = grads.shape
    shape = jax.ShapeDtypeStruct((rows, experts, width), F32)
    return pl.pallas_call(
        collect_kernel,
        grid_spec=pltpu.PrefetchScalarGridSpec(
            num_scalar_prefetch=1,
            grid=(1,),
            in_specs=[whole(*grads.shape)],
            out_specs=[whole(rows, experts, width)] * 2,
            scratch_shapes=[pltpu.VMEM((experts, rows, width), F32)] * 2,
        ),
        out_shape=[shape, shape],
        compiler_params=params(),
        name="collect_grads",
    )(ids, grads)


def project_kernel(heads, x, seg, gain, weight, normed, qa, ka, va):
    scaled, _ = normalize(x[...].astype(F32))
    low = (scaled * gain[...]).astype(LOW)
    normed[...] = low
    rows = dot(low, weight[...])
    lane = lanes_of((x.shape[0], LANES))
    same = (lane - SEG_COL) == seg[...]
    in_seg = (lane >= SEG_COL) & (lane < SEG_COL + SEGMENTS)
    q_more = jnp.where(same, 1.0, 0.0)
    k_more = jnp.where(in_seg & jnp.logical_not(same), -FAR, 0.0)
    k_more = jnp.where((lane >= LSE_COL) & (lane < LSE_COL + 3), 1.0, k_more)
    v_more = jnp.where((lane >= HEAD) & (lane < HEAD + 3), 1.0, 0.0)
    for h in range(heads):
        at = h * LANES
        step = heads * LANES
        query = rows[:, at : at + LANES].astype(LOW).astype(F32) * HEAD**-0.5
        qa[h] = (query + q_more).astype(LOW)
        ka[h] = (rows[:, at + step : at + step + LANES] + k_more).astype(LOW)
        va[h] = (rows[:, at + 2 * step : at + 2 * step + LANES] + v_more).astype(LOW)


def project(x, seg, gain, weight, heads, block):
    tokens, width = x.shape
    wide = jax.ShapeDtypeStruct((heads, tokens, LANES), LOW)
    spec = pl.BlockSpec((heads, block, LANES), lambda i: (0, i, 0))
    row = pl.BlockSpec((block, width), lambda i: (i, 0))
    return pl.pallas_call(
        functools.partial(project_kernel, heads),
        grid=(tokens // block,),
        in_specs=[
            row,
            pl.BlockSpec((block, 1), lambda i: (i, 0)),
            whole(1, width),
            whole(*weight.shape),
        ],
        out_specs=[row, spec, spec, spec],
        out_shape=[jax.ShapeDtypeStruct((tokens, width), LOW), wide, wide, wide],
        compiler_params=params(),
        name="project",
    )(x, seg, gain, weight)


def attend_kernel(qa, ka, va, out, lse):
    parts = []
    for h in range(2):
        scores = dot_nt(qa[h], ka[h])
        top = jnp.max(scores, axis=1, keepdims=True)
        probs = jnp.exp(scores - top).astype(LOW)
        mixed = dot(probs, va[h])
        total = mixed[:, HEAD : HEAD + 1]
        parts.append(mixed[:, :HEAD] / total)
        lse[h] = top + jnp.log(total)
    out[...] = jnp.concatenate(parts, axis=1).astype(LOW)


def attend(qa, ka, va, block):
    heads, tokens, _ = qa.shape
    full = pl.BlockSpec((2, tokens, LANES), lambda h, i: (h, 0, 0))
    return pl.pallas_call(
        attend_kernel,
        grid=(heads // 2, tokens // block),
        in_specs=[pl.BlockSpec((2, block, LANES), lambda h, i: (h, i, 0)), full, full],
        out_specs=[
            pl.BlockSpec((block, LANES), lambda h, i: (i, h)),
            pl.BlockSpec((2, block, 1), lambda h, i: (h, i, 0)),
        ],
        out_shape=[
            jax.ShapeDtypeStruct((tokens, heads * HEAD), LOW),
            jax.ShapeDtypeStruct((heads, tokens, 1), F32),
        ],
        compiler_params=params(),
        name="attend",
    )(qa, ka, va)


def attend_back_kernel(block, qa, ka, va, lse, att, grad, dq, dk, dv, qb, gb, dq_acc):
    tokens = qa.shape[1]
    lane = lanes_of((tokens, LANES))
    halves = []
    for h in range(2):
        pair_grad = grad[...].astype(F32)
        inner = pair_grad * att[...].astype(F32)
        if h == 1:
            pair_grad = pltpu.roll(pair_grad, HEAD, 1)
            inner = pltpu.roll(inner, HEAD, 1)
        delta = jnp.sum(jnp.where(lane < HEAD, inner, 0.0), axis=1, keepdims=True)
        gb[...] = put_thirds(jnp.where(lane < HEAD, pair_grad, 0.0), -delta, HEAD).astype(LOW)
        qb[...] = put_thirds(qa[h].astype(F32), -lse[h], LSE_COL).astype(LOW)
        key_t = ka[h].T[:HEAD]
        dq_acc[...] = jnp.zeros_like(dq_acc)
        for i in range(tokens // block):
            r = pl.ds(i * block, block)
            weights = jnp.exp(dot_nt(ka[h, r, :], qb[...]))
            centered = dot_nt(va[h, r, :], gb[...])
            score_grad = (weights * centered).astype(LOW)
            out = pl.ds(h * HEAD, HEAD)
            dv[r, out] = dot(weights.astype(LOW), gb[...])[:, :HEAD].astype(LOW)
            dk[r, out] = dot(score_grad, qb[...])[:, :HEAD].astype(LOW)
            dq_acc[...] += dot(key_t[:, i * block : (i + 1) * block], score_grad)
        halves.append(dq_acc[...].T * HEAD**-0.5)
    dq[...] = jnp.concatenate(halves, axis=1).astype(LOW)


def attend_back(qa, ka, va, lse, att, grad, block):
    heads, tokens, _ = qa.shape
    full = pl.BlockSpec((2, tokens, LANES), lambda h: (h, 0, 0))
    row = pl.BlockSpec((tokens, LANES), lambda h: (0, h))
    shape = jax.ShapeDtypeStruct((tokens, heads * HEAD), LOW)
    return pl.pallas_call(
        functools.partial(attend_back_kernel, block),
        grid=(heads // 2,),
        in_specs=[full, full, full, pl.BlockSpec((2, tokens, 1), lambda h: (h, 0, 0)), row, row],
        out_specs=[row, row, row],
        out_shape=[shape, shape, shape],
        scratch_shapes=[
            pltpu.VMEM((tokens, LANES), LOW),
            pltpu.VMEM((tokens, LANES), LOW),
            pltpu.VMEM((HEAD, tokens), F32),
        ],
        compiler_params=params(),
        name="attend_back",
    )(qa, ka, va, lse, att, grad)


def middle_kernel(ids, x, att, att_far, weight, gain, router, up, res, normed, gates, slot):
    near = weight.shape[0] // 2
    residual = x[...].astype(F32)
    residual += dot(att[...], weight[:near]) + dot(att_far[...], weight[near:])
    res[...] = residual
    scaled, _ = normalize(residual)
    low = (scaled * gain[...]).astype(LOW)
    normed[...] = low
    logits = dot(low, router[...])
    lane = lanes_of(logits.shape)
    mine = jnp.sum(jnp.where(lane == ids[0], logits, 0.0), axis=1, keepdims=True)
    other = jnp.sum(jnp.where(lane == ids[1], logits, 0.0), axis=1, keepdims=True)
    top = jnp.maximum(mine, other)
    mine = jnp.exp(mine - top)
    other = jnp.exp(other - top)
    total = mine + other
    gate = mine / total
    gates[...] = jnp.where(lane == 0, gate, jnp.where(lane == 1, other / total, 0.0))
    slot[...] = (gate * up[...].astype(F32)).astype(LOW)


def middle(ids, x, att, att_far, weight, gain, router, up, block):
    tokens, width = x.shape
    steps = tokens // block
    row = pl.BlockSpec((block, width), lambda i, ids: (i, 0))
    part = pl.BlockSpec((block, att.shape[1]), lambda i, ids: (i, 0))
    far = pl.BlockSpec((block, att.shape[1]), lambda i, ids: ((i + steps // 2) % steps, 0))
    shape = lambda n, t: jax.ShapeDtypeStruct((tokens, n), t)
    return pl.pallas_call(
        middle_kernel,
        grid_spec=pltpu.PrefetchScalarGridSpec(
            num_scalar_prefetch=1,
            grid=(steps,),
            in_specs=[
                row,
                part,
                far,
                whole(*weight.shape),
                whole(1, width),
                whole(*router.shape),
                row,
            ],
            out_specs=[row, row, pl.BlockSpec((block, LANES), lambda i, ids: (i, 0)), row],
        ),
        out_shape=[shape(width, F32), shape(width, LOW), shape(LANES, F32), shape(width, LOW)],
        compiler_params=params(),
        name="middle",
    )(ids, x, att, att_far, weight, gain, router, up)


def expert_kernel(x, slot, up, gates, weight, own, far, grads, out, dx):
    step = pl.program_id(0)

    @pl.when(step == 0)
    def _():
        out[...] = jnp.zeros_like(out)
        dx[...] = jnp.zeros_like(dx)

    sources, _, rows, width = weight.shape
    win = weight[:, 0].reshape(sources * rows, width)
    wout = weight[:, 1].reshape(sources * rows, width)
    pre = dot_nt(x[...], win)
    hidden_grad = dot_nt(slot[...], wout)
    cdf = 0.5 * (1.0 + lax.erf(pre * 0.7071067811865476))
    slope = cdf + pre * jnp.exp(-0.5 * pre * pre) * 0.3989422804014327
    hidden = (pre * cdf).astype(LOW)
    pre_grad = (hidden_grad * slope).astype(LOW)
    out[...] += dot(hidden, wout)
    dx[...] += dot(pre_grad, win)
    grads[:, 0] = dot_tn(pre_grad, x[...]).astype(LOW).reshape(sources, rows, width)
    grads[:, 1] = dot_tn(hidden, slot[...]).astype(LOW).reshape(sources, rows, width)

    @pl.when(step == pl.num_programs(0) - 1)
    def _():
        half = own.shape[0]
        for at in range(0, 2 * half, half // 2):
            r = pl.ds(at, half // 2)
            value = out[r, :]
            gate_grad = jnp.sum(value * up[r, :].astype(F32), axis=1, keepdims=True)
            value = value * gates[r, 0:1]
            tail = jnp.zeros((half // 2, LANES), F32)
            tail = put_thirds(tail, gate_grad, 0)
            target, to = (own, at) if at < half else (far, at - half)
            t = pl.ds(to, half // 2)
            target[t, :width] = value.astype(target.dtype)
            target[t, width : 2 * width] = dx[r, :].astype(target.dtype)
            target[t, 2 * width :] = tail.astype(target.dtype)


def expert(x, slot, up, gates, weight, block):
    tokens, width = x.shape
    count, _, rows, _ = weight.shape
    per = block // rows
    once = lambda *s: pl.BlockSpec(s, lambda i: (0,) * len(s), pipeline_mode=pl.Buffered(1))
    part = pl.BlockSpec((per, 2, rows, width), lambda i: (i, 0, 0, 0))
    half = (tokens // 2, 2 * width + LANES)
    return pl.pallas_call(
        expert_kernel,
        grid=(count // per,),
        in_specs=[
            once(tokens, width),
            once(tokens, width),
            once(tokens, width),
            once(tokens, LANES),
            part,
        ],
        out_specs=[whole(*half), whole(*half), part],
        out_shape=[
            jax.ShapeDtypeStruct(half, F32),
            jax.ShapeDtypeStruct(half, LOW),
            jax.ShapeDtypeStruct(weight.shape, LOW),
        ],
        scratch_shapes=[pltpu.VMEM((tokens, width), F32)] * 2,
        compiler_params=params(60 << 20),
        name="expert",
    )(x, slot, up, gates, weight)


def post_kernel(
    ids, res, own, far, gates, up, normed, att, att_far, weight, gain, router,
    outputs, res_grad, near_grad, far_grad, attn_grad, router_grad, gain_grad,
):
    @pl.when(pl.program_id(0) == 0)
    def _():
        attn_grad[...] = jnp.zeros_like(attn_grad)
        router_grad[...] = jnp.zeros_like(router_grad)
        gain_grad[...] = jnp.zeros_like(gain_grad)

    width = res.shape[1]
    near = weight.shape[0] // 2
    residual = res[...]
    upstream = up[...].astype(F32)
    outputs[...] = (residual + own[:, :width] + far[:, :width].astype(F32)).astype(LOW)
    grad_mine = jnp.sum(own[:, 2 * width :], axis=1, keepdims=True)
    grad_other = jnp.sum(far[:, 2 * width :].astype(F32), axis=1, keepdims=True)
    gate_mine = gates[:, 0:1]
    gate_other = gates[:, 1:2]
    mean = gate_mine * grad_mine + gate_other * grad_other
    lane = lanes_of(gates.shape)
    logit_grad = jnp.where(lane == ids[0], gate_mine * (grad_mine - mean), 0.0)
    logit_grad += jnp.where(lane == ids[1], gate_other * (grad_other - mean), 0.0)
    normed_grad = own[:, width : 2 * width] + far[:, width : 2 * width].astype(F32)
    for part in thirds(logit_grad):
        part = part.astype(LOW)
        router_grad[...] += dot_tn(normed[...], part)
        normed_grad += dot_nt(part, router[...])
    scaled, inverse = normalize(residual)
    gain_grad[...] += jnp.sum(normed_grad * scaled, axis=0, keepdims=True)
    residual_grad = upstream + norm_backward(normed_grad, scaled, inverse, gain[...])
    res_grad[...] = residual_grad
    low = residual_grad.astype(LOW)
    attn_grad[:near] += dot_tn(att[...], low)
    attn_grad[near:] += dot_tn(att_far[...], low)
    near_grad[...] = dot_nt(low, weight[:near]).astype(LOW)
    far_grad[...] = dot_nt(low, weight[near:]).astype(LOW)


def post(ids, res, own, far, gates, up, normed, att, att_far, weight, gain, router, block):
    half, packed = own.shape
    width = res.shape[1]
    steps = half // block
    heads = att.shape[1]
    spec = lambda n: pl.BlockSpec((block, n), lambda i, ids: (i, 0))
    shape = lambda n, t: jax.ShapeDtypeStruct((half, n), t)
    return pl.pallas_call(
        post_kernel,
        grid_spec=pltpu.PrefetchScalarGridSpec(
            num_scalar_prefetch=1,
            grid=(steps,),
            in_specs=[
                spec(width),
                spec(packed),
                spec(packed),
                spec(LANES),
                spec(width),
                spec(width),
                spec(heads),
                pl.BlockSpec((block, heads), lambda i, ids: (i + steps, 0)),
                whole(*weight.shape),
                whole(1, width),
                whole(*router.shape),
            ],
            out_specs=[
                spec(width),
                spec(width),
                spec(heads),
                spec(heads),
                whole(*weight.shape),
                whole(*router.shape),
                whole(1, width),
            ],
        ),
        out_shape=[
            shape(width, LOW),
            shape(width, F32),
            shape(heads, LOW),
            shape(heads, LOW),
            jax.ShapeDtypeStruct(weight.shape, F32),
            jax.ShapeDtypeStruct(router.shape, F32),
            jax.ShapeDtypeStruct((1, width), F32),
        ],
        compiler_params=params(),
        name="post",
    )(ids, res, own, far, gates, up, normed, att, att_far, weight, gain, router)


def project_back_kernel(steps, normed, dq, dk, dv, weight, near, far, grad):
    step = pl.program_id(0)

    @pl.when(step == 0)
    def _():
        grad[...] = jnp.zeros_like(grad)

    rows = jnp.concatenate([dq[...], dk[...], dv[...]], axis=1)
    back = dot_nt(rows, weight[...])
    grad[...] += dot_tn(normed[...], rows)

    @pl.when(step < steps // 2)
    def _():
        far[...] = back.astype(LOW)

    @pl.when(step >= steps // 2)
    def _():
        near[...] = back


def project_back(normed, dq, dk, dv, weight, block):
    tokens, width = normed.shape
    heads = dq.shape[1]
    steps = tokens // block
    turn = lambda i: ((i + steps // 2) % steps, 0)
    part = pl.BlockSpec((block, heads), turn)
    shape = lambda t: jax.ShapeDtypeStruct((tokens // 2, width), t)
    return pl.pallas_call(
        functools.partial(project_back_kernel, steps),
        grid=(steps,),
        in_specs=[pl.BlockSpec((block, width), turn), part, part, part, whole(*weight.shape)],
        out_specs=[
            pl.BlockSpec((block, width), lambda i: (jnp.maximum(i - steps // 2, 0), 0)),
            pl.BlockSpec((block, width), lambda i: (jnp.minimum(i, steps // 2 - 1), 0)),
            whole(*weight.shape),
        ],
        out_shape=[shape(F32), shape(LOW), jax.ShapeDtypeStruct(weight.shape, F32)],
        compiler_params=params(),
        name="project_back",
    )(normed, dq, dk, dv, weight)


def finish_kernel(x, near, far, res_grad, gain, out, gain_grad):
    @pl.when(pl.program_id(0) == 0)
    def _():
        gain_grad[...] = jnp.zeros_like(gain_grad)

    scaled, inverse = normalize(x[...].astype(F32))
    grad = near[...] + far[...].astype(F32)
    gain_grad[...] += jnp.sum(grad * scaled, axis=0, keepdims=True)
    out[...] = (res_grad[...] + norm_backward(grad, scaled, inverse, gain[...])).astype(LOW)


def finish(x, near, far, res_grad, gain, block):
    half, width = near.shape
    row = pl.BlockSpec((block, width), lambda i: (i, 0))
    return pl.pallas_call(
        finish_kernel,
        grid=(half // block,),
        in_specs=[row, row, row, row, whole(1, width)],
        out_specs=[row, whole(1, width)],
        out_shape=[
            jax.ShapeDtypeStruct((half, width), LOW),
            jax.ShapeDtypeStruct((1, width), F32),
        ],
        compiler_params=params(),
        name="finish",
    )(x, near, far, res_grad, gain)


def local(
    activations, qkv_weight, attn_weight, router_weight, gain_one, gain_two,
    expert_in, expert_out, segments, task_ids, task_experts, out_grad,
):
    packs, length, width = activations.shape
    positions = lax.axis_size("seq")
    groups = lax.axis_size("dp")
    core = lax.axis_index("dp") % 2
    place = lax.axis_index("seq")
    pair_packs = 2 * packs
    assert pair_packs == positions and groups % 2 == 0
    tokens = positions * length
    half = tokens // 2
    piece = length // 2
    experts = router_weight.shape[1]
    dense_rows = qkv_weight.shape[0]
    heads = width // HEAD // 2
    near_width = heads * HEAD
    swap_pairs = [(i, i ^ 1) for i in range(groups)]
    block = min(512, half)

    def swap(values):
        return lax.ppermute(values, "dp", swap_pairs)

    def pick(values, index, axis):
        return lax.dynamic_index_in_dim(values, index, axis, keepdims=False)

    def ordered(mine, other):
        stacked = jnp.stack([mine, other])
        return jnp.where(core == 0, stacked, stacked[::-1])

    def to_pack(values):
        cut = values.reshape(packs, 2, piece, -1)
        four = ordered(pick(cut, core, 1), swap(pick(cut, 1 - core, 1)))
        four = four.reshape(pair_packs, piece, -1)
        return lax.all_to_all(four, "seq", 0, 0).reshape(half, -1)

    def from_pack(values):
        four = lax.all_to_all(values.reshape(positions, piece, -1), "seq", 0, 0)
        four = four.reshape(2, packs, piece, -1)
        parts = ordered(pick(four, core, 0), swap(pick(four, 1 - core, 0)))
        return jnp.swapaxes(parts, 0, 1).reshape(packs, length, -1)

    small = jnp.concatenate(
        [router_weight, gain_one[:, None], gain_two[:, None]]
        + [jnp.zeros((dense_rows, LANES - experts - 2), LOW)],
        axis=1,
    )
    dense = jnp.concatenate([qkv_weight, attn_weight, small], axis=1)
    dense = lax.all_gather(dense, "dp", axis=0, tiled=True)
    qkv_full = dense[:, : 3 * width].reshape(width, 3, 2, near_width)
    attn_full = dense[:, 3 * width : 4 * width].reshape(2, near_width, width)
    small = dense[:, 4 * width :]
    lane = jnp.arange(LANES)
    router = jnp.where(lane < experts, small, 0)
    first_gain = small[:, experts].astype(F32)[None]
    second_gain = small[:, experts + 1].astype(F32)[None]
    qkv_near = pick(qkv_full, core, 2).reshape(width, 3 * near_width)
    attn_near = jnp.where(core == 0, attn_full, attn_full[::-1]).reshape(width, width)
    qkv_wide = jnp.pad(
        qkv_near.reshape(width, 3 * heads, HEAD), ((0, 0), (0, 0), (0, LANES - HEAD))
    ).reshape(width, 3 * heads * LANES)

    tasks = lax.all_gather(task_ids[:, 0], "dp", axis=0, tiled=True)
    chosen = jnp.take(task_experts, tasks, axis=0).reshape(groups // 2, positions, 2)
    device_expert = jnp.swapaxes(chosen, 1, 2).reshape(groups * positions)
    mine = chosen[lax.axis_index("dp") // 2, place]
    pair = jnp.stack([mine[core], mine[1 - core]])

    x_half = to_pack(activations)
    x = jnp.concatenate([x_half, swap(x_half)])
    seg_half = to_pack(segments[..., None])
    seg = jnp.concatenate([seg_half, swap(seg_half)])
    chosen_weights = select_weights(
        device_expert, jnp.swapaxes(expert_in, 0, 1), jnp.swapaxes(expert_out, 0, 1)
    )
    weights = lax.all_to_all(chosen_weights, ("dp", "seq"), 0, 0)
    up_half = to_pack(out_grad.astype(LOW))
    up = jnp.concatenate([up_half, swap(up_half)])

    normed_one, qa, ka, va = project(x, seg, first_gain, qkv_wide, heads, block)
    att, lse = attend(qa, ka, va, block)
    att_far = swap(att)
    res, normed_two, gates, slot = middle(
        pair, x, att, att_far, attn_near, second_gain, router, up, block
    )
    own, far, grads = expert(normed_two, slot, up, gates, weights, 256)
    grads = lax.all_to_all(grads, ("dp", "seq"), 0, 0)
    far = swap(far)
    outputs, res_grad, near_grad, far_grad, attn_grad, router_grad, gain_two_grad = post(
        pair, res, own, far, gates, up, normed_two, att, att_far, attn_near, second_gain, router, block
    )
    att_grad = jnp.concatenate([near_grad, swap(far_grad)])
    dq, dk, dv = attend_back(qa, ka, va, lse, att, att_grad, 512)
    near_back, far_back, qkv_grad = project_back(normed_one, dq, dk, dv, qkv_near, block)
    input_half, gain_one_grad = finish(
        x, near_back, swap(far_back), res_grad, first_gain, block
    )
    outputs = from_pack(outputs)
    input_grad = from_pack(input_half).astype(F32)
    expert_in_grad, expert_out_grad = collect_grads(device_expert, grads, experts)

    attn_grad = attn_grad.reshape(2, near_width, width)
    attn_grad = jnp.where(core == 0, attn_grad, attn_grad[::-1]).reshape(width, width)
    small = jnp.where(
        lane == experts,
        gain_one_grad[0][:, None],
        jnp.where(lane == experts + 1, gain_two_grad[0][:, None], router_grad),
    )
    dense = jnp.concatenate([qkv_grad, attn_grad, small], axis=1).astype(LOW)
    dense = lax.all_to_all(dense.reshape(groups, dense_rows, -1), "dp", 0, 0)
    dense = dense.reshape(groups // 2, 2, dense_rows, -1).astype(F32)
    qkv_sum = jnp.sum(dense[..., : 3 * near_width], axis=0)
    qkv_sum = qkv_sum.reshape(2, dense_rows, 3, near_width)
    qkv_sum = jnp.moveaxis(qkv_sum, 0, 2).reshape(dense_rows, 3 * width)
    rest = jnp.sum(dense[..., 3 * near_width :], axis=(0, 1))
    total = jnp.concatenate([qkv_sum, rest], axis=1).astype(LOW)
    total = lax.all_gather(total, "seq", axis=0, tiled=False)
    total = jnp.sum(total.astype(F32), axis=0)
    at = 4 * width
    return (
        outputs,
        input_grad,
        total[:, : 3 * width],
        total[:, 3 * width : at],
        total[:, at : at + experts],
        total[:, at + experts],
        total[:, at + experts + 1],
        expert_in_grad,
        expert_out_grad,
    )


def solution(mesh):
    placed = (
        P("dp", "seq", None),
        P("dp", None),
        P("dp", None),
        P("dp", None),
        P("dp"),
        P("dp"),
        P(("dp", "seq"), None, None),
        P(("dp", "seq"), None, None),
        P("dp", "seq"),
        P("dp", "seq"),
        P(),
        P("dp", "seq", None),
    )
    return jax.shard_map(
        local,
        mesh=mesh,
        in_specs=placed,
        out_specs=(
            P("dp", "seq", None),
            P("dp", "seq", None),
            P("dp", None),
            P("dp", None),
            P("dp", None),
            P("dp"),
            P("dp"),
            P(("dp", "seq"), None, None),
            P(("dp", "seq"), None, None),
        ),
        check_vma=False,
    )
```

```python
import functools

import jax
import jax.numpy as jnp
from jax import lax
from jax.experimental import pallas as pl
from jax.experimental.pallas import tpu as pltpu
from jax.sharding import PartitionSpec as P

HEAD = 64
LANES = 128
SEG_COL = HEAD
LSE_COL = HEAD + 16
SEGMENTS = 16
FAR = 1e9
VMEM = 56 << 20
NT = (((1,), (1,)), ((), ()))
TN = (((0,), (0,)), ((), ()))
MESH = pl.DeviceIdType.MESH
EXPERTS_AT = LANES - 1
PAD = 16
F32 = jnp.float32
LOW = jnp.bfloat16


def dot(a, b):
    return jnp.dot(a, b, preferred_element_type=F32)


def dot_nt(a, b):
    return lax.dot_general(a, b, NT, preferred_element_type=F32)


def dot_tn(a, b):
    return lax.dot_general(a, b, TN, preferred_element_type=F32)


def thirds(values):
    high = values.astype(LOW).astype(F32)
    rest = values - high
    mid = rest.astype(LOW).astype(F32)
    return high, mid, rest - mid


def lanes_of(shape):
    return lax.broadcasted_iota(jnp.int32, shape, len(shape) - 1)


def put_thirds(base, values, column):
    lane = lanes_of(base.shape)
    high, mid, last = thirds(values)
    base = jnp.where(lane == column, high, base)
    base = jnp.where(lane == column + 1, mid, base)
    return jnp.where(lane == column + 2, last, base)


def normalize(values):
    center = values - jnp.mean(values, axis=-1, keepdims=True)
    inverse = lax.rsqrt(jnp.mean(center * center, axis=-1, keepdims=True) + 1e-05)
    return center * inverse, inverse


def norm_backward(upstream, scaled, inverse, gain_vec):
    direct = upstream * gain_vec
    return inverse * (
        direct
        - jnp.mean(direct, axis=-1, keepdims=True)
        - scaled * jnp.mean(direct * scaled, axis=-1, keepdims=True)
    )


def params(limit=VMEM):
    return pltpu.CompilerParams(vmem_limit_bytes=limit)


def cost(micros):
    return pl.CostEstimate(flops=int(micros * 1e7), bytes_accessed=1 << 10, transcendentals=0)


def whole(*shape):
    return pl.BlockSpec(shape, lambda *_: (0,) * len(shape))


def remote(source, target, send, receive, device):
    return pltpu.make_async_remote_copy(
        src_ref=source,
        dst_ref=target,
        send_sem=send,
        recv_sem=receive,
        device_id=device,
        device_id_type=MESH,
    )


def each(count, body):
    def step(i, carry):
        body(i)
        return carry

    lax.fori_loop(0, count, step, 0)


def greet(base, place, planes, groups=None):
    me = lax.axis_index("dp")
    barrier = pltpu.get_barrier_semaphore()

    def signal(dp, z):
        pl.semaphore_signal(barrier, inc=1, device_id=(dp, z), device_id_type=MESH)

    def column(i):
        z = lax.rem(i, planes)

        @pl.when(z != place)
        def _():
            signal(base + i // planes, z)

    def plane(i):
        @pl.when(i != me)
        def _():
            signal(i, place)

    each(2 * planes, column)
    if groups is None:
        signal(2 * base + 1 - me, place)
        pl.semaphore_wait(barrier, 2 * (planes - 1) + 1)
    else:
        each(groups, plane)
        pl.semaphore_wait(barrier, 2 * (planes - 1) + groups - 1)


def gather_kernel(
    groups, planes, pieces, near, rest, x, near_all, rest_all,
    send_x, got_x, send_on, got_on, send_near, got_near, send_rest, got_rest, local,
):
    me = lax.axis_index("dp")
    place = lax.axis_index("seq")
    core = lax.rem(me, 2)
    base = me - core
    partner = base + 1 - core
    greet(base, place, planes, groups)
    stays = (place // 2) == core
    at_home = pltpu.make_async_copy(pieces.at[core + 2 * lax.rem(place, 2)], x.at[place], local.at[0])

    def send(d):
        return remote(
            pieces.at[d],
            x.at[place],
            send_x.at[d],
            got_x.at[place],
            (base + lax.rem(d, 2), 2 * core + d // 2),
        )

    def goes(d):
        return jnp.logical_not(stays & (d == core + 2 * lax.rem(place, 2)))

    def start(d):
        @pl.when(goes(d))
        def _():
            send(d).start()

    each(planes, start)

    @pl.when(stays)
    def _():
        at_home.start()

    def give_near(i):
        return remote(
            near.at[lax.rem(i, 2)], near_all.at[me], send_near.at[i], got_near.at[me], (i, place)
        )

    def give_rest(i):
        return remote(rest, rest_all.at[me], send_rest.at[i], got_rest.at[me], (i, place))

    def others(body):
        def run(i):
            @pl.when(i != me)
            def _():
                body(i)

        each(groups, run)

    def start_dense(i):
        give_rest(i).start()
        give_near(i).start()

    others(start_dense)
    mine_near = pltpu.make_async_copy(near.at[core], near_all.at[me], local.at[1])
    mine_rest = pltpu.make_async_copy(rest, rest_all.at[me], local.at[2])
    mine_near.start()
    mine_rest.start()

    def onward(slot):
        return remote(
            x.at[slot], x.at[planes + slot], send_on.at[slot], got_on.at[slot], (partner, place)
        )

    def arrived(slot):
        remote(
            pieces.at[0], x.at[slot], send_x.at[0], got_x.at[slot], (partner, place)
        ).wait_recv()

    def pass_on(k):
        slot = lax.rem(place + k, planes)
        home = stays & (k == 0)

        @pl.when(home)
        def _():
            at_home.wait()

        @pl.when(jnp.logical_not(home))
        def _():
            arrived(slot)

        onward(slot).start()

    each(planes, pass_on)

    def finish(d):
        @pl.when(goes(d))
        def _():
            send(d).wait_send()

    each(planes, finish)

    def end_dense(i):
        give_near(i).wait_send()
        give_rest(i).wait_send()
        remote(near.at[0], near_all.at[i], send_near.at[i], got_near.at[i], (i, place)).wait_recv()
        remote(rest, rest_all.at[i], send_rest.at[i], got_rest.at[i], (i, place)).wait_recv()

    others(end_dense)
    mine_near.wait()
    mine_rest.wait()
    each(planes, lambda slot: onward(slot).wait())


def gather(pieces, near, rest, groups, planes):
    anywhere = pl.BlockSpec(memory_space=pl.ANY)
    dma = pltpu.SemaphoreType.DMA
    return pl.pallas_call(
        functools.partial(gather_kernel, groups, planes),
        in_specs=[anywhere] * 3,
        out_specs=[anywhere] * 3,
        out_shape=[
            jax.ShapeDtypeStruct((2 * planes,) + pieces.shape[1:], LOW),
            jax.ShapeDtypeStruct((groups,) + near.shape[1:], LOW),
            jax.ShapeDtypeStruct((groups,) + rest.shape, LOW),
        ],
        scratch_shapes=[dma((planes,))] * 4 + [dma((groups,))] * 4 + [dma((3,))],
        compiler_params=pltpu.CompilerParams(collective_id=0, has_side_effects=True),
        cost_estimate=cost(30),
        name="gather",
    )(pieces, near, rest)


def bring_back_kernel(
    planes, values, part, out, total, heard, mine, summed,
    send_sem, got_sem, send_part, got_part, send_sum, got_sum, local,
):
    me = lax.axis_index("dp")
    place = lax.axis_index("seq")
    core = lax.rem(me, 2)
    base = me - core
    greet(base, place, planes)
    stays = (place // 2) == core
    spot = core + 2 * lax.rem(place, 2)
    at_home = pltpu.make_async_copy(values.at[place], out.at[spot], local.at[0])
    keep = pltpu.make_async_copy(part.at[place], mine, local.at[1])
    put = pltpu.make_async_copy(summed, total.at[place], local.at[2])

    def others(body):
        def run(z):
            @pl.when(z != place)
            def _():
                body(z)

        each(planes, run)

    def share(z):
        return remote(part.at[z], heard.at[place], send_part.at[z], got_part.at[place], (me, z))

    def heard_from(z):
        return remote(part.at[z], heard.at[z], send_part.at[z], got_part.at[z], (me, z))

    def tell(z):
        return remote(summed, total.at[place], send_sum.at[z], got_sum.at[place], (me, z))

    def told_by(z):
        return remote(summed, total.at[z], send_sum.at[z], got_sum.at[z], (me, z))

    others(lambda z: share(z).start())
    keep.start()

    def send(slot):
        return remote(
            values.at[slot],
            out.at[spot],
            send_sem.at[slot],
            got_sem.at[spot],
            (base + place // 2, slot),
        )

    def start(slot):
        @pl.when(jnp.logical_not(stays & (slot == place)))
        def _():
            send(slot).start()

    each(planes, start)

    @pl.when(stays)
    def _():
        at_home.start()

    others(lambda z: heard_from(z).wait_recv())
    keep.wait()
    sum_of = mine[...].astype(F32)
    for k in range(1, planes):
        sum_of += heard[lax.rem(place + k, planes)].astype(F32)
    summed[...] = sum_of.astype(LOW)
    others(lambda z: tell(z).start())
    put.start()

    def end(d):
        @pl.when(jnp.logical_not(stays & (d == place)))
        def _():
            send(d).wait_send()

        @pl.when(jnp.logical_not(stays & (d == spot)))
        def _():
            remote(
                values.at[0], out.at[d], send_sem.at[0], got_sem.at[d], (base + 1 - core, place)
            ).wait_recv()

    each(planes, end)
    others(lambda z: share(z).wait_send())
    others(lambda z: tell(z).wait_send())
    others(lambda z: told_by(z).wait_recv())
    put.wait()

    @pl.when(stays)
    def _():
        at_home.wait()


def bring_back(values, part):
    planes = values.shape[0]
    anywhere = pl.BlockSpec(memory_space=pl.ANY)
    dma = pltpu.SemaphoreType.DMA
    return pl.pallas_call(
        functools.partial(bring_back_kernel, planes),
        in_specs=[anywhere] * 2,
        out_specs=[anywhere] * 2,
        out_shape=[
            jax.ShapeDtypeStruct(values.shape, LOW),
            jax.ShapeDtypeStruct(part.shape, LOW),
        ],
        scratch_shapes=[
            pltpu.VMEM(part.shape, LOW),
            pltpu.VMEM(part.shape[1:], LOW),
            pltpu.VMEM(part.shape[1:], LOW),
        ]
        + [dma((planes,))] * 6
        + [dma((3,))],
        compiler_params=pltpu.CompilerParams(collective_id=1, has_side_effects=True),
        cost_estimate=cost(30),
        name="bring_back",
    )(values, part)


def select_kernel(ids, win, wout, out):
    def body(i, carry):
        out[i, 0] = win[ids[i]]
        out[i, 1] = wout[ids[i]]
        return carry

    lax.fori_loop(0, out.shape[0], body, 0)


def select_weights(ids, win, wout):
    experts, rows, width = win.shape
    count = ids.shape[0]
    return pl.pallas_call(
        select_kernel,
        grid_spec=pltpu.PrefetchScalarGridSpec(
            num_scalar_prefetch=1,
            grid=(1,),
            in_specs=[whole(experts, rows, width)] * 2,
            out_specs=whole(count, 2, rows, width),
        ),
        out_shape=jax.ShapeDtypeStruct((count, 2, rows, width), LOW),
        compiler_params=params(),
        cost_estimate=cost(3),
        name="select_weights",
    )(ids, win, wout)


def add_up(ids, grads, acc_in, acc_out):
    acc_in[...] = jnp.zeros_like(acc_in)
    acc_out[...] = jnp.zeros_like(acc_out)

    def body(i, carry):
        acc_in[ids[i]] += grads[i, 0].astype(F32)
        acc_out[ids[i]] += grads[i, 1].astype(F32)
        return carry

    lax.fori_loop(0, grads.shape[0], body, 0)


def partial_kernel(ids, grads, out, acc_in, acc_out):
    add_up(ids, grads, acc_in, acc_out)
    out[0] = acc_in[...].astype(LOW)
    out[1] = acc_out[...].astype(LOW)


def collect_kernel(ids, grads, other, out_in, out_out, acc_in, acc_out):
    add_up(ids, grads, acc_in, acc_out)
    for e in range(acc_in.shape[0]):
        out_in[:, e, :] = acc_in[e] + other[0, e].astype(F32)
        out_out[:, e, :] = acc_out[e] + other[1, e].astype(F32)


def collect(ids, grads, experts, other=None):
    _, _, rows, width = grads.shape
    packed = (2, experts, rows, width)
    final = (rows, experts, width)
    if other is None:
        kernel, operands = partial_kernel, (grads,)
        specs, shapes = whole(*packed), jax.ShapeDtypeStruct(packed, LOW)
    else:
        kernel, operands = collect_kernel, (grads, other)
        specs, shapes = [whole(*final)] * 2, [jax.ShapeDtypeStruct(final, F32)] * 2
    return pl.pallas_call(
        kernel,
        grid_spec=pltpu.PrefetchScalarGridSpec(
            num_scalar_prefetch=1,
            grid=(1,),
            in_specs=[whole(*o.shape) for o in operands],
            out_specs=specs,
            scratch_shapes=[pltpu.VMEM((experts, rows, width), F32)] * 2,
        ),
        out_shape=shapes,
        compiler_params=params(),
        cost_estimate=cost(4),
        name="collect_grads",
    )(ids, *operands)


def project_kernel(heads, x, gain, weight, normed, qa, ka, va):
    piece = normed.shape[0]
    scaled, _ = normalize(x[0, :piece].astype(F32))
    low = (scaled * gain[...]).astype(LOW)
    normed[...] = low
    rows = dot(low, weight[...])
    lane = lanes_of((piece, LANES))
    seg = x[0, piece : piece + PAD, :piece].astype(F32)[0:1]
    seg = jnp.broadcast_to(seg, (LANES, piece)).T
    same = (lane - SEG_COL).astype(F32) == seg
    in_seg = (lane >= SEG_COL) & (lane < SEG_COL + SEGMENTS)
    q_more = jnp.where(same, 1.0, 0.0)
    k_more = jnp.where(in_seg & jnp.logical_not(same), -FAR, 0.0)
    k_more = jnp.where((lane >= LSE_COL) & (lane < LSE_COL + 3), 1.0, k_more)
    v_more = jnp.where((lane >= HEAD) & (lane < HEAD + 3), 1.0, 0.0)
    step = heads * HEAD

    def head(kind, h, more):
        at = kind * step + h // 2 * LANES
        values = rows[:, at : at + LANES]
        if h % 2:
            values = pltpu.roll(values, HEAD, 1)
        return jnp.where(lane < HEAD, values, more)

    for h in range(heads):
        query = head(0, h, 0.0).astype(LOW).astype(F32) * HEAD**-0.5
        qa[h] = (query + q_more).astype(LOW)
        ka[h] = head(1, h, k_more).astype(LOW)
        va[h] = head(2, h, v_more).astype(LOW)


def project(x, gain, weight, heads):
    count, rows, width = x.shape
    block = rows - PAD
    tokens = count * block
    wide = jax.ShapeDtypeStruct((heads, tokens, LANES), LOW)
    spec = pl.BlockSpec((heads, block, LANES), lambda i: (0, i, 0))
    return pl.pallas_call(
        functools.partial(project_kernel, heads),
        grid=(count,),
        in_specs=[
            pl.BlockSpec((1, rows, width), lambda i: (i, 0, 0)),
            whole(1, width),
            whole(*weight.shape),
        ],
        out_specs=[pl.BlockSpec((block, width), lambda i: (i, 0)), spec, spec, spec],
        out_shape=[jax.ShapeDtypeStruct((tokens, width), LOW), wide, wide, wide],
        compiler_params=params(),
        cost_estimate=cost(8),
        name="project",
    )(x, gain, weight)


def across_start(values, out, send, got):
    place = lax.axis_index("seq")
    peer = (lax.axis_index("dp"), place + 2 - 4 * (place // 2))
    barrier = pltpu.get_barrier_semaphore()
    pl.semaphore_signal(barrier, inc=1, device_id=peer, device_id_type=MESH)
    pl.semaphore_wait(barrier, 1)
    remote(values, out, send.at[0], got.at[0], peer).start()


def across_end(values, out, send, got):
    place = lax.axis_index("seq")
    peer = (lax.axis_index("dp"), place + 2 - 4 * (place // 2))
    remote(values, out, send.at[0], got.at[0], peer).wait()


def attend_kernel(qa, ka, va, both, out, lse, other, send, got):
    first = (pl.program_id(0) == 0) & (pl.program_id(1) == 0)
    last = (pl.program_id(0) == pl.num_programs(0) - 1) & (
        pl.program_id(1) == pl.num_programs(1) - 1
    )

    @pl.when(first)
    def _():
        across_start(both, other, send, got)

    parts = []
    for h in range(2):
        scores = dot_nt(qa[h], ka[h])
        top = jnp.max(scores, axis=1, keepdims=True)
        probs = jnp.exp(scores - top).astype(LOW)
        mixed = dot(probs, va[h])
        total = mixed[:, HEAD : HEAD + 1]
        parts.append(mixed[:, :HEAD] / total)
        lse[h] = top + jnp.log(total)
    out[...] = jnp.concatenate(parts, axis=1).astype(LOW)

    @pl.when(last)
    def _():
        across_end(both, other, send, got)


def attend(qa, ka, va, both, block):
    heads, tokens, _ = qa.shape
    full = pl.BlockSpec((2, tokens, LANES), lambda h, i: (h, 0, 0))
    anywhere = pl.BlockSpec(memory_space=pl.ANY)
    return pl.pallas_call(
        attend_kernel,
        grid=(heads // 2, tokens // block),
        in_specs=[pl.BlockSpec((2, block, LANES), lambda h, i: (h, i, 0)), full, full, anywhere],
        out_specs=[
            pl.BlockSpec((block, LANES), lambda h, i: (i, h)),
            pl.BlockSpec((2, block, 1), lambda h, i: (h, i, 0)),
            anywhere,
        ],
        out_shape=[
            jax.ShapeDtypeStruct((tokens, heads * HEAD), LOW),
            jax.ShapeDtypeStruct((heads, tokens, 1), F32),
            jax.ShapeDtypeStruct(both.shape, LOW),
        ],
        scratch_shapes=[pltpu.SemaphoreType.DMA((1,))] * 2,
        compiler_params=pltpu.CompilerParams(
            vmem_limit_bytes=VMEM, collective_id=2, has_side_effects=True
        ),
        cost_estimate=cost(50),
        name="attend",
    )(qa, ka, va, both)


def attend_back_kernel(block, riding, *refs):
    qa, ka, va, lse, att, grad = refs[:6]
    refs = refs[6:]
    if riding:
        sums, dq, dk, dv, other, qb, gb, dq_acc, send, got = refs
        across_start(sums, other, send, got)
    else:
        dq, dk, dv, qb, gb, dq_acc = refs
    tokens = qa.shape[1]
    lane = lanes_of((tokens, LANES))
    halves = []
    for h in range(2):
        pair_grad = grad[...].astype(F32)
        inner = pair_grad * att[...].astype(F32)
        if h == 1:
            pair_grad = pltpu.roll(pair_grad, HEAD, 1)
            inner = pltpu.roll(inner, HEAD, 1)
        delta = jnp.sum(jnp.where(lane < HEAD, inner, 0.0), axis=1, keepdims=True)
        gb[...] = put_thirds(jnp.where(lane < HEAD, pair_grad, 0.0), -delta, HEAD).astype(LOW)
        qb[...] = put_thirds(qa[h].astype(F32), -lse[h], LSE_COL).astype(LOW)
        key_t = ka[h].T[:HEAD]
        dq_acc[...] = jnp.zeros_like(dq_acc)
        for i in range(tokens // block):
            r = pl.ds(i * block, block)
            weights = jnp.exp(dot_nt(ka[h, r, :], qb[...]))
            centered = dot_nt(va[h, r, :], gb[...])
            score_grad = (weights * centered).astype(LOW)
            out = pl.ds(h * HEAD, HEAD)
            dv[r, out] = dot(weights.astype(LOW), gb[...])[:, :HEAD].astype(LOW)
            dk[r, out] = dot(score_grad, qb[...])[:, :HEAD].astype(LOW)
            dq_acc[...] += dot(key_t[:, i * block : (i + 1) * block], score_grad)
        halves.append(dq_acc[...].T * HEAD**-0.5)
    dq[...] = jnp.concatenate(halves, axis=1).astype(LOW)
    if riding:
        across_end(sums, other, send, got)


def attend_back(pair, qa, ka, va, lse, att, grad, block, sums=None):
    tokens = qa.shape[1]
    full = pl.BlockSpec((2, tokens, LANES), lambda h: (pair, 0, 0))
    row = pl.BlockSpec((tokens, LANES), lambda h: (0, pair))
    out = whole(tokens, LANES)
    shape = jax.ShapeDtypeStruct((tokens, LANES), LOW)
    riding = sums is not None
    ride = [sums] if riding else []
    anywhere = [pl.BlockSpec(memory_space=pl.ANY)] * len(ride)
    more = dict(collective_id=3, has_side_effects=True) if riding else {}
    return pl.pallas_call(
        functools.partial(attend_back_kernel, block, riding),
        grid=(1,),
        in_specs=[full, full, full, pl.BlockSpec((2, tokens, 1), lambda h: (pair, 0, 0)), row, row]
        + anywhere,
        out_specs=[out, out, out] + anywhere,
        out_shape=[shape, shape, shape] + [jax.ShapeDtypeStruct(s.shape, s.dtype) for s in ride],
        scratch_shapes=[
            pltpu.VMEM((tokens, LANES), LOW),
            pltpu.VMEM((tokens, LANES), LOW),
            pltpu.VMEM((HEAD, tokens), F32),
        ]
        + [pltpu.SemaphoreType.DMA((1,))] * (2 * len(ride)),
        compiler_params=pltpu.CompilerParams(vmem_limit_bytes=VMEM, **more),
        cost_estimate=cost(24),
        name="attend_back",
    )(qa, ka, va, lse, att, grad, *ride)


def near_rows(ids, weight, width, far=False):
    rows = weight.shape[0] // 2
    core = 1 - ids[2] if far else ids[2]
    return weight[pl.ds(pl.multiple_of(core * rows, rows), rows), :width]


def middle_kernel(ids, x, att, att_far, dense, gain, res, normed, gates):
    piece, width = res.shape
    residual = x[0, :piece].astype(F32)
    residual += dot(att[...], near_rows(ids, dense, width))
    residual += dot(att_far[...], near_rows(ids, dense, width, far=True))

    res[...] = residual
    scaled, _ = normalize(residual)
    low = (scaled * gain[...]).astype(LOW)
    normed[...] = low
    logits = dot(low, dense[:, width:])
    lane = lanes_of(logits.shape)
    mine = jnp.sum(jnp.where(lane == ids[0], logits, 0.0), axis=1, keepdims=True)
    other = jnp.sum(jnp.where(lane == ids[1], logits, 0.0), axis=1, keepdims=True)
    top = jnp.maximum(mine, other)
    mine = jnp.exp(mine - top)
    other = jnp.exp(other - top)
    total = mine + other
    gates[...] = jnp.where(lane == 0, mine / total, jnp.where(lane == 1, other / total, 0.0))


def middle(ids, x, att, att_far, dense, gain):
    steps, rows, width = x.shape
    block = rows - PAD
    tokens = steps * block
    row = pl.BlockSpec((block, width), lambda i, ids: (i, 0))
    heads = att.shape[1]
    part = pl.BlockSpec((block, heads), lambda i, ids: (i, 0))
    far = pl.BlockSpec((block, heads), lambda i, ids: ((i + steps // 2) % steps, 0))
    shape = lambda n, t: jax.ShapeDtypeStruct((tokens, n), t)
    return pl.pallas_call(
        middle_kernel,
        grid_spec=pltpu.PrefetchScalarGridSpec(
            num_scalar_prefetch=1,
            grid=(steps,),
            in_specs=[
                pl.BlockSpec((1, rows, width), lambda i, ids: (i, 0, 0)),
                part,
                far,
                whole(*dense.shape),
                whole(1, width),
            ],
            out_specs=[row, row, pl.BlockSpec((block, LANES), lambda i, ids: (i, 0))],
        ),
        out_shape=[shape(width, F32), shape(width, LOW), shape(LANES, F32)],
        compiler_params=params(),
        cost_estimate=cost(10),
        name="middle",
    )(ids, x, att, att_far, dense, gain)


def expert_step(x, slot, weight, grads, out, dx):
    sources, _, rows, width = weight.shape
    win = weight[:, 0].reshape(sources * rows, width)
    wout = weight[:, 1].reshape(sources * rows, width)
    pre = dot_nt(x[...], win)
    hidden_grad = dot_nt(slot[...], wout)
    cdf = 0.5 * (1.0 + lax.erf(pre * 0.7071067811865476))
    slope = cdf + pre * jnp.exp(-0.5 * pre * pre) * 0.3989422804014327
    hidden = (pre * cdf).astype(LOW)
    pre_grad = (hidden_grad * slope).astype(LOW)
    out[...] += dot(hidden, wout)
    dx[...] += dot(pre_grad, win)
    grads[:, 0] = dot_tn(pre_grad, x[...]).astype(LOW).reshape(sources, rows, width)
    grads[:, 1] = dot_tn(hidden, slot[...]).astype(LOW).reshape(sources, rows, width)


def fill_slot(up, gates, slot):
    rows = min(512, slot.shape[0])
    for at in range(0, slot.shape[0], rows):
        r = pl.ds(at, rows)
        slot[r, :] = (gates[r, 0:1] * up[r, :].astype(F32)).astype(LOW)


def expert_first_kernel(x, up, gates, weight, out, dx, grads, slot):
    @pl.when(pl.program_id(0) == 0)
    def _():
        out[...] = jnp.zeros_like(out)
        dx[...] = jnp.zeros_like(dx)
        fill_slot(up, gates, slot)

    expert_step(x, slot, weight, grads, out, dx)


def expert_second_kernel(x, up, gates, weight, out_first, dx_first, own, far, grads, out, dx, slot):
    step = pl.program_id(0)

    @pl.when(step == 0)
    def _():
        out[...] = out_first[...]
        dx[...] = dx_first[...]
        fill_slot(up, gates, slot)

    expert_step(x, slot, weight, grads, out, dx)

    @pl.when(step == pl.num_programs(0) - 1)
    def _():
        half, width = own.shape[0], x.shape[1]
        for at in range(0, 2 * half, half // 2):
            r = pl.ds(at, half // 2)
            value = out[r, :]
            gate_grad = jnp.sum(value * up[r, :].astype(F32), axis=1, keepdims=True)
            value = value * gates[r, 0:1]
            tail = jnp.zeros((half // 2, LANES), F32)
            tail = put_thirds(tail, gate_grad, 0)
            target, to = (own, at) if at < half else (far, at - half)
            t = pl.ds(to, half // 2)
            target[t, :width] = value.astype(target.dtype)
            target[t, width : 2 * width] = dx[r, :].astype(target.dtype)
            target[t, 2 * width :] = tail.astype(target.dtype)


def once(*shape):
    return pl.BlockSpec(shape, lambda i: (0,) * len(shape), pipeline_mode=pl.Buffered(1))


def expert_first(x, up, gates, weight, block):
    tokens, width = x.shape
    count, _, rows, _ = weight.shape
    per = block // rows
    part = pl.BlockSpec((per, 2, rows, width), lambda i: (i, 0, 0, 0))
    total = jax.ShapeDtypeStruct((tokens, width), F32)
    return pl.pallas_call(
        expert_first_kernel,
        grid=(count // per,),
        in_specs=[once(tokens, width), once(tokens, width), once(tokens, LANES), part],
        out_specs=[once(tokens, width), once(tokens, width), part],
        out_shape=[total, total, jax.ShapeDtypeStruct(weight.shape, LOW)],
        scratch_shapes=[pltpu.VMEM((tokens, width), LOW)],
        compiler_params=params(),
        cost_estimate=cost(20),
        name="expert_first",
    )(x, up, gates, weight)


def expert_second(x, up, gates, weight, out, dx, block):
    tokens, width = x.shape
    count, _, rows, _ = weight.shape
    per = block // rows
    part = pl.BlockSpec((per, 2, rows, width), lambda i: (i, 0, 0, 0))
    half = (tokens // 2, 2 * width + LANES)
    return pl.pallas_call(
        expert_second_kernel,
        grid=(count // per,),
        in_specs=[
            once(tokens, width),
            once(tokens, width),
            once(tokens, LANES),
            part,
            once(tokens, width),
            once(tokens, width),
        ],
        out_specs=[once(*half), once(*half), part],
        out_shape=[
            jax.ShapeDtypeStruct(half, F32),
            jax.ShapeDtypeStruct(half, LOW),
            jax.ShapeDtypeStruct(weight.shape, LOW),
        ],
        scratch_shapes=[pltpu.VMEM((tokens, width), F32)] * 2 + [pltpu.VMEM((tokens, width), LOW)],
        compiler_params=params(),
        cost_estimate=cost(22),
        name="expert_second",
    )(x, up, gates, weight, out, dx)


def post_kernel(
    ids, res, own, far, gates, up, normed, att, att_far, dense, gain,
    outputs, res_grad, near_grad, far_grad, dense_grad, attn_grad, router_grad, gain_grad,
):
    @pl.when(pl.program_id(0) == 0)
    def _():
        attn_grad[...] = jnp.zeros_like(attn_grad)
        router_grad[...] = jnp.zeros_like(router_grad)
        gain_grad[...] = jnp.zeros_like(gain_grad)

    width = res.shape[1]
    near = dense.shape[0] // 2
    residual = res[...]
    upstream = up[...].astype(F32)
    outputs[...] = (residual + own[:, :width] + far[:, :width].astype(F32)).astype(LOW)
    grad_mine = jnp.sum(own[:, 2 * width :], axis=1, keepdims=True)
    grad_other = jnp.sum(far[:, 2 * width :].astype(F32), axis=1, keepdims=True)
    gate_mine = gates[:, 0:1]
    gate_other = gates[:, 1:2]
    mean = gate_mine * grad_mine + gate_other * grad_other
    lane = lanes_of(gates.shape)
    logit_grad = jnp.where(lane == ids[0], gate_mine * (grad_mine - mean), 0.0)
    logit_grad += jnp.where(lane == ids[1], gate_other * (grad_other - mean), 0.0)
    normed_grad = own[:, width : 2 * width] + far[:, width : 2 * width].astype(F32)
    for part in thirds(logit_grad):
        part = part.astype(LOW)
        router_grad[...] += dot_tn(normed[...], part)
        normed_grad += dot_nt(part, dense[:, width:])
    scaled, inverse = normalize(residual)
    gain_grad[...] += jnp.sum(normed_grad * scaled, axis=0, keepdims=True)
    residual_grad = upstream + norm_backward(normed_grad, scaled, inverse, gain[...])
    res_grad[...] = residual_grad
    low = residual_grad.astype(LOW)
    attn_grad[:near] += dot_tn(att[...], low)
    attn_grad[near:] += dot_tn(att_far[...], low)
    near_grad[...] = dot_nt(low, near_rows(ids, dense, width)).astype(LOW)
    far_grad[...] = dot_nt(low, near_rows(ids, dense, width, far=True)).astype(LOW)

    @pl.when(pl.program_id(0) == pl.num_programs(0) - 1)
    def _():
        core = ids[2]
        dense_grad[pl.ds(pl.multiple_of(core * near, near), near), :width] = attn_grad[:near]
        dense_grad[pl.ds(pl.multiple_of((1 - core) * near, near), near), :width] = attn_grad[near:]
        turned = jnp.broadcast_to(gain_grad[...], (LANES, width)).T
        lane = lanes_of(turned.shape)
        dense_grad[:, width:] = jnp.where(lane == EXPERTS_AT, turned, router_grad[...])


def post(ids, res, own, far, gates, up, normed, att, att_far, dense, gain, block):
    half, packed = own.shape
    width = res.shape[1]
    steps = half // block
    heads = att.shape[1]
    turned = pl.BlockSpec((block, heads), lambda i, ids: (i + steps, 0))
    spec = lambda n: pl.BlockSpec((block, n), lambda i, ids: (i, 0))
    shape = lambda n, t: jax.ShapeDtypeStruct((half, n), t)
    return pl.pallas_call(
        post_kernel,
        grid_spec=pltpu.PrefetchScalarGridSpec(
            num_scalar_prefetch=1,
            grid=(steps,),
            in_specs=[
                spec(width),
                spec(packed),
                spec(packed),
                spec(LANES),
                spec(width),
                spec(width),
                spec(heads),
                turned,
                whole(*dense.shape),
                whole(1, width),
            ],
            out_specs=[
                spec(width),
                spec(width),
                spec(heads),
                spec(heads),
                whole(width, width + LANES),
            ],
            scratch_shapes=[
                pltpu.VMEM((width, width), F32),
                pltpu.VMEM((width, LANES), F32),
                pltpu.VMEM((1, width), F32),
            ],
        ),
        out_shape=[
            shape(width, LOW),
            shape(width, F32),
            shape(heads, LOW),
            shape(heads, LOW),
            jax.ShapeDtypeStruct((width, width + LANES), F32),
        ],
        compiler_params=params(),
        cost_estimate=cost(12),
        name="post",
    )(ids, res, own, far, gates, up, normed, att, att_far, dense, gain)


def project_back_kernel(steps, x, normed, q0, q1, k0, k1, v0, v1, weight, near, far, dense, grad, gain):
    step = pl.program_id(0)
    piece, width = normed.shape

    @pl.when(step == 0)
    def _():
        grad[...] = jnp.zeros_like(grad)
        gain[...] = jnp.zeros_like(gain)

    rows = jnp.concatenate([q0[...], q1[...], k0[...], k1[...], v0[...], v1[...]], axis=1)
    back = dot_nt(rows, weight[...])
    grad[...] += dot_tn(normed[...], rows)
    scaled, _ = normalize(x[0, :piece].astype(F32))
    gain[...] += jnp.sum(back * scaled, axis=0, keepdims=True)

    @pl.when(step < steps // 2)
    def _():
        far[...] = back.astype(LOW)

    @pl.when(step >= steps // 2)
    def _():
        near[...] = back

    @pl.when(step == steps - 1)
    def _():
        dense[:, : grad.shape[1]] = grad[...].astype(LOW)
        dense[:, grad.shape[1] :] = jnp.broadcast_to(gain[...], (LANES, width)).T.astype(LOW)


def project_back(x, normed, parts, weight):
    tokens, width = normed.shape
    steps, rows, _ = x.shape
    block = rows - PAD
    turn = lambda i: ((i + steps // 2) % steps, 0)
    part = pl.BlockSpec((block, LANES), turn)
    shape = lambda t: jax.ShapeDtypeStruct((tokens // 2, width), t)
    dense = (width, weight.shape[1] + LANES)
    return pl.pallas_call(
        functools.partial(project_back_kernel, steps),
        grid=(steps,),
        in_specs=[
            pl.BlockSpec((1, rows, width), lambda i: ((i + steps // 2) % steps, 0, 0)),
            pl.BlockSpec((block, width), turn),
        ]
        + [part] * 6
        + [whole(*weight.shape)],
        out_specs=[
            pl.BlockSpec((block, width), lambda i: (jnp.maximum(i - steps // 2, 0), 0)),
            pl.BlockSpec((block, width), lambda i: (jnp.minimum(i, steps // 2 - 1), 0)),
            whole(*dense),
        ],
        out_shape=[shape(F32), shape(LOW), jax.ShapeDtypeStruct(dense, LOW)],
        scratch_shapes=[pltpu.VMEM(weight.shape, F32), pltpu.VMEM((1, width), F32)],
        compiler_params=params(),
        cost_estimate=cost(8),
        name="project_back",
    )(x, normed, *parts, weight)


def finish_kernel(x, near, far, res_grad, gain, out):
    scaled, inverse = normalize(x[0, : out.shape[0]].astype(F32))
    grad = near[...] + far[...].astype(F32)
    out[...] = (res_grad[...] + norm_backward(grad, scaled, inverse, gain[...])).astype(LOW)


def finish(x, near, far, res_grad, gain):
    half, width = near.shape
    block = x.shape[1] - PAD
    row = pl.BlockSpec((block, width), lambda i: (i, 0))
    return pl.pallas_call(
        finish_kernel,
        grid=(half // block,),
        in_specs=[
            pl.BlockSpec((1,) + x.shape[1:], lambda i: (i, 0, 0)),
            row,
            row,
            row,
            whole(1, width),
        ],
        out_specs=row,
        out_shape=jax.ShapeDtypeStruct((half, width), LOW),
        compiler_params=params(),
        cost_estimate=cost(5),
        name="finish",
    )(x, near, far, res_grad, gain)


def local(
    activations, qkv_weight, attn_weight, router_weight, gain_one, gain_two,
    expert_in, expert_out, segments, task_ids, task_experts, out_grad,
):
    packs, length, width = activations.shape
    planes = lax.axis_size("seq")
    groups = lax.axis_size("dp")
    me = lax.axis_index("dp")
    core = me % 2
    place = lax.axis_index("seq")
    cuts = 2 * packs
    assert cuts == planes == 4 and groups % 2 == 0
    tokens = planes * length
    half = tokens // 2
    piece = length // 2
    experts = router_weight.shape[1]
    dense_rows = qkv_weight.shape[0]
    heads = width // HEAD // 2
    near_width = heads * HEAD
    lane = jnp.arange(LANES)
    swap_pairs = [(i, i ^ 1) for i in range(groups)]
    across = [(s, s ^ 2) for s in range(planes)]
    bands = [
        [dp * planes + 2 * g + b for dp in range(groups) for b in range(2)]
        for g in range(planes // 2)
    ]

    def swap(values):
        return lax.ppermute(values, "dp", swap_pairs)

    def pick(values, index, axis):
        return lax.dynamic_index_in_dim(values, index, axis, keepdims=False)

    def after(values, *others):
        return lax.optimization_barrier((values, *others))[0]

    def band_exchange(values):
        return lax.all_to_all(values, ("dp", "seq"), 0, 0, axis_index_groups=bands)

    def ordered(mine, other):
        stacked = jnp.stack([mine, other])
        return jnp.where(core == 0, stacked, stacked[::-1])

    seg_rows = segments.astype(LOW).reshape(cuts, 1, piece)
    seg_rows = jnp.pad(seg_rows, ((0, 0), (0, PAD - 1), (0, width - piece)))
    pieces = jnp.concatenate([activations.reshape(cuts, piece, width), seg_rows], axis=1)
    near = jnp.swapaxes(qkv_weight.reshape(dense_rows, 3, 2, near_width), 0, 2)
    near = jnp.swapaxes(near, 1, 2).reshape(2, dense_rows, 3 * near_width)
    rest = jnp.concatenate(
        [attn_weight, router_weight, gain_one[:, None], gain_two[:, None]]
        + [jnp.broadcast_to(task_ids[:, 0].astype(LOW)[None], (dense_rows, packs))]
        + [jnp.zeros((dense_rows, LANES - experts - 2 - packs), LOW)],
        axis=1,
    )
    x, qkv_near, dense = gather(pieces, near, rest, groups, planes)
    qkv_near = qkv_near.reshape(width, 3 * near_width)
    at = width + experts + 2
    tasks = dense[:, 0, at : at + packs].reshape(-1).astype(jnp.int32)
    dense = dense.reshape(width, width + LANES)
    gains = dense[:, width + experts : width + experts + 2].astype(F32).T
    first_gain, second_gain = gains[:1], gains[1:]

    chosen = jnp.take(task_experts, tasks, axis=0).reshape(groups // 2, planes, 2)
    device_expert = jnp.swapaxes(chosen, 1, 2).reshape(groups, planes // 2, 2)
    band_expert = pick(device_expert, place // 2, 1).reshape(groups * 2)
    mine = chosen[me // 2, place]
    pair = jnp.stack([mine[core], mine[1 - core], core])

    win = jnp.swapaxes(expert_in, 0, 1)
    wout = jnp.swapaxes(expert_out, 0, 1)
    both = jnp.stack([win, wout])
    weight_first = band_exchange(select_weights(band_expert, win, wout))
    low_grad = out_grad.astype(LOW).reshape(packs, 2, piece, width)
    low_grad = ordered(pick(low_grad, core, 1), swap(after(pick(low_grad, 1 - core, 1), x)))

    normed_one, qa, ka, va = project(x, first_gain, qkv_near, heads)
    low_grad = after(low_grad.reshape(cuts, piece, width), qa, weight_first)
    up = lax.all_to_all(low_grad, "seq", 0, 0).reshape(half, width)
    att, lse, both = attend(after(qa, low_grad), ka, va, both, 512)
    att_far = swap(att)
    res, normed_two, gates = middle(pair, x, att, att_far, dense, second_gain)
    up = after(up, gates)
    up = jnp.concatenate([up, swap(up)])
    weight_second = band_exchange(select_weights(after(band_expert, up), both[0], both[1]))
    out, dx, grads_first = expert_first(normed_two, up, gates, weight_first, 256)
    grads_first = band_exchange(grads_first)
    own, far, grads_second = expert_second(normed_two, up, gates, weight_second, out, dx, 256)
    grads_second = band_exchange(grads_second)
    far = swap(far)
    outputs, res_grad, near_grad, far_grad, rest_grad = post(
        pair, res, own, far, gates, up, normed_two, att, att_far, dense, second_gain, 512
    )
    att_grad = jnp.concatenate([near_grad, swap(far_grad)])
    rest_grad = lax.psum_scatter(rest_grad, "dp", scatter_dimension=0, tiled=True)
    back_zero = attend_back(0, qa, ka, va, lse, att, att_grad, 512)
    other = collect(band_expert, after(grads_second, back_zero[0]), experts)
    att_grad = after(att_grad, other)
    outputs = lax.all_to_all(after(outputs, att_grad).reshape(cuts, piece, width), "seq", 0, 0)
    outputs = outputs.reshape(2, packs, piece, width)
    outputs = ordered(pick(outputs, core, 0), swap(pick(outputs, 1 - core, 0)))
    outputs = jnp.swapaxes(outputs, 0, 1).reshape(packs, length, width)
    *back_one, other = attend_back(1, qa, ka, va, lse, att, att_grad, 512, other)
    parts = [p for pairs in zip(back_zero, back_one) for p in pairs]
    near_back, far_back, qkv_grad = project_back(x, normed_one, parts, qkv_near)

    qkv_grad = lax.all_to_all(qkv_grad.reshape(groups, dense_rows, -1), "dp", 0, 0)
    qkv_grad = qkv_grad.reshape(groups // 2, 2, dense_rows, -1).astype(F32)
    qkv_sum = jnp.sum(qkv_grad[..., : 3 * near_width], axis=0)
    qkv_sum = qkv_sum.reshape(2, dense_rows, 3, near_width)
    qkv_sum = jnp.moveaxis(qkv_sum, 0, 2).reshape(dense_rows, 3 * width)
    gain_sum = jnp.sum(qkv_grad[..., 3 * near_width :], axis=(0, 1))
    part = jnp.concatenate([qkv_sum, rest_grad, gain_sum], axis=1).astype(LOW)
    part = part.reshape(planes, dense_rows // planes, -1)

    input_half = finish(x, near_back, swap(far_back), res_grad, first_gain)
    input_grad, total = bring_back(input_half.reshape(cuts, piece, width), part)
    input_grad = input_grad.astype(F32).reshape(packs, length, width)
    expert_in_grad, expert_out_grad = collect(band_expert, grads_first, experts, other)
    total = total.reshape(dense_rows, -1).astype(F32)
    return (
        outputs,
        input_grad,
        total[:, : 3 * width],
        total[:, 3 * width : 4 * width],
        total[:, 4 * width : 4 * width + experts],
        total[:, 4 * width + LANES],
        total[:, 4 * width + EXPERTS_AT],
        expert_in_grad,
        expert_out_grad,
    )


def solution(mesh):
    placed = (
        P("dp", "seq", None),
        P("dp", None),
        P("dp", None),
        P("dp", None),
        P("dp"),
        P("dp"),
        P(("dp", "seq"), None, None),
        P(("dp", "seq"), None, None),
        P("dp", "seq"),
        P("dp", "seq"),
        P(),
        P("dp", "seq", None),
    )
    return jax.shard_map(
        local,
        mesh=mesh,
        in_specs=placed,
        out_specs=(
            P("dp", "seq", None),
            P("dp", "seq", None),
            P("dp", None),
            P("dp", None),
            P("dp", None),
            P("dp"),
            P("dp"),
            P(("dp", "seq"), None, None),
            P(("dp", "seq"), None, None),
        ),
        check_vma=False,
    )
```

```python
import functools

import jax
import jax.numpy as jnp
from jax import lax
from jax.experimental import pallas as pl
from jax.experimental.pallas import tpu as pltpu
from jax.sharding import PartitionSpec as P

HEAD = 64
LANES = 128
SEG_COL = HEAD
LSE_COL = HEAD + 16
SEGMENTS = 16
FAR = 1e9
LARGE = 60 << 20
NT = (((1,), (1,)), ((), ()))
TN = (((0,), (0,)), ((), ()))
MESH = pl.DeviceIdType.MESH
EXPERTS_AT = LANES - 1
GAIN_AT = 32
F32 = jnp.float32
LOW = jnp.bfloat16


def dot(a, b):
    return jnp.dot(a, b, preferred_element_type=F32)


def dot_nt(a, b):
    return lax.dot_general(a, b, NT, preferred_element_type=F32)


def dot_tn(a, b):
    return lax.dot_general(a, b, TN, preferred_element_type=F32)


def thirds(values):
    high = values.astype(LOW).astype(F32)
    rest = values - high
    mid = rest.astype(LOW).astype(F32)
    return high, mid, rest - mid


def lanes_of(shape):
    return lax.broadcasted_iota(jnp.int32, shape, len(shape) - 1)


def put_thirds(base, values, column):
    lane = lanes_of(base.shape)
    high, mid, last = thirds(values)
    base = jnp.where(lane == column, high, base)
    base = jnp.where(lane == column + 1, mid, base)
    return jnp.where(lane == column + 2, last, base)


def normalize(values):
    center = values - jnp.mean(values, axis=-1, keepdims=True)
    inverse = lax.rsqrt(jnp.mean(center * center, axis=-1, keepdims=True) + 1e-05)
    return center * inverse, inverse


def norm_backward(upstream, scaled, inverse, gain_vec):
    direct = upstream * gain_vec
    return inverse * (
        direct
        - jnp.mean(direct, axis=-1, keepdims=True)
        - scaled * jnp.mean(direct * scaled, axis=-1, keepdims=True)
    )


def cost(micros):
    return pl.CostEstimate(flops=int(micros * 1e7), bytes_accessed=1 << 10, transcendentals=0)


def whole(*shape):
    return pl.BlockSpec(shape, lambda *_: (0,) * len(shape))


def remote(source, target, send, receive, device):
    return pltpu.make_async_remote_copy(
        src_ref=source,
        dst_ref=target,
        send_sem=send,
        recv_sem=receive,
        device_id=device,
        device_id_type=MESH,
    )


def each(count, body):
    def step(i, carry):
        body(i)
        return carry

    lax.fori_loop(0, count, step, 0)


def greet(base, place, planes, groups=None):
    me = lax.axis_index("dp")
    barrier = pltpu.get_barrier_semaphore()

    def signal(dp, z):
        pl.semaphore_signal(barrier, inc=1, device_id=(dp, z), device_id_type=MESH)

    def column(i):
        z = lax.rem(i, planes)

        @pl.when(z != place)
        def _():
            signal(base + i // planes, z)

    def plane(i):
        @pl.when(i != me)
        def _():
            signal(i, place)

    each(2 * planes, column)
    if groups is None:
        signal(2 * base + 1 - me, place)
        pl.semaphore_wait(barrier, 2 * (planes - 1) + 1)
    else:
        each(groups, plane)
        pl.semaphore_wait(barrier, 2 * (planes - 1) + groups - 1)


def front_kernel(
    groups, planes, te, acts, seg, up_in, near, rest, task, both_in,
    ids_out, x_out, qa_out, ka_out, va_out, att_out, attf_out, res_out, normed_out, up_out,
    gates_out, own_out, dx_out, near_out, rest_out, far_got, ga_got, gb_got,
    x, segx, up, both, other, near_all, rest_all, task_all, task_s, qa, ka, va, att, attf, res,
    normed, gates, slot, send_a, send_b, got_a, got_b, out, dx, far,
    sem_x, sem_seg, sem_on, sem_seg_on, sem_up, sem_up_on, sem_near, sem_rest, sem_task, sem_phase,
    sem_a, sem_b, sem_ga, sem_gb, sem_att, sem_far, local,
):
    me = lax.axis_index("dp")
    place = lax.axis_index("seq")
    core = lax.rem(me, 2)
    base = me - core
    partner = (base + 1 - core, place)
    band = 2 * (place // 2)
    mine = me * 2 + lax.rem(place, 2)
    piece, width = x.shape[1], x.shape[2]
    tokens = 2 * planes * piece
    half = tokens // 2
    rows = both.shape[2]
    heads = qa.shape[0]
    stays = (place // 2) == core
    spot = core + 2 * lax.rem(place, 2)

    greet_all(groups, planes)

    def goes(d):
        return jnp.logical_not(stays & (d == spot))

    def home_of(d):
        return (base + lax.rem(d, 2), 2 * core + d // 2)

    def token_copies(source, target, sem, sem_on, local_at):
        def send(d):
            return remote(source.at[d], target.at[place], sem.at[0, d], sem.at[1, place], home_of(d))

        at_home = pltpu.make_async_copy(source.at[spot], target.at[place], local.at[local_at])

        def start():
            def one(d):
                @pl.when(goes(d))
                def _():
                    send(d).start()

            each(planes, one)

            @pl.when(stays)
            def _():
                at_home.start()

        def onward(k):
            return remote(target.at[k], target.at[planes + k], sem_on.at[0, k], sem_on.at[1, k], partner)

        def receive(k):
            home = stays & (k == place)

            @pl.when(home)
            def _():
                at_home.wait()

            @pl.when(jnp.logical_not(home))
            def _():
                remote(source.at[0], target.at[k], sem.at[0, 0], sem.at[1, k], partner).wait_recv()

            onward(k).start()

        def finish():
            def one(d):
                @pl.when(goes(d))
                def _():
                    send(d).wait_send()

                onward(d).wait_send()

            each(planes, one)

        return start, receive, lambda k: onward(k).wait_recv(), finish

    x_start, x_receive, x_far, x_finish = token_copies(acts, x, sem_x, sem_on, 0)
    seg_start, seg_receive, seg_far, seg_finish = token_copies(seg, segx, sem_seg, sem_seg_on, 1)
    up_start, up_receive, up_far, up_finish = token_copies(up_in, up, sem_up, sem_up_on, 2)

    def others(body):
        def run(i):
            @pl.when(i != me)
            def _():
                body(i)

        each(groups, run)

    def give(source, target, sem, i):
        return remote(source, target.at[me], sem.at[0, i], sem.at[1, me], (i, place))

    def taken(source, target, sem, i):
        return remote(source, target.at[i], sem.at[0, i], sem.at[1, i], (i, place))

    def dense_of(i):
        return near.at[lax.rem(i, 2)]

    peer = (me, place + 2 - 4 * (place // 2))
    phase = remote(both_in, other, sem_phase.at[0], sem_phase.at[1], peer)

    def band_device(m):
        return (m // 2, band + lax.rem(m, 2))

    def band_copies(source, target, sem, local_at):
        def send(m):
            return remote(source.at[m], target.at[mine], sem.at[0, m], sem.at[1, mine], band_device(m))

        at_home = pltpu.make_async_copy(source.at[mine], target.at[mine], local.at[local_at])

        def start(first, count):
            def one(i):
                m = first + i

                @pl.when(m != mine)
                def _():
                    send(m).start()

                @pl.when(m == mine)
                def _():
                    at_home.start()

            each(count, one)

        def run(body, home):
            def one(m):
                @pl.when(m != mine)
                def _():
                    body(m)

                @pl.when(m == mine)
                def _():
                    home()

            each(2 * groups, one)

        def sent():
            run(lambda m: send(m).wait_send(), lambda: None)

        def received():
            run(
                lambda m: remote(
                    source.at[m], target.at[m], sem.at[0, m], sem.at[1, m], band_device(m)
                ).wait_recv(),
                at_home.wait,
            )

        return start, sent, received

    a_start, a_sent, a_received = band_copies(send_a, got_a, sem_a, 3)
    b_start, b_sent, b_received = band_copies(send_b, got_b, sem_b, 4)
    ga_start, ga_sent, ga_received = band_copies(send_a, ga_got, sem_ga, 5)
    gb_start, gb_sent, gb_received = band_copies(send_b, gb_got, sem_gb, 6)

    x_start()
    seg_start()
    others(lambda i: give(task, task_all, sem_task, i).start())
    others(lambda i: give(dense_of(i), near_all, sem_near, i).start())
    others(lambda i: give(rest, rest_all, sem_rest, i).start())
    own_task = pltpu.make_async_copy(task, task_all.at[me], local.at[7])
    own_near = pltpu.make_async_copy(near.at[core], near_all.at[me], local.at[8])
    own_rest = pltpu.make_async_copy(rest, rest_all.at[me], local.at[9])
    own_both = pltpu.make_async_copy(both_in, both, local.at[10])
    for copy in (own_task, own_near, own_rest, own_both):
        copy.start()
    others(lambda i: taken(task, task_all, sem_task, i).wait_recv())
    own_task.wait()
    to_scalars = pltpu.make_async_copy(task_all, task_s, local.at[7])
    to_scalars.start()
    to_scalars.wait()

    def expert_of(dp, z):
        at = z // 2 + dp - lax.rem(dp, 2)
        return te[task_s[at, 0, lax.rem(z, 2)], lax.rem(dp, 2)]

    def note(m):
        dp, z = band_device(m)
        ids_out[m] = expert_of(dp, z)

    each(2 * groups, note)
    ids_out[2 * groups] = expert_of(me, place)
    ids_out[2 * groups + 1] = expert_of(partner[0], place)
    mine_id = expert_of(me, place)
    other_id = expert_of(partner[0], place)

    def choose(source, target):
        def one(m):
            dp, z = band_device(m)
            e = expert_of(dp, z)
            target[m, 0] = source[0, e]
            target[m, 1] = source[1, e]

        each(2 * groups, one)

    own_both.wait()
    choose(both, send_a)
    others(lambda i: taken(near.at[0], near_all, sem_near, i).wait_recv())
    others(lambda i: taken(rest, rest_all, sem_rest, i).wait_recv())
    own_near.wait()
    own_rest.wait()
    keep = []

    def save(source, target):
        copy = pltpu.make_async_copy(source, target, local.at[11 + len(keep)])
        copy.start()
        keep.append(copy)

    save(near_all, near_out)
    save(rest_all, rest_out)

    small = rest_all[...].reshape(width, rest_all.shape[2])[:, width:].astype(F32).T
    first_gain = small[GAIN_AT : GAIN_AT + 1]
    second_gain = small[GAIN_AT + 1 : GAIN_AT + 2]
    lane = lanes_of((piece, LANES))

    def project(slot_at):
        scaled, _ = normalize(x[slot_at].astype(F32))
        low = (scaled * first_gain).astype(LOW)
        weight = near_all[...].reshape(width, near_all.shape[2])
        values = dot(low, weight)
        segment = jnp.broadcast_to(segx[slot_at].astype(F32), (LANES, piece)).T
        same = (lane - SEG_COL).astype(F32) == segment
        in_seg = (lane >= SEG_COL) & (lane < SEG_COL + SEGMENTS)
        q_more = jnp.where(same, 1.0, 0.0)
        k_more = jnp.where(in_seg & jnp.logical_not(same), -FAR, 0.0)
        k_more = jnp.where((lane >= LSE_COL) & (lane < LSE_COL + 3), 1.0, k_more)
        v_more = jnp.where((lane >= HEAD) & (lane < HEAD + 3), 1.0, 0.0)
        r = pl.ds(pl.multiple_of(slot_at * piece, piece), piece)

        def head(kind, h, more):
            at = kind * heads * HEAD + h // 2 * LANES
            part = values[:, at : at + LANES]
            if h % 2:
                part = pltpu.roll(part, HEAD, 1)
            return jnp.where(lane < HEAD, part, more)

        for h in range(heads):
            query = head(0, h, 0.0).astype(LOW).astype(F32) * HEAD**-0.5
            qa[h, r, :] = (query + q_more).astype(LOW)
            ka[h, r, :] = head(1, h, k_more).astype(LOW)
            va[h, r, :] = head(2, h, v_more).astype(LOW)

    def arrive(k):
        k = lax.rem(place + k, planes)
        x_receive(k)
        seg_receive(k)

    each(planes, arrive)
    phase.start()
    a_start(0, 2 * groups)
    up_start()

    def near_piece(k):
        project(lax.rem(place + k, planes))

    each(planes, near_piece)

    def far_piece(k):
        x_far(k)
        seg_far(k)
        project(planes + k)

    each(planes, far_piece)
    save(x, x_out)
    save(ka, ka_out)
    save(va, va_out)

    block = min(512, half)

    def att_copy(p):
        return remote(att.at[p], attf.at[p], sem_att.at[0, p], sem_att.at[1, p], partner)

    for p in range(heads // 2):

        def attend(i):
            r = pl.ds(pl.multiple_of(i * block, block), block)
            parts = []
            for h in (2 * p, 2 * p + 1):
                query = qa[h, r, :]
                scores = dot_nt(query, ka[h])
                top = jnp.max(scores, axis=1, keepdims=True)
                probs = jnp.exp(scores - top).astype(LOW)
                mixed = dot(probs, va[h])
                total = mixed[:, HEAD : HEAD + 1]
                parts.append(mixed[:, :HEAD] / total)
                lse = top + jnp.log(total)
                qa[h, r, :] = put_thirds(query.astype(F32), -lse, LSE_COL).astype(LOW)
            att[p, r, :] = jnp.concatenate(parts, axis=1).astype(LOW)

        each(tokens // block, attend)
        att_copy(p).start()
    save(qa, qa_out)
    save(att, att_out)

    phase.wait_recv()
    choose(other, send_b)
    b_start(0, 2 * groups)
    each(planes, lambda k: up_receive(lax.rem(place + k, planes)))
    for p in range(heads // 2):
        att_copy(p).wait_recv()
    save(attf, attf_out)
    each(planes, up_far)
    save(up.at[pl.ds(0, planes)], up_out)

    def weight_rows(which):
        part = rest_all[pl.ds(which * (groups // 2), groups // 2)]
        return part.reshape(width // 2, rest_all.shape[2])[:, :width]

    def middle(b):
        r = pl.ds(pl.multiple_of(b * piece, piece), piece)
        f = pl.ds(pl.multiple_of(lax.rem(b + planes, 2 * planes) * piece, piece), piece)
        residual = x[b].astype(F32)
        pairs = range(heads // 2)
        residual += dot(jnp.concatenate([att[p, r, :] for p in pairs], axis=1), weight_rows(core))
        residual += dot(
            jnp.concatenate([attf[p, f, :] for p in pairs], axis=1), weight_rows(1 - core)
        )

        @pl.when(b < planes)
        def _():
            res[r, :] = residual

        scaled, _ = normalize(residual)
        low = (scaled * second_gain).astype(LOW)
        normed[r, :] = low
        logits = dot(low, rest_all[...].reshape(width, rest_all.shape[2])[:, width:])
        of_mine = jnp.sum(jnp.where(lane == mine_id, logits, 0.0), axis=1, keepdims=True)
        of_other = jnp.sum(jnp.where(lane == other_id, logits, 0.0), axis=1, keepdims=True)
        top = jnp.maximum(of_mine, of_other)
        of_mine = jnp.exp(of_mine - top)
        of_other = jnp.exp(of_other - top)
        total = of_mine + of_other
        gate = of_mine / total
        gates[r, :] = jnp.where(lane == 0, gate, jnp.where(lane == 1, of_other / total, 0.0))
        slot[r, :] = (gate * up[b].astype(F32)).astype(LOW)

    each(2 * planes, middle)
    save(res, res_out)
    save(normed.at[pl.ds(0, half)], normed_out)

    out[...] = jnp.zeros_like(out)
    dx[...] = jnp.zeros_like(dx)
    per = max(1, 256 // rows)

    def expert(source, target, start):
        def tile(t):
            at = pl.ds(t * per, per)
            win = source[at, 0].reshape(per * rows, width)
            wout = source[at, 1].reshape(per * rows, width)
            pre = dot_nt(normed[...], win)
            hidden_grad = dot_nt(slot[...], wout)
            cdf = 0.5 * (1.0 + lax.erf(pre * 0.7071067811865476))
            slope = cdf + pre * jnp.exp(-0.5 * pre * pre) * 0.3989422804014327
            hidden = (pre * cdf).astype(LOW)
            pre_grad = (hidden_grad * slope).astype(LOW)
            out[...] += dot(hidden, wout)
            dx[...] += dot(pre_grad, win)
            target[at, 0] = dot_tn(pre_grad, normed[...]).astype(LOW).reshape(per, rows, width)
            target[at, 1] = dot_tn(hidden, slot[...]).astype(LOW).reshape(per, rows, width)
            start(t * per, per)

        each(2 * groups // per, tile)

    a_received()
    a_sent()
    expert(got_a, send_a, ga_start)
    b_received()
    b_sent()
    expert(got_b, send_b, gb_start)

    step = half // 2
    for at in range(0, tokens, step):
        r = pl.ds(at, step)
        value = out[r, :]
        grads = up[pl.ds(at // piece, step // piece)].reshape(step, width).astype(F32)
        gate_grad = jnp.sum(value * grads, axis=1, keepdims=True)
        value = value * gates[r, 0:1]
        tail = put_thirds(jnp.zeros((step, LANES), F32), gate_grad, 0)
        if at < half:
            out[r, :] = value
            gates[r, :] = gates[r, :] + pltpu.roll(tail, 2, 1)
        else:
            t = pl.ds(at - half, step)
            far[t, :width] = value.astype(LOW)
            far[t, width : 2 * width] = dx[r, :].astype(LOW)
            far[t, 2 * width :] = tail.astype(LOW)
    far_copy = remote(far, far_got, sem_far.at[0], sem_far.at[1], partner)
    far_copy.start()
    save(out.at[pl.ds(0, half)], own_out)
    save(dx.at[pl.ds(0, half)], dx_out)
    save(gates.at[pl.ds(0, half)], gates_out)

    phase.wait_send()
    x_finish()
    seg_finish()
    up_finish()
    for p in range(heads // 2):
        att_copy(p).wait_send()

    def end_dense(i):
        give(task, task_all, sem_task, i).wait_send()
        give(dense_of(i), near_all, sem_near, i).wait_send()
        give(rest, rest_all, sem_rest, i).wait_send()

    others(end_dense)
    for copy in keep:
        copy.wait()
    ga_sent()
    ga_received()
    gb_sent()
    gb_received()
    far_copy.wait()


def greet_all(groups, planes):
    me = lax.axis_index("dp")
    place = lax.axis_index("seq")
    base = me - lax.rem(me, 2)
    band = 2 * (place // 2)
    barrier = pltpu.get_barrier_semaphore()

    def signal(dp, z):
        pl.semaphore_signal(barrier, inc=1, device_id=(dp, z), device_id_type=MESH)

    def near_planes(m):
        dp, z = m // 2, band + lax.rem(m, 2)

        @pl.when(jnp.logical_not((dp == me) & (z == place)))
        def _():
            signal(dp, z)

    def far_planes(i):
        signal(base + i // 2, 2 - band + lax.rem(i, 2))

    each(2 * groups, near_planes)
    each(4, far_planes)
    pl.semaphore_wait(barrier, 2 * groups + 3)


def front(te, acts, seg, up_in, near, rest, task, both, groups, planes):
    _, piece, width = acts.shape
    half = planes * piece
    tokens = 2 * half
    heads = width // HEAD // 2
    experts, rows = both.shape[1], both.shape[2]
    count = 2 * groups
    anywhere = pl.BlockSpec(memory_space=pl.ANY)
    scalars = pl.BlockSpec(memory_space=pltpu.SMEM)
    dma = pltpu.SemaphoreType.DMA
    S = lambda shape, t: jax.ShapeDtypeStruct(shape, t)
    head_shape = (heads, tokens, LANES)
    pair_shape = (heads // 2, tokens, LANES)
    band_shape = (count, 2, rows, width)
    far_shape = (half, 2 * width + LANES)
    near_shape = (groups,) + near.shape[1:]
    rest_shape = (groups,) + rest.shape
    return pl.pallas_call(
        functools.partial(front_kernel, groups, planes),
        in_specs=[scalars] + [anywhere] * 7,
        out_specs=[scalars] + [anywhere] * 17,
        out_shape=[
            S((count + 2,), jnp.int32),
            S((2 * planes, piece, width), LOW),
            S(head_shape, LOW),
            S(head_shape, LOW),
            S(head_shape, LOW),
            S(pair_shape, LOW),
            S(pair_shape, LOW),
            S((half, width), F32),
            S((half, width), LOW),
            S((planes, piece, width), LOW),
            S((half, LANES), F32),
            S((half, width), F32),
            S((half, width), F32),
            S(near_shape, LOW),
            S(rest_shape, LOW),
            S(far_shape, LOW),
            S(band_shape, LOW),
            S(band_shape, LOW),
        ],
        scratch_shapes=[
            pltpu.VMEM((2 * planes, piece, width), LOW),
            pltpu.VMEM((2 * planes, 1, piece), jnp.int32),
            pltpu.VMEM((2 * planes, piece, width), LOW),
            pltpu.VMEM(both.shape, LOW),
            pltpu.VMEM(both.shape, LOW),
            pltpu.VMEM(near_shape, LOW),
            pltpu.VMEM(rest_shape, LOW),
            pltpu.VMEM((groups, 1, LANES), jnp.int32),
            pltpu.SMEM((groups, 1, LANES), jnp.int32),
            pltpu.VMEM(head_shape, LOW),
            pltpu.VMEM(head_shape, LOW),
            pltpu.VMEM(head_shape, LOW),
            pltpu.VMEM(pair_shape, LOW),
            pltpu.VMEM(pair_shape, LOW),
            pltpu.VMEM((half, width), F32),
            pltpu.VMEM((tokens, width), LOW),
            pltpu.VMEM((tokens, LANES), F32),
            pltpu.VMEM((tokens, width), LOW),
            pltpu.VMEM(band_shape, LOW),
            pltpu.VMEM(band_shape, LOW),
            pltpu.VMEM(band_shape, LOW),
            pltpu.VMEM(band_shape, LOW),
            pltpu.VMEM((tokens, width), F32),
            pltpu.VMEM((tokens, width), F32),
            pltpu.VMEM(far_shape, LOW),
        ]
        + [dma((2, planes))] * 6
        + [dma((2, groups))] * 3
        + [dma((2,))]
        + [dma((2, count))] * 4
        + [dma((2, heads // 2)), dma((2,)), dma((32,))],
        compiler_params=pltpu.CompilerParams(
            collective_id=0, has_side_effects=True, vmem_limit_bytes=LARGE
        ),
        cost_estimate=cost(130),
        name="front",
    )(te, acts, seg, up_in, near, rest, task, both)


def back_kernel(
    groups, planes, ids, x_in, qa_in, ka_in, va_in, att_in, attf_in, res_in, normed_in, up_in,
    gates_in, own_in, dx_in, near_in, rest_in, far_in, ga_in, sums,
    tokens_out, grads_out, total_out, win_out, wout_out,
    x, qa, ka, va, att, attf, res, normed, up, gates, own, dx, near_w, rest_w, far, ga, other,
    outputs, res_grad, att_grad, att_send, attn_acc, router_acc, gain_acc, rest_part, rest_got,
    dqkv, gb, key_t, dq_acc, qkv_acc, first_acc, back_near, back_send, back_got, qkv_part, qkv_got,
    out_grads, part, heard, summed, win_grad, wout_grad,
    sem_phase, sem_out, sem_att, sem_rest, sem_back, sem_qkv, sem_in, sem_part, sem_sum, local,
):
    me = lax.axis_index("dp")
    place = lax.axis_index("seq")
    core = lax.rem(me, 2)
    base = me - core
    partner = (base + 1 - core, place)
    piece, width = x.shape[1], x.shape[2]
    half = planes * piece
    tokens = 2 * half
    heads = qa.shape[0]
    pairs = heads // 2
    stays = (place // 2) == core
    spot = core + 2 * lax.rem(place, 2)
    near_width = heads * HEAD
    experts, rows = other.shape[1], other.shape[2]
    used = [0]

    def load(source, target):
        copy = pltpu.make_async_copy(source, target, local.at[used[0]])
        used[0] += 1
        copy.start()
        return copy

    early = [
        load(res_in, res),
        load(own_in, own),
        load(dx_in, dx),
        load(far_in, far),
        load(gates_in, gates),
        load(up_in, up),
        load(normed_in, normed),
        load(rest_in, rest_w),
        load(att_in, att),
        load(attf_in.at[:, pl.ds(half, half)], attf),
    ]
    late = [load(qa_in, qa), load(ka_in, ka), load(va_in, va)]
    last = [load(x_in, x), load(near_in, near_w), load(ga_in, ga)]
    greet(base, place, planes, groups)

    peer = (me, place + 2 - 4 * (place // 2))
    phase = remote(sums, other, sem_phase.at[0], sem_phase.at[1], peer)
    phase.start()

    def others(body):
        def run(i):
            @pl.when(i != me)
            def _():
                body(i)

        each(groups, run)

    def give(source, target, sem, i):
        return remote(source.at[i], target.at[me], sem.at[0, i], sem.at[1, me], (i, place))

    def taken(source, target, sem, i):
        return remote(source.at[i], target.at[i], sem.at[0, i], sem.at[1, i], (i, place))

    def way_back(source, target, sem, local_at):
        def send(slot):
            return remote(
                source.at[slot],
                target.at[spot],
                sem.at[0, slot],
                sem.at[1, spot],
                (base + place // 2, slot),
            )

        at_home = pltpu.make_async_copy(source.at[place], target.at[spot], local.at[local_at])

        def start(slot):
            home = stays & (slot == place)

            @pl.when(jnp.logical_not(home))
            def _():
                send(slot).start()

            @pl.when(home)
            def _():
                at_home.start()

        def end(d):
            @pl.when(jnp.logical_not(stays & (d == place)))
            def _():
                send(d).wait_send()

            @pl.when(jnp.logical_not(stays & (d == spot)))
            def _():
                remote(source.at[0], target.at[d], sem.at[0, 0], sem.at[1, d], partner).wait_recv()

            @pl.when(stays & (d == place))
            def _():
                at_home.wait()

        return start, lambda: each(planes, end)

    out_start, out_end = way_back(outputs, tokens_out, sem_out, 24)
    in_start, in_end = way_back(out_grads, grads_out, sem_in, 25)

    for copy in early:
        copy.wait()
    attn_acc[...] = jnp.zeros_like(attn_acc)
    router_acc[...] = jnp.zeros_like(router_acc)
    gain_acc[...] = jnp.zeros_like(gain_acc)
    lane = lanes_of((piece, LANES))
    small = rest_w[...].reshape(width, rest_w.shape[2])[:, width:].astype(F32).T
    first_gain = small[GAIN_AT : GAIN_AT + 1]
    second_gain = small[GAIN_AT + 1 : GAIN_AT + 2]
    mine_id = ids[2 * groups]
    other_id = ids[2 * groups + 1]

    def weight_rows(which):
        values = rest_w[pl.ds(which * (groups // 2), groups // 2)]
        return values.reshape(width // 2, rest_w.shape[2])[:, :width]

    def post(b):
        r = pl.ds(pl.multiple_of(b * piece, piece), piece)
        residual = res[r, :]
        upstream = up[b].astype(F32)
        outputs[b] = (residual + own[r, :] + far[r, :width].astype(F32)).astype(LOW)
        out_start(b)
        gate = gates[r, :]
        gate_mine, gate_other = gate[:, 0:1], gate[:, 1:2]
        grad_mine = jnp.sum(jnp.where((lane >= 2) & (lane < 5), gate, 0.0), axis=1, keepdims=True)
        grad_other = jnp.sum(far[r, 2 * width :].astype(F32), axis=1, keepdims=True)
        mean = gate_mine * grad_mine + gate_other * grad_other
        logit_grad = jnp.where(lane == mine_id, gate_mine * (grad_mine - mean), 0.0)
        logit_grad += jnp.where(lane == other_id, gate_other * (grad_other - mean), 0.0)
        normed_grad = dx[r, :] + far[r, width : 2 * width].astype(F32)
        router = rest_w[...].reshape(width, rest_w.shape[2])[:, width:]
        for third in thirds(logit_grad):
            third = third.astype(LOW)
            router_acc[...] += dot_tn(normed[r, :], third)
            normed_grad += dot_nt(third, router)
        scaled, inverse = normalize(residual)
        gain_acc[...] += jnp.sum(normed_grad * scaled, axis=0, keepdims=True)
        residual_grad = upstream + norm_backward(normed_grad, scaled, inverse, second_gain)
        res_grad[r, :] = residual_grad
        low = residual_grad.astype(LOW)
        both_att = [att[p, r, :] for p in range(pairs)] + [attf[p, r, :] for p in range(pairs)]
        for i, part_att in enumerate(both_att):
            attn_acc[i * LANES : (i + 1) * LANES] += dot_tn(part_att, low)
        near_back = dot_nt(low, weight_rows(core)).astype(LOW)
        far_back = dot_nt(low, weight_rows(1 - core)).astype(LOW)
        for p in range(pairs):
            att_grad[p, r, :] = near_back[:, p * LANES : (p + 1) * LANES]
            att_send[p, r, :] = far_back[:, p * LANES : (p + 1) * LANES]

    each(planes, post)

    def att_copy(p):
        return remote(
            att_send.at[p],
            att_grad.at[p, pl.ds(half, half)],
            sem_att.at[0, p],
            sem_att.at[1, p],
            partner,
        )

    for p in range(pairs):
        att_copy(p).start()
    dense_rows = rest_part.shape[1]
    own_rows = near_width // dense_rows
    turned = jnp.broadcast_to(gain_acc[...], (LANES, width)).T
    wide_lane = lanes_of(turned.shape)
    tail = jnp.where(wide_lane == EXPERTS_AT, turned, router_acc[...]).astype(LOW)
    rest_part[:, :, width:] = tail.reshape(groups, dense_rows, LANES)
    for side in range(2):
        values = attn_acc[side * near_width : (side + 1) * near_width].astype(LOW)
        at = core if side == 0 else 1 - core
        rest_part[pl.ds(at * own_rows, own_rows), :, :width] = values.reshape(
            own_rows, dense_rows, width
        )
    others(lambda i: give(rest_part, rest_got, sem_rest, i).start())

    for copy in late:
        copy.wait()
    block = min(512, half)
    all_lane = lanes_of((tokens, LANES))
    for p in range(pairs):
        att_copy(p).wait_recv()
        halves = []
        for side in range(2):
            h = 2 * p + side
            pair_grad = att_grad[p].astype(F32)
            inner = pair_grad * att[p].astype(F32)
            if side == 1:
                pair_grad = pltpu.roll(pair_grad, HEAD, 1)
                inner = pltpu.roll(inner, HEAD, 1)
            delta = jnp.sum(jnp.where(all_lane < HEAD, inner, 0.0), axis=1, keepdims=True)
            pair_grad = jnp.where(all_lane < HEAD, pair_grad, 0.0)
            gb[...] = put_thirds(pair_grad, -delta, HEAD).astype(LOW)
            key_t[...] = ka[h].T[:HEAD]
            dq_acc[...] = jnp.zeros_like(dq_acc)
            cols = pl.ds(side * HEAD, HEAD)

            def keys(i):
                r = pl.ds(pl.multiple_of(i * block, block), block)
                weights = jnp.exp(dot_nt(ka[h, r, :], qa[h]))
                centered = dot_nt(va[h, r, :], gb[...])
                score_grad = (weights * centered).astype(LOW)
                dqkv[2 * pairs + p, r, cols] = dot(weights.astype(LOW), gb[...])[:, :HEAD].astype(LOW)
                dqkv[pairs + p, r, cols] = dot(score_grad, qa[h])[:, :HEAD].astype(LOW)
                dq_acc[...] += dot(key_t[:, r], score_grad)

            each(tokens // block, keys)
            halves.append(dq_acc[...].T * HEAD**-0.5)
        dqkv[p] = jnp.concatenate(halves, axis=1).astype(LOW)

    for copy in last:
        copy.wait()
    qkv_acc[...] = jnp.zeros_like(qkv_acc)
    first_acc[...] = jnp.zeros_like(first_acc)

    def project_back(b):
        r = pl.ds(pl.multiple_of(b * piece, piece), piece)
        values = jnp.concatenate([dqkv[i, r, :] for i in range(3 * pairs)], axis=1)
        scaled, _ = normalize(x[b].astype(F32))
        back = dot_nt(values, near_w[...].reshape(width, near_w.shape[2]))
        qkv_acc[...] += dot_tn((scaled * first_gain).astype(LOW), values)
        first_acc[...] += jnp.sum(back * scaled, axis=0, keepdims=True)
        return back

    def far_block(i):
        back = project_back(planes + i)
        back_send[pl.ds(pl.multiple_of(i * piece, piece), piece), :] = back.astype(LOW)

    def near_block(i):
        back_near[pl.ds(pl.multiple_of(i * piece, piece), piece), :] = project_back(i)

    each(planes, far_block)
    back_copy = remote(back_send, back_got, sem_back.at[0], sem_back.at[1], partner)
    back_copy.start()
    each(planes, near_block)
    near_cols = near_w.shape[2]
    qkv_part[:, :, :near_cols] = qkv_acc[...].astype(LOW).reshape(groups, dense_rows, near_cols)
    turned = jnp.broadcast_to(first_acc[...], (LANES, width)).T.astype(LOW)
    qkv_part[:, :, near_cols:] = turned.reshape(groups, dense_rows, LANES)
    others(lambda i: give(qkv_part, qkv_got, sem_qkv, i).start())

    back_copy.wait_recv()

    def finish(b):
        r = pl.ds(pl.multiple_of(b * piece, piece), piece)
        scaled, inverse = normalize(x[b].astype(F32))
        grad = back_near[r, :] + back_got[r, :].astype(F32)
        first = norm_backward(grad, scaled, inverse, first_gain)
        out_grads[b] = (res_grad[r, :] + first).astype(LOW)
        in_start(b)

    each(planes, finish)

    others(lambda i: taken(qkv_part, qkv_got, sem_qkv, i).wait_recv())
    others(lambda i: taken(rest_part, rest_got, sem_rest, i).wait_recv())

    def from_group(mine_part, got, i):
        return jnp.where(i == me, mine_part[i], got[i]).astype(F32)

    def add(j, sums_of):
        first, second, rest = sums_of
        first += from_group(qkv_part, qkv_got, 2 * j)
        second += from_group(qkv_part, qkv_got, 2 * j + 1)
        rest += from_group(rest_part, rest_got, 2 * j)
        rest += from_group(rest_part, rest_got, 2 * j + 1)
        return first, second, rest

    zero = jnp.zeros(qkv_part.shape[1:], F32)
    first, second, rest = lax.fori_loop(
        0, groups // 2, add, (zero, zero, jnp.zeros(rest_part.shape[1:], F32))
    )
    columns = []
    for kind in range(3):
        for side in (first, second):
            columns.append(side[:, kind * near_width : (kind + 1) * near_width])
    columns += [rest, first[:, near_cols:] + second[:, near_cols:]]
    share = jnp.concatenate(columns, axis=1).astype(LOW)
    cut = dense_rows // planes
    for z in range(planes):
        part[z] = share[z * cut : (z + 1) * cut]

    def over_planes(body):
        def run(z):
            @pl.when(z != place)
            def _():
                body(z)

        each(planes, run)

    def tell_part(z):
        return remote(part.at[z], heard.at[place], sem_part.at[0, z], sem_part.at[1, place], (me, z))

    def hear_part(z):
        return remote(part.at[z], heard.at[z], sem_part.at[0, z], sem_part.at[1, z], (me, z))

    def tell_sum(z):
        return remote(summed, total_out.at[place], sem_sum.at[0, z], sem_sum.at[1, place], (me, z))

    def hear_sum(z):
        return remote(summed, total_out.at[z], sem_sum.at[0, z], sem_sum.at[1, z], (me, z))

    over_planes(lambda z: tell_part(z).start())

    phase.wait_recv()
    for e in range(experts):
        for kind, grad in ((0, win_grad), (1, wout_grad)):

            def source(m, acc):
                return acc + jnp.where(ids[m] == e, ga[m, kind].astype(F32), 0.0)

            grad[:, e, :] = lax.fori_loop(0, 2 * groups, source, other[kind, e].astype(F32))
    keep_in = pltpu.make_async_copy(win_grad, win_out, local.at[26])
    keep_out = pltpu.make_async_copy(wout_grad, wout_out, local.at[27])
    keep_in.start()
    keep_out.start()

    over_planes(lambda z: hear_part(z).wait_recv())
    sum_of = part[place].astype(F32)
    for k in range(1, planes):
        sum_of += heard[lax.rem(place + k, planes)].astype(F32)
    summed[...] = sum_of.astype(LOW)
    over_planes(lambda z: tell_sum(z).start())
    put = pltpu.make_async_copy(summed, total_out.at[place], local.at[28])
    put.start()

    phase.wait_send()
    back_copy.wait_send()
    for p in range(pairs):
        att_copy(p).wait_send()
    others(lambda i: give(rest_part, rest_got, sem_rest, i).wait_send())
    others(lambda i: give(qkv_part, qkv_got, sem_qkv, i).wait_send())
    over_planes(lambda z: tell_part(z).wait_send())
    over_planes(lambda z: tell_sum(z).wait_send())
    over_planes(lambda z: hear_sum(z).wait_recv())
    put.wait()
    keep_in.wait()
    keep_out.wait()
    out_end()
    in_end()


def back(ids, saved, sums, groups, planes, experts):
    x, qa, ka, va, att, attf, res, normed, up, gates, own, dx, near, rest, far, ga = saved
    _, piece, width = x.shape
    half = planes * piece
    tokens = 2 * half
    heads = qa.shape[0]
    dense_rows = near.shape[1]
    near_cols = near.shape[2]
    rows = ga.shape[2]
    total = (planes, dense_rows // planes, 4 * width + 2 * LANES)
    anywhere = pl.BlockSpec(memory_space=pl.ANY)
    dma = pltpu.SemaphoreType.DMA
    S = lambda shape, t: jax.ShapeDtypeStruct(shape, t)
    V = lambda shape, t=LOW: pltpu.VMEM(shape, t)
    pair_half = (heads // 2, half, LANES)
    return pl.pallas_call(
        functools.partial(back_kernel, groups, planes),
        in_specs=[pl.BlockSpec(memory_space=pltpu.SMEM)] + [anywhere] * 17,
        out_specs=[anywhere] * 5,
        out_shape=[
            S((planes, piece, width), LOW),
            S((planes, piece, width), LOW),
            S(total, LOW),
            S((rows, experts, width), F32),
            S((rows, experts, width), F32),
        ],
        scratch_shapes=[
            V(x.shape),
            V(qa.shape),
            V(ka.shape),
            V(va.shape),
            V(att.shape),
            V(pair_half),
            V(res.shape, F32),
            V(normed.shape),
            V(up.shape),
            V(gates.shape, F32),
            V(own.shape, F32),
            V(dx.shape, F32),
            V(near.shape),
            V(rest.shape),
            V(far.shape),
            V(ga.shape),
            V(sums.shape),
            V(up.shape),
            V(res.shape, F32),
            V(att.shape),
            V(pair_half),
            V((width, width), F32),
            V((width, LANES), F32),
            V((1, width), F32),
            V(rest.shape),
            V(rest.shape),
            V((3 * heads // 2, tokens, LANES)),
            V((tokens, LANES)),
            V((HEAD, tokens)),
            V((HEAD, tokens), F32),
            V((width, near_cols), F32),
            V((1, width), F32),
            V((half, width), F32),
            V((half, width)),
            V((half, width)),
            V((groups, dense_rows, near_cols + LANES)),
            V((groups, dense_rows, near_cols + LANES)),
            V(up.shape),
            V(total),
            V(total),
            V(total[1:]),
            V((rows, experts, width), F32),
            V((rows, experts, width), F32),
            dma((2,)),
            dma((2, planes)),
            dma((2, heads // 2)),
            dma((2, groups)),
            dma((2,)),
            dma((2, groups)),
            dma((2, planes)),
            dma((2, planes)),
            dma((2, planes)),
            dma((32,)),
        ],
        compiler_params=pltpu.CompilerParams(
            collective_id=1, has_side_effects=True, vmem_limit_bytes=LARGE
        ),
        cost_estimate=cost(110),
        name="back",
    )(ids, *saved, sums)


def partial_kernel(ids, grads, out, acc_in, acc_out):
    acc_in[...] = jnp.zeros_like(acc_in)
    acc_out[...] = jnp.zeros_like(acc_out)

    def add(i):
        acc_in[ids[i]] += grads[i, 0].astype(F32)
        acc_out[ids[i]] += grads[i, 1].astype(F32)

    each(grads.shape[0], add)
    out[0] = acc_in[...].astype(LOW)
    out[1] = acc_out[...].astype(LOW)


def partial_sums(ids, grads, experts):
    _, _, rows, width = grads.shape
    packed = (2, experts, rows, width)
    return pl.pallas_call(
        partial_kernel,
        grid_spec=pltpu.PrefetchScalarGridSpec(
            num_scalar_prefetch=1,
            grid=(1,),
            in_specs=[whole(*grads.shape)],
            out_specs=whole(*packed),
            scratch_shapes=[pltpu.VMEM((experts, rows, width), F32)] * 2,
        ),
        out_shape=jax.ShapeDtypeStruct(packed, LOW),
        compiler_params=pltpu.CompilerParams(vmem_limit_bytes=LARGE),
        cost_estimate=cost(4),
        name="partial_sums",
    )(ids, grads)


def local(
    activations, qkv_weight, attn_weight, router_weight, gain_one, gain_two,
    expert_in, expert_out, segments, task_ids, task_experts, out_grad,
):
    packs, length, width = activations.shape
    planes = lax.axis_size("seq")
    groups = lax.axis_size("dp")
    cuts = 2 * packs
    assert cuts == planes == 4 and groups % 2 == 0
    piece = length // 2
    experts = router_weight.shape[1]
    dense_rows = qkv_weight.shape[0]
    near_width = width // 2
    assert experts <= GAIN_AT

    near = jnp.swapaxes(qkv_weight.reshape(dense_rows, 3, 2, near_width), 0, 2)
    near = jnp.swapaxes(near, 1, 2).reshape(2, dense_rows, 3 * near_width)
    rest = jnp.concatenate(
        [attn_weight, router_weight, jnp.zeros((dense_rows, GAIN_AT - experts), LOW)]
        + [gain_one[:, None], gain_two[:, None]]
        + [jnp.zeros((dense_rows, LANES - GAIN_AT - 2), LOW)],
        axis=1,
    )
    task = jnp.pad(task_ids[:, 0][None], ((0, 0), (0, LANES - packs)))
    both = jnp.stack([jnp.swapaxes(expert_in, 0, 1), jnp.swapaxes(expert_out, 0, 1)])
    ids, *saved = front(
        task_experts,
        activations.reshape(cuts, piece, width),
        segments.reshape(cuts, 1, piece),
        out_grad.astype(LOW).reshape(cuts, piece, width),
        near,
        rest,
        task,
        both,
        groups,
        planes,
    )
    sums = partial_sums(ids, saved[-1], experts)
    outputs, input_grad, total, win_grad, wout_grad = back(
        ids, saved[:-1], sums, groups, planes, experts
    )
    total = total.reshape(dense_rows, -1).astype(F32)
    at = 4 * width
    return (
        outputs.reshape(packs, length, width),
        input_grad.reshape(packs, length, width).astype(F32),
        total[:, : 3 * width],
        total[:, 3 * width : at],
        total[:, at : at + experts],
        total[:, at + LANES],
        total[:, at + EXPERTS_AT],
        win_grad,
        wout_grad,
    )


def solution(mesh):
    placed = (
        P("dp", "seq", None),
        P("dp", None),
        P("dp", None),
        P("dp", None),
        P("dp"),
        P("dp"),
        P(("dp", "seq"), None, None),
        P(("dp", "seq"), None, None),
        P("dp", "seq"),
        P("dp", "seq"),
        P(),
        P("dp", "seq", None),
    )
    return jax.shard_map(
        local,
        mesh=mesh,
        in_specs=placed,
        out_specs=(
            P("dp", "seq", None),
            P("dp", "seq", None),
            P("dp", None),
            P("dp", None),
            P("dp", None),
            P("dp"),
            P("dp"),
            P(("dp", "seq"), None, None),
            P(("dp", "seq"), None, None),
        ),
        check_vma=False,
    )
```

```python
import functools

import jax
import jax.numpy as jnp
from jax import lax
from jax.experimental import pallas as pl
from jax.experimental.pallas import tpu as pltpu
from jax.sharding import PartitionSpec as P

HEAD = 64
LANES = 128
SEG_COL = HEAD
LSE_COL = HEAD + 16
SEGMENTS = 16
FAR = 1e9
LARGE = 60 << 20
NT = (((1,), (1,)), ((), ()))
TN = (((0,), (0,)), ((), ()))
MESH = pl.DeviceIdType.MESH
EXPERTS_AT = LANES - 1
TINY = 16
F32 = jnp.float32
LOW = jnp.bfloat16


def dot(a, b):
    return jnp.dot(a, b, preferred_element_type=F32)


def dot_nt(a, b):
    return lax.dot_general(a, b, NT, preferred_element_type=F32)


def dot_tn(a, b):
    return lax.dot_general(a, b, TN, preferred_element_type=F32)


def thirds(values):
    high = values.astype(LOW).astype(F32)
    rest = values - high
    mid = rest.astype(LOW).astype(F32)
    return high, mid, rest - mid


def lanes_of(shape):
    return lax.broadcasted_iota(jnp.int32, shape, len(shape) - 1)


def put_thirds(base, values, column):
    lane = lanes_of(base.shape)
    high, mid, last = thirds(values)
    base = jnp.where(lane == column, high, base)
    base = jnp.where(lane == column + 1, mid, base)
    return jnp.where(lane == column + 2, last, base)


def normalize(values):
    center = values - jnp.mean(values, axis=-1, keepdims=True)
    inverse = lax.rsqrt(jnp.mean(center * center, axis=-1, keepdims=True) + 1e-05)
    return center * inverse, inverse


def norm_backward(upstream, scaled, inverse, gain_vec):
    direct = upstream * gain_vec
    return inverse * (
        direct
        - jnp.mean(direct, axis=-1, keepdims=True)
        - scaled * jnp.mean(direct * scaled, axis=-1, keepdims=True)
    )


def cost(micros):
    return pl.CostEstimate(flops=int(micros * 1e7), bytes_accessed=1 << 10, transcendentals=0)


def whole(*shape):
    return pl.BlockSpec(shape, lambda *_: (0,) * len(shape))


def remote(source, target, send, receive, device):
    return pltpu.make_async_remote_copy(
        src_ref=source,
        dst_ref=target,
        send_sem=send,
        recv_sem=receive,
        device_id=device,
        device_id_type=MESH,
    )


def each(count, body):
    def step(i, carry):
        body(i)
        return carry

    lax.fori_loop(0, count, step, 0)


def greet(base, place, planes, groups=None):
    me = lax.axis_index("dp")
    barrier = pltpu.get_barrier_semaphore()

    def signal(dp, z):
        pl.semaphore_signal(barrier, inc=1, device_id=(dp, z), device_id_type=MESH)

    def column(i):
        z = lax.rem(i, planes)

        @pl.when(z != place)
        def _():
            signal(base + i // planes, z)

    def plane(i):
        @pl.when(i != me)
        def _():
            signal(i, place)

    each(2 * planes, column)
    if groups is None:
        signal(2 * base + 1 - me, place)
        pl.semaphore_wait(barrier, 2 * (planes - 1) + 1)
    else:
        each(groups, plane)
        pl.semaphore_wait(barrier, 2 * (planes - 1) + groups - 1)


def front_kernel(
    groups, planes, experts, te, acts, seg, up_in, qkv_in, attn_in, tiny_in, task, win_in, wout_in,
    ids_out, x_out, qa_out, ka_out, va_out, att_out, attf_out, res_out, normed_out, up_out,
    gates_out, own_out, dx_out, near_out, attn_out, small_out, sel_out, ga_out, gb_out, far_got,
    x, segx, up, up_wide, up_low, both, other, near_all, attn_all, tiny_all, small, sel, task_all,
    task_s, qa, ka, va, att, attf, res, normed, gates, slot, send_a, send_b, got_a, got_b, out, dx,
    far, sem_x, sem_seg, sem_on, sem_seg_on, sem_up, sem_up_on, sem_near, sem_attn, sem_tiny,
    sem_task, sem_phase, sem_a, sem_b, sem_att, sem_far, local,
):
    me = lax.axis_index("dp")
    place = lax.axis_index("seq")
    core = lax.rem(me, 2)
    base = me - core
    partner = (base + 1 - core, place)
    band = 2 * (place // 2)
    mine = me * 2 + lax.rem(place, 2)
    piece, width = x.shape[1], x.shape[2]
    tokens = 2 * planes * piece
    half = tokens // 2
    chunks, _, _, rows, _ = send_a.shape
    heads = qa.shape[0]
    near_width = heads * HEAD
    stays = (place // 2) == core
    spot = core + 2 * lax.rem(place, 2)
    used = [0]

    def copy_here(source, target):
        copy = pltpu.make_async_copy(source, target, local.at[used[0]])
        used[0] += 1
        return copy

    load_up = copy_here(up_in, up_wide)
    load_both = [copy_here(win_in, both.at[0]), copy_here(wout_in, both.at[1])]
    load_up.start()
    for copy in load_both:
        copy.start()
    greet_all(groups, planes)

    def goes(d):
        return jnp.logical_not(stays & (d == spot))

    def home_of(d):
        return (base + lax.rem(d, 2), 2 * core + d // 2)

    def token_copies(piece_of, target, sem, sem_on):
        def send(d):
            return remote(piece_of(d), target.at[place], sem.at[0, d], sem.at[1, place], home_of(d))

        at_home = copy_here(piece_of(spot), target.at[place])

        def start():
            def one(d):
                @pl.when(goes(d))
                def _():
                    send(d).start()

            each(planes, one)

            @pl.when(stays)
            def _():
                at_home.start()

        def onward(k):
            return remote(target.at[k], target.at[planes + k], sem_on.at[0, k], sem_on.at[1, k], partner)

        def receive(k):
            home = stays & (k == place)

            @pl.when(home)
            def _():
                at_home.wait()

            @pl.when(jnp.logical_not(home))
            def _():
                remote(piece_of(0), target.at[k], sem.at[0, 0], sem.at[1, k], partner).wait_recv()

            onward(k).start()

        def finish():
            def one(d):
                @pl.when(goes(d))
                def _():
                    send(d).wait_send()

                onward(d).wait_send()

            each(planes, one)

        return start, receive, lambda k: onward(k).wait_recv(), finish

    def seg_piece(d):
        return seg.at[:, pl.ds(pl.multiple_of(lax.rem(d, 2) * piece, piece), piece)]

    x_start, x_receive, x_far, x_finish = token_copies(lambda d: acts.at[d], x, sem_x, sem_on)
    seg_start, seg_receive, seg_far, seg_finish = token_copies(seg_piece, segx, sem_seg, sem_seg_on)
    up_start, up_receive, up_far, up_finish = token_copies(
        lambda d: up_low.at[d], up, sem_up, sem_up_on
    )

    def others(body):
        def run(i):
            @pl.when(i != me)
            def _():
                body(i)

        each(groups, run)

    def give(source, target, sem, i):
        return remote(source, target.at[me], sem.at[0, i], sem.at[1, me], (i, place))

    def taken(source, target, sem, i):
        return remote(source, target.at[i], sem.at[0, i], sem.at[1, i], (i, place))

    def near_part(i, kind):
        at = 2 * kind * near_width + lax.rem(i, 2) * near_width
        return qkv_in.at[:, pl.ds(pl.multiple_of(at, near_width), near_width)]

    def near_copy(i, kind, to, of):
        return remote(
            near_part(to, kind),
            near_all.at[of, :, pl.ds(kind * near_width, near_width)],
            sem_near.at[0, i, kind],
            sem_near.at[1, of, kind],
            (i, place),
        )

    peer = (me, place + 2 - 4 * (place // 2))
    chunk_rows = rows * experts

    def phase_copy(kind, c):
        r = pl.ds(c * chunk_rows, chunk_rows)
        source = (win_in, wout_in)[kind]
        return remote(
            source.at[r], other.at[kind, r], sem_phase.at[0, kind, c], sem_phase.at[1, kind, c], peer
        )

    def band_device(m):
        return (m // 2, band + lax.rem(m, 2))

    def band_copies(source, target, sem):
        def send(m):
            return remote(source(m), target(mine), sem.at[0, m], sem.at[1, mine], band_device(m))

        at_home = copy_here(source(mine), target(mine))

        def run(body, home):
            def one(m):
                @pl.when(m != mine)
                def _():
                    body(m)

                @pl.when(m == mine)
                def _():
                    home()

            each(2 * groups, one)

        def start():
            run(lambda m: send(m).start(), at_home.start)

        def sent():
            run(lambda m: send(m).wait_send(), lambda: None)

        def received():
            run(
                lambda m: remote(
                    source(m), target(m), sem.at[0, m], sem.at[1, m], band_device(m)
                ).wait_recv(),
                at_home.wait,
            )

        return start, sent, received

    a_start, a_sent, a_received = band_copies(
        lambda m: send_a.at[:, m], lambda m: got_a.at[:, m], sem_a
    )
    b_copies = [
        band_copies(
            lambda m, c=c: send_b.at[c, m], lambda m, c=c: got_b.at[c, m], sem_b.at[c]
        )
        for c in range(chunks)
    ]

    x_start()
    seg_start()
    task_part = task.at[:, pl.ds(0, LANES)]
    others(lambda i: give(task_part, task_all, sem_task, i).start())
    others(lambda i: give(tiny_in, tiny_all, sem_tiny, i).start())
    kinds = range(3)

    def start_near(i):
        for kind in kinds:
            near_copy(i, kind, i, me).start()

    others(start_near)
    others(lambda i: give(attn_in, attn_all, sem_attn, i).start())
    own_task = copy_here(task_part, task_all.at[me])
    own_dense = [
        copy_here(tiny_in, tiny_all.at[me]),
        copy_here(attn_in, attn_all.at[me]),
    ] + [
        copy_here(near_part(me, kind), near_all.at[me, :, pl.ds(kind * near_width, near_width)])
        for kind in kinds
    ]
    for copy in [own_task] + own_dense:
        copy.start()
    load_up.wait()
    up_low[...] = up_wide[...].astype(LOW)
    others(lambda i: taken(task_part, task_all, sem_task, i).wait_recv())
    own_task.wait()
    to_scalars = copy_here(task_all, task_s)
    to_scalars.start()
    to_scalars.wait()

    def expert_of(dp, z):
        at = z // 2 + dp - lax.rem(dp, 2)
        return te[lax.rem(dp, 2), task_s[at, lax.rem(z, 2), 0]]

    ids_out[0] = expert_of(me, place)
    ids_out[1] = expert_of(partner[0], place)
    mine_id = ids_out[0]
    other_id = ids_out[1]

    sel_row = lax.broadcasted_iota(jnp.int32, (rows, chunk_rows), 0)
    sel_col = lax.broadcasted_iota(jnp.int32, (rows, chunk_rows), 1)

    def fill_sel(m):
        dp, z = band_device(m)
        hit = sel_col == sel_row * experts + expert_of(dp, z)
        sel[m] = jnp.where(hit, 1.0, 0.0).astype(LOW)

    each(2 * groups, fill_sel)

    def choose(source, target, c):
        choice = sel[...].reshape(2 * groups * rows, chunk_rows)
        for kind in range(2):
            values = dot(choice, source[kind, c * chunk_rows : (c + 1) * chunk_rows])
            target[c, :, kind] = values.astype(LOW).reshape(2 * groups, rows, width)

    for copy in load_both:
        copy.wait()
    for c in range(chunks):
        choose(both, send_a, c)

    def end_near(i):
        for kind in kinds:
            near_copy(i, kind, i, i).wait_recv()

    others(end_near)
    others(lambda i: taken(attn_in, attn_all, sem_attn, i).wait_recv())
    others(lambda i: taken(tiny_in, tiny_all, sem_tiny, i).wait_recv())
    for copy in own_dense:
        copy.wait()
    dense_rows = tiny_all.shape[2]
    eye = lax.broadcasted_iota(jnp.int32, (TINY, LANES), 0) == lanes_of((TINY, LANES))
    eye = jnp.where(eye, 1.0, 0.0).astype(LOW)

    def turn(i):
        r = pl.ds(pl.multiple_of(i * dense_rows, dense_rows), dense_rows)
        small[r, :] = dot_tn(tiny_all[i], eye)

    each(groups, turn)
    keep = []

    def save(source, target):
        copy = copy_here(source, target)
        copy.start()
        keep.append(copy)

    save(near_all, near_out)
    save(attn_all, attn_out)
    save(small, small_out)
    save(sel, sel_out)

    turned = small[...].T
    first_gain = turned[experts : experts + 1]
    second_gain = turned[experts + 1 : experts + 2]
    lane = lanes_of((piece, LANES))

    def project(slot_at):
        scaled, _ = normalize(x[slot_at].astype(F32))
        low = (scaled * first_gain).astype(LOW)
        weight = near_all[...].reshape(width, near_all.shape[2])
        values = dot(low, weight)
        segment = jnp.broadcast_to(
            segx[slot_at, pl.ds(lax.rem(place, 2), 1)].astype(F32), (LANES, piece)
        ).T
        same = (lane - SEG_COL).astype(F32) == segment
        in_seg = (lane >= SEG_COL) & (lane < SEG_COL + SEGMENTS)
        q_more = jnp.where(same, 1.0, 0.0)
        k_more = jnp.where(in_seg & jnp.logical_not(same), -FAR, 0.0)
        k_more = jnp.where((lane >= LSE_COL) & (lane < LSE_COL + 3), 1.0, k_more)
        v_more = jnp.where((lane >= HEAD) & (lane < HEAD + 3), 1.0, 0.0)
        r = pl.ds(pl.multiple_of(slot_at * piece, piece), piece)

        def head(kind, h, more):
            at = kind * heads * HEAD + h // 2 * LANES
            part = values[:, at : at + LANES]
            if h % 2:
                part = pltpu.roll(part, HEAD, 1)
            return jnp.where(lane < HEAD, part, more)

        for h in range(heads):
            query = head(0, h, 0.0).astype(LOW).astype(F32) * HEAD**-0.5
            qa[h, r, :] = (query + q_more).astype(LOW)
            ka[h, r, :] = head(1, h, k_more).astype(LOW)
            va[h, r, :] = head(2, h, v_more).astype(LOW)

    def arrive(k):
        k = lax.rem(place + k, planes)
        x_receive(k)
        seg_receive(k)

    each(planes, arrive)
    up_start()
    a_start()
    for c in range(chunks):
        for kind in range(2):
            phase_copy(kind, c).start()

    def near_piece(k):
        project(lax.rem(place + k, planes))

    each(planes, near_piece)

    def far_piece(k):
        x_far(k)
        seg_far(k)
        project(planes + k)

    each(planes, far_piece)
    save(x, x_out)
    save(ka, ka_out)
    save(va, va_out)

    block = min(512, half)

    def att_copy(p):
        return remote(att.at[p], attf.at[p], sem_att.at[0, p], sem_att.at[1, p], partner)

    for p in range(heads // 2):

        def attend(i):
            r = pl.ds(pl.multiple_of(i * block, block), block)
            parts = []
            for h in (2 * p, 2 * p + 1):
                query = qa[h, r, :]
                scores = dot_nt(query, ka[h])
                top = jnp.max(scores, axis=1, keepdims=True)
                probs = jnp.exp(scores - top).astype(LOW)
                mixed = dot(probs, va[h])
                total = mixed[:, HEAD : HEAD + 1]
                parts.append(mixed[:, :HEAD] / total)
                lse = top + jnp.log(total)
                qa[h, r, :] = put_thirds(query.astype(F32), -lse, LSE_COL).astype(LOW)
            att[p, r, :] = jnp.concatenate(parts, axis=1).astype(LOW)

        each(tokens // block, attend)
        att_copy(p).start()
    save(qa, qa_out)
    save(att, att_out)

    def other_weights(c):
        for kind in range(2):
            phase_copy(kind, c).wait_recv()
        choose(other, send_b, c)
        b_copies[c][0]()

    for c in range(chunks - 1):
        other_weights(c)
    each(planes, lambda k: up_receive(lax.rem(place + k, planes)))
    for p in range(heads // 2):
        att_copy(p).wait_recv()
    save(attf, attf_out)
    save(up.at[pl.ds(0, planes)], up_out)

    def weight_rows(which):
        part = attn_all[pl.ds(which * (groups // 2), groups // 2)]
        return part.reshape(width // 2, width)

    def middle(b):
        @pl.when(b >= planes)
        def _():
            up_far(b - planes)

        r = pl.ds(pl.multiple_of(b * piece, piece), piece)
        f = pl.ds(pl.multiple_of(lax.rem(b + planes, 2 * planes) * piece, piece), piece)
        residual = x[b].astype(F32)
        pairs = range(heads // 2)
        residual += dot(jnp.concatenate([att[p, r, :] for p in pairs], axis=1), weight_rows(core))
        residual += dot(
            jnp.concatenate([attf[p, f, :] for p in pairs], axis=1), weight_rows(1 - core)
        )

        @pl.when(b < planes)
        def _():
            res[r, :] = residual

        scaled, _ = normalize(residual)
        low = (scaled * second_gain).astype(LOW)
        normed[r, :] = low
        logits = dot(low, small[...].astype(LOW))
        of_mine = jnp.sum(jnp.where(lane == mine_id, logits, 0.0), axis=1, keepdims=True)
        of_other = jnp.sum(jnp.where(lane == other_id, logits, 0.0), axis=1, keepdims=True)
        top = jnp.maximum(of_mine, of_other)
        of_mine = jnp.exp(of_mine - top)
        of_other = jnp.exp(of_other - top)
        total = of_mine + of_other
        gate = of_mine / total
        gates[r, :] = jnp.where(lane == 0, gate, jnp.where(lane == 1, of_other / total, 0.0))
        slot[r, :] = (gate * up[b].astype(F32)).astype(LOW)

    each(2 * planes, middle)
    save(res, res_out)
    save(normed.at[pl.ds(0, half)], normed_out)

    out[...] = jnp.zeros_like(out)
    dx[...] = jnp.zeros_like(dx)
    per = max(1, 256 // rows)

    def expert(source, target, c):
        def tile(t):
            at = pl.ds(t * per, per)
            win = source[c, at, 0].reshape(per * rows, width)
            wout = source[c, at, 1].reshape(per * rows, width)
            pre = dot_nt(normed[...], win)
            hidden_grad = dot_nt(slot[...], wout)
            cdf = 0.5 * (1.0 + lax.erf(pre * 0.7071067811865476))
            slope = cdf + pre * jnp.exp(-0.5 * pre * pre) * 0.3989422804014327
            hidden = (pre * cdf).astype(LOW)
            pre_grad = (hidden_grad * slope).astype(LOW)
            out[...] += dot(hidden, wout)
            dx[...] += dot(pre_grad, win)
            target[c, at, 0] = dot_tn(pre_grad, normed[...]).astype(LOW).reshape(per, rows, width)
            target[c, at, 1] = dot_tn(hidden, slot[...]).astype(LOW).reshape(per, rows, width)

        each(2 * groups // per, tile)

    a_received()
    a_sent()
    each(chunks, lambda c: expert(got_a, send_a, c))
    save(send_a, ga_out)
    other_weights(chunks - 1)

    def second(c):
        start, sent, received = b_copies[c]
        received()
        sent()
        expert(got_b, send_b, c)

    for c in range(chunks):
        second(c)
    save(send_b, gb_out)

    step = half // 2
    for at in range(0, tokens, step):
        r = pl.ds(at, step)
        value = out[r, :]
        grads = up[pl.ds(at // piece, step // piece)].reshape(step, width).astype(F32)
        gate_grad = jnp.sum(value * grads, axis=1, keepdims=True)
        value = value * gates[r, 0:1]
        tail = put_thirds(jnp.zeros((step, LANES), F32), gate_grad, 0)
        if at < half:
            out[r, :] = value
            gates[r, :] = gates[r, :] + pltpu.roll(tail, 2, 1)
        else:
            t = pl.ds(at - half, step)
            far[t, :width] = value.astype(LOW)
            far[t, width : 2 * width] = dx[r, :].astype(LOW)
            far[t, 2 * width :] = tail.astype(LOW)
    far_copy = remote(far, far_got, sem_far.at[0], sem_far.at[1], partner)
    far_copy.start()
    save(out.at[pl.ds(0, half)], own_out)
    save(dx.at[pl.ds(0, half)], dx_out)
    save(gates.at[pl.ds(0, half)], gates_out)

    for c in range(chunks):
        for kind in range(2):
            phase_copy(kind, c).wait_send()
    x_finish()
    seg_finish()
    up_finish()
    for p in range(heads // 2):
        att_copy(p).wait_send()

    def end_dense(i):
        give(task_part, task_all, sem_task, i).wait_send()
        give(tiny_in, tiny_all, sem_tiny, i).wait_send()
        give(attn_in, attn_all, sem_attn, i).wait_send()
        for kind in kinds:
            near_copy(i, kind, i, me).wait_send()

    others(end_dense)
    for copy in keep:
        copy.wait()
    far_copy.wait()


def greet_all(groups, planes):
    me = lax.axis_index("dp")
    place = lax.axis_index("seq")
    base = me - lax.rem(me, 2)
    band = 2 * (place // 2)
    barrier = pltpu.get_barrier_semaphore()

    def signal(dp, z):
        pl.semaphore_signal(barrier, inc=1, device_id=(dp, z), device_id_type=MESH)

    def near_planes(m):
        dp, z = m // 2, band + lax.rem(m, 2)

        @pl.when(jnp.logical_not((dp == me) & (z == place)))
        def _():
            signal(dp, z)

    def far_planes(i):
        signal(base + i // 2, 2 - band + lax.rem(i, 2))

    each(2 * groups, near_planes)
    each(4, far_planes)
    pl.semaphore_wait(barrier, 2 * groups + 3)


def front(te, acts, seg, up_in, qkv, attn, tiny, task, win, wout, groups, planes, experts):
    _, piece, width = acts.shape
    half = planes * piece
    tokens = 2 * half
    heads = width // HEAD // 2
    hidden = win.shape[0] // experts
    chunks = 2 if hidden % 32 == 0 else 1
    rows = hidden // chunks
    count = 2 * groups
    dense_rows = qkv.shape[0]
    near_cols = 3 * heads * HEAD
    anywhere = pl.BlockSpec(memory_space=pl.ANY)
    scalars = pl.BlockSpec(memory_space=pltpu.SMEM)
    dma = pltpu.SemaphoreType.DMA
    S = lambda shape, t=LOW: jax.ShapeDtypeStruct(shape, t)
    V = lambda shape, t=LOW: pltpu.VMEM(shape, t)
    head_shape = (heads, tokens, LANES)
    pair_shape = (heads // 2, tokens, LANES)
    band_shape = (chunks, count, 2, rows, width)
    far_shape = (half, 2 * width + LANES)
    near_shape = (groups, dense_rows, near_cols)
    attn_shape = (groups, dense_rows, width)
    sel_shape = (count, rows, rows * experts)
    both_shape = (2,) + win.shape
    pieces = (planes, piece, width)
    return pl.pallas_call(
        functools.partial(front_kernel, groups, planes, experts),
        in_specs=[scalars] + [anywhere] * 9,
        out_specs=[scalars] + [anywhere] * 19,
        out_shape=[
            S((2,), jnp.int32),
            S((2 * planes, piece, width)),
            S(head_shape),
            S(head_shape),
            S(head_shape),
            S(pair_shape),
            S(pair_shape),
            S((half, width), F32),
            S((half, width)),
            S(pieces),
            S((half, LANES), F32),
            S((half, width), F32),
            S((half, width), F32),
            S(near_shape),
            S(attn_shape),
            S((width, LANES), F32),
            S(sel_shape),
            S(band_shape),
            S(band_shape),
            S(far_shape),
        ],
        scratch_shapes=[
            V((2 * planes, piece, width)),
            V((2 * planes, 2, piece), jnp.int32),
            V((2 * planes, piece, width)),
            V(pieces, F32),
            V(pieces),
            V(both_shape),
            V(both_shape),
            V(near_shape),
            V(attn_shape),
            V((groups,) + tiny.shape),
            V((width, LANES), F32),
            V(sel_shape),
            V((groups, 2, LANES), jnp.int32),
            pltpu.SMEM((groups, 2, LANES), jnp.int32),
            V(head_shape),
            V(head_shape),
            V(head_shape),
            V(pair_shape),
            V(pair_shape),
            V((half, width), F32),
            V((tokens, width)),
            V((tokens, LANES), F32),
            V((tokens, width)),
            V(band_shape),
            V(band_shape),
            V(band_shape),
            V(band_shape),
            V((tokens, width), F32),
            V((tokens, width), F32),
            V(far_shape),
        ]
        + [dma((2, planes))] * 6
        + [dma((2, groups, 3))]
        + [dma((2, groups))] * 3
        + [dma((2, 2, chunks))]
        + [dma((2, count)), dma((chunks, 2, count))]
        + [dma((2, heads // 2)), dma((2,)), dma((48,))],
        compiler_params=pltpu.CompilerParams(
            collective_id=0, has_side_effects=True, vmem_limit_bytes=LARGE
        ),
        cost_estimate=cost(130),
        name="front",
    )(te, acts, seg, up_in, qkv, attn, tiny, task, win, wout)


def back_kernel(
    groups, planes, ids, x_in, qa_in, ka_in, va_in, att_in, attf_in, res_in, normed_in, up_in,
    gates_in, own_in, dx_in, near_in, attn_in, small_in, sel_in, ga_in, gb_in, far_in,
    tokens_out, grads_out, total_out, ga_got, other_got,
    x, qa, ka, va, att, attf, res, normed, up, gates, own, dx, near_w, attn_w, small, sel, far,
    gb_got, sums,
    outputs, res_grad, att_grad, att_send, attn_acc, router_acc, gain_acc, rest_part, rest_got,
    dqkv, gb, key_t, dq_acc, qkv_acc, first_acc, back_near, back_send, back_got, qkv_part, qkv_got,
    out_grads, part, heard, summed,
    sem_phase, sem_a, sem_b, sem_out, sem_att, sem_rest, sem_back, sem_qkv, sem_in, sem_part, sem_sum, local,
):
    me = lax.axis_index("dp")
    place = lax.axis_index("seq")
    core = lax.rem(me, 2)
    base = me - core
    partner = (base + 1 - core, place)
    piece, width = x.shape[1], x.shape[2]
    half = planes * piece
    tokens = 2 * half
    heads = qa.shape[0]
    pairs = heads // 2
    stays = (place // 2) == core
    spot = core + 2 * lax.rem(place, 2)
    near_width = heads * HEAD
    experts = sel.shape[2] // sel.shape[1]
    chunks, count, _, rows, _ = gb_got.shape
    band = 2 * (place // 2)
    mine = me * 2 + lax.rem(place, 2)
    used = [0]

    def load(source, target):
        copy = pltpu.make_async_copy(source, target, local.at[used[0]])
        used[0] += 1
        copy.start()
        return copy

    early = [
        load(res_in, res),
        load(own_in, own),
        load(dx_in, dx),
        load(far_in, far),
        load(gates_in, gates),
        load(up_in, up),
        load(normed_in, normed),
        load(attn_in, attn_w),
        load(small_in, small),
        load(att_in, att),
        load(attf_in.at[:, pl.ds(half, half)], attf),
    ]
    late = [load(qa_in, qa), load(ka_in, ka), load(va_in, va)]
    last = [load(x_in, x), load(near_in, near_w)]
    load_sel = load(sel_in, sel)
    greet_all(groups, planes)

    peer = (me, place + 2 - 4 * (place // 2))
    phase = remote(sums, other_got, sem_phase.at[0], sem_phase.at[1], peer)

    def band_device(m):
        return (m // 2, band + lax.rem(m, 2))

    def band_copies(source, target, sem, local_at):
        def send(m):
            return remote(
                source.at[:, m], target.at[:, mine], sem.at[0, m], sem.at[1, mine], band_device(m)
            )

        at_home = pltpu.make_async_copy(source.at[:, mine], target.at[:, mine], local.at[local_at])

        def run(body, home):
            def one(m):
                @pl.when(m != mine)
                def _():
                    body(m)

                @pl.when(m == mine)
                def _():
                    home()

            each(count, one)

        def start():
            run(lambda m: send(m).start(), at_home.start)

        def sent():
            run(lambda m: send(m).wait_send(), lambda: None)

        def received():
            run(
                lambda m: remote(
                    source.at[:, m], target.at[:, m], sem.at[0, m], sem.at[1, m], band_device(m)
                ).wait_recv(),
                at_home.wait,
            )

        return start, sent, received

    a_start, a_sent, a_received = band_copies(ga_in, ga_got, sem_a, 26)
    b_start, b_sent, b_received = band_copies(gb_in, gb_got, sem_b, 27)
    b_start()

    def others(body):
        def run(i):
            @pl.when(i != me)
            def _():
                body(i)

        each(groups, run)

    def give(source, target, sem, i):
        return remote(source.at[i], target.at[me], sem.at[0, i], sem.at[1, me], (i, place))

    def taken(source, target, sem, i):
        return remote(source.at[i], target.at[i], sem.at[0, i], sem.at[1, i], (i, place))

    def way_back(source, target, sem, local_at):
        def send(slot):
            return remote(
                source.at[slot],
                target.at[spot],
                sem.at[0, slot],
                sem.at[1, spot],
                (base + place // 2, slot),
            )

        at_home = pltpu.make_async_copy(source.at[place], target.at[spot], local.at[local_at])

        def start(slot):
            home = stays & (slot == place)

            @pl.when(jnp.logical_not(home))
            def _():
                send(slot).start()

            @pl.when(home)
            def _():
                at_home.start()

        def end(d):
            @pl.when(jnp.logical_not(stays & (d == place)))
            def _():
                send(d).wait_send()

            @pl.when(jnp.logical_not(stays & (d == spot)))
            def _():
                remote(source.at[0], target.at[d], sem.at[0, 0], sem.at[1, d], partner).wait_recv()

            @pl.when(stays & (d == place))
            def _():
                at_home.wait()

        return start, lambda: each(planes, end)

    out_start, out_end = way_back(outputs, tokens_out, sem_out, 24)
    in_start, in_end = way_back(out_grads, grads_out, sem_in, 25)

    for copy in early:
        copy.wait()
    attn_acc[...] = jnp.zeros_like(attn_acc)
    router_acc[...] = jnp.zeros_like(router_acc)
    gain_acc[...] = jnp.zeros_like(gain_acc)
    lane = lanes_of((piece, LANES))
    turned = small[...].T
    first_gain = turned[experts : experts + 1]
    second_gain = turned[experts + 1 : experts + 2]
    mine_id = ids[0]
    other_id = ids[1]

    def weight_rows(which):
        values = attn_w[pl.ds(which * (groups // 2), groups // 2)]
        return values.reshape(width // 2, width)

    def post(b):
        r = pl.ds(pl.multiple_of(b * piece, piece), piece)
        residual = res[r, :]
        upstream = up[b].astype(F32)
        outputs[b] = (residual + own[r, :] + far[r, :width].astype(F32)).astype(LOW)
        out_start(b)
        gate = gates[r, :]
        gate_mine, gate_other = gate[:, 0:1], gate[:, 1:2]
        grad_mine = jnp.sum(jnp.where((lane >= 2) & (lane < 5), gate, 0.0), axis=1, keepdims=True)
        grad_other = jnp.sum(far[r, 2 * width :].astype(F32), axis=1, keepdims=True)
        mean = gate_mine * grad_mine + gate_other * grad_other
        logit_grad = jnp.where(lane == mine_id, gate_mine * (grad_mine - mean), 0.0)
        logit_grad += jnp.where(lane == other_id, gate_other * (grad_other - mean), 0.0)
        normed_grad = dx[r, :] + far[r, width : 2 * width].astype(F32)
        router = small[...].astype(LOW)
        for third in thirds(logit_grad):
            third = third.astype(LOW)
            router_acc[...] += dot_tn(normed[r, :], third)
            normed_grad += dot_nt(third, router)
        scaled, inverse = normalize(residual)
        gain_acc[...] += jnp.sum(normed_grad * scaled, axis=0, keepdims=True)
        residual_grad = upstream + norm_backward(normed_grad, scaled, inverse, second_gain)
        res_grad[r, :] = residual_grad
        low = residual_grad.astype(LOW)
        both_att = [att[p, r, :] for p in range(pairs)] + [attf[p, r, :] for p in range(pairs)]
        for i, part_att in enumerate(both_att):
            attn_acc[i * LANES : (i + 1) * LANES] += dot_tn(part_att, low)
        near_back = dot_nt(low, weight_rows(core)).astype(LOW)
        far_back = dot_nt(low, weight_rows(1 - core)).astype(LOW)
        for p in range(pairs):
            att_grad[p, r, :] = near_back[:, p * LANES : (p + 1) * LANES]
            att_send[p, r, :] = far_back[:, p * LANES : (p + 1) * LANES]

    each(planes, post)

    def att_copy(p):
        return remote(
            att_send.at[p],
            att_grad.at[p, pl.ds(half, half)],
            sem_att.at[0, p],
            sem_att.at[1, p],
            partner,
        )

    for p in range(pairs):
        att_copy(p).start()
    dense_rows = rest_part.shape[1]
    own_rows = near_width // dense_rows
    turned = jnp.broadcast_to(gain_acc[...], (LANES, width)).T
    wide_lane = lanes_of(turned.shape)
    tail = jnp.where(wide_lane == EXPERTS_AT, turned, router_acc[...]).astype(LOW)
    rest_part[:, :, width:] = tail.reshape(groups, dense_rows, LANES)
    for side in range(2):
        values = attn_acc[side * near_width : (side + 1) * near_width].astype(LOW)
        at = core if side == 0 else 1 - core
        rest_part[pl.ds(at * own_rows, own_rows), :, :width] = values.reshape(
            own_rows, dense_rows, width
        )
    others(lambda i: give(rest_part, rest_got, sem_rest, i).start())

    def add_up_others():
        b_received()
        load_sel.wait()
        choice = sel[...].reshape(count * rows, rows * experts)
        for c in range(chunks):
            for kind in range(2):
                r = pl.ds(c * rows * experts, rows * experts)
                values = gb_got[c, :, kind].reshape(count * rows, width)
                sums[kind, r] = dot_tn(choice, values).astype(LOW)
        phase.start()
        a_start()

    for copy in late:
        copy.wait()
    block = min(512, half)
    all_lane = lanes_of((tokens, LANES))
    for p in range(pairs):
        att_copy(p).wait_recv()
        halves = []
        for side in range(2):
            h = 2 * p + side
            pair_grad = att_grad[p].astype(F32)
            inner = pair_grad * att[p].astype(F32)
            if side == 1:
                pair_grad = pltpu.roll(pair_grad, HEAD, 1)
                inner = pltpu.roll(inner, HEAD, 1)
            delta = jnp.sum(jnp.where(all_lane < HEAD, inner, 0.0), axis=1, keepdims=True)
            pair_grad = jnp.where(all_lane < HEAD, pair_grad, 0.0)
            gb[...] = put_thirds(pair_grad, -delta, HEAD).astype(LOW)
            key_t[...] = ka[h].T[:HEAD]
            dq_acc[...] = jnp.zeros_like(dq_acc)
            cols = pl.ds(side * HEAD, HEAD)

            def keys(i):
                r = pl.ds(pl.multiple_of(i * block, block), block)
                weights = jnp.exp(dot_nt(ka[h, r, :], qa[h]))
                centered = dot_nt(va[h, r, :], gb[...])
                score_grad = (weights * centered).astype(LOW)
                dqkv[2 * pairs + p, r, cols] = dot(weights.astype(LOW), gb[...])[:, :HEAD].astype(LOW)
                dqkv[pairs + p, r, cols] = dot(score_grad, qa[h])[:, :HEAD].astype(LOW)
                dq_acc[...] += dot(key_t[:, r], score_grad)

            each(tokens // block, keys)
            halves.append(dq_acc[...].T * HEAD**-0.5)
            if h == 0:
                add_up_others()
        dqkv[p] = jnp.concatenate(halves, axis=1).astype(LOW)

    for copy in last:
        copy.wait()
    qkv_acc[...] = jnp.zeros_like(qkv_acc)
    first_acc[...] = jnp.zeros_like(first_acc)

    def project_back(b):
        r = pl.ds(pl.multiple_of(b * piece, piece), piece)
        values = jnp.concatenate([dqkv[i, r, :] for i in range(3 * pairs)], axis=1)
        scaled, _ = normalize(x[b].astype(F32))
        back = dot_nt(values, near_w[...].reshape(width, near_w.shape[2]))
        qkv_acc[...] += dot_tn((scaled * first_gain).astype(LOW), values)
        first_acc[...] += jnp.sum(back * scaled, axis=0, keepdims=True)
        return back

    def far_block(i):
        back = project_back(planes + i)
        back_send[pl.ds(pl.multiple_of(i * piece, piece), piece), :] = back.astype(LOW)

    def near_block(i):
        back_near[pl.ds(pl.multiple_of(i * piece, piece), piece), :] = project_back(i)

    each(planes, far_block)
    back_copy = remote(back_send, back_got, sem_back.at[0], sem_back.at[1], partner)
    back_copy.start()
    each(planes, near_block)
    near_cols = near_w.shape[2]
    qkv_part[:, :, :near_cols] = qkv_acc[...].astype(LOW).reshape(groups, dense_rows, near_cols)
    turned = jnp.broadcast_to(first_acc[...], (LANES, width)).T.astype(LOW)
    qkv_part[:, :, near_cols:] = turned.reshape(groups, dense_rows, LANES)
    others(lambda i: give(qkv_part, qkv_got, sem_qkv, i).start())

    back_copy.wait_recv()

    def finish(b):
        r = pl.ds(pl.multiple_of(b * piece, piece), piece)
        scaled, inverse = normalize(x[b].astype(F32))
        grad = back_near[r, :] + back_got[r, :].astype(F32)
        first = norm_backward(grad, scaled, inverse, first_gain)
        out_grads[b] = (res_grad[r, :] + first).astype(LOW)
        in_start(b)

    each(planes, finish)

    others(lambda i: taken(qkv_part, qkv_got, sem_qkv, i).wait_recv())
    others(lambda i: taken(rest_part, rest_got, sem_rest, i).wait_recv())

    def from_group(mine_part, got, i):
        return jnp.where(i == me, mine_part[i], got[i]).astype(F32)

    def add(j, sums_of):
        first, second, rest = sums_of
        first += from_group(qkv_part, qkv_got, 2 * j)
        second += from_group(qkv_part, qkv_got, 2 * j + 1)
        rest += from_group(rest_part, rest_got, 2 * j)
        rest += from_group(rest_part, rest_got, 2 * j + 1)
        return first, second, rest

    zero = jnp.zeros(qkv_part.shape[1:], F32)
    first, second, rest = lax.fori_loop(
        0, groups // 2, add, (zero, zero, jnp.zeros(rest_part.shape[1:], F32))
    )
    columns = []
    for kind in range(3):
        for side in (first, second):
            columns.append(side[:, kind * near_width : (kind + 1) * near_width])
    columns += [rest, first[:, near_cols:] + second[:, near_cols:]]
    share = jnp.concatenate(columns, axis=1).astype(LOW)
    cut = dense_rows // planes
    for z in range(planes):
        part[z] = share[z * cut : (z + 1) * cut]

    def over_planes(body):
        def run(z):
            @pl.when(z != place)
            def _():
                body(z)

        each(planes, run)

    def tell_part(z):
        return remote(part.at[z], heard.at[place], sem_part.at[0, z], sem_part.at[1, place], (me, z))

    def hear_part(z):
        return remote(part.at[z], heard.at[z], sem_part.at[0, z], sem_part.at[1, z], (me, z))

    def tell_sum(z):
        return remote(summed, total_out.at[place], sem_sum.at[0, z], sem_sum.at[1, place], (me, z))

    def hear_sum(z):
        return remote(summed, total_out.at[z], sem_sum.at[0, z], sem_sum.at[1, z], (me, z))

    over_planes(lambda z: tell_part(z).start())

    over_planes(lambda z: hear_part(z).wait_recv())
    sum_of = part[place].astype(F32)
    for k in range(1, planes):
        sum_of += heard[lax.rem(place + k, planes)].astype(F32)
    summed[...] = sum_of.astype(LOW)
    over_planes(lambda z: tell_sum(z).start())
    put = pltpu.make_async_copy(summed, total_out.at[place], local.at[28])
    put.start()

    phase.wait()
    a_received()
    a_sent()
    b_sent()
    back_copy.wait_send()
    for p in range(pairs):
        att_copy(p).wait_send()
    others(lambda i: give(rest_part, rest_got, sem_rest, i).wait_send())
    others(lambda i: give(qkv_part, qkv_got, sem_qkv, i).wait_send())
    over_planes(lambda z: tell_part(z).wait_send())
    over_planes(lambda z: tell_sum(z).wait_send())
    over_planes(lambda z: hear_sum(z).wait_recv())
    put.wait()
    out_end()
    in_end()


def back(ids, saved, groups, planes):
    x, qa, ka, va, att, attf, res, normed, up, gates, own, dx, near, attn, small, sel, ga, gb, far = (
        saved
    )
    _, piece, width = x.shape
    half = planes * piece
    tokens = 2 * half
    heads = qa.shape[0]
    dense_rows = near.shape[1]
    near_cols = near.shape[2]
    count = ga.shape[1]
    sums = (2, ga.shape[0] * sel.shape[2], width)
    total = (planes, dense_rows // planes, 4 * width + 2 * LANES)
    rest = (groups, dense_rows, width + LANES)
    anywhere = pl.BlockSpec(memory_space=pl.ANY)
    dma = pltpu.SemaphoreType.DMA
    S = lambda shape, t: jax.ShapeDtypeStruct(shape, t)
    V = lambda shape, t=LOW: pltpu.VMEM(shape, t)
    pair_half = (heads // 2, half, LANES)
    return pl.pallas_call(
        functools.partial(back_kernel, groups, planes),
        in_specs=[pl.BlockSpec(memory_space=pltpu.SMEM)] + [anywhere] * 19,
        out_specs=[anywhere] * 5,
        out_shape=[
            S((planes, piece, width), LOW),
            S((planes, piece, width), LOW),
            S(total, LOW),
            S(ga.shape, LOW),
            S(sums, LOW),
        ],
        scratch_shapes=[
            V(x.shape),
            V(qa.shape),
            V(ka.shape),
            V(va.shape),
            V(att.shape),
            V(pair_half),
            V(res.shape, F32),
            V(normed.shape),
            V(up.shape),
            V(gates.shape, F32),
            V(own.shape, F32),
            V(dx.shape, F32),
            V(near.shape),
            V(attn.shape),
            V(small.shape, F32),
            V(sel.shape),
            V(far.shape),
            V(gb.shape),
            V(sums),
            V(up.shape),
            V(res.shape, F32),
            V(att.shape),
            V(pair_half),
            V((width, width), F32),
            V((width, LANES), F32),
            V((1, width), F32),
            V(rest),
            V(rest),
            V((3 * heads // 2, tokens, LANES)),
            V((tokens, LANES)),
            V((HEAD, tokens)),
            V((HEAD, tokens), F32),
            V((width, near_cols), F32),
            V((1, width), F32),
            V((half, width), F32),
            V((half, width)),
            V((half, width)),
            V((groups, dense_rows, near_cols + LANES)),
            V((groups, dense_rows, near_cols + LANES)),
            V(up.shape),
            V(total),
            V(total),
            V(total[1:]),
            dma((2,)),
            dma((2, count)),
            dma((2, count)),
            dma((2, planes)),
            dma((2, heads // 2)),
            dma((2, groups)),
            dma((2,)),
            dma((2, groups)),
            dma((2, planes)),
            dma((2, planes)),
            dma((2, planes)),
            dma((32,)),
        ],
        compiler_params=pltpu.CompilerParams(
            collective_id=1, has_side_effects=True, vmem_limit_bytes=LARGE
        ),
        cost_estimate=cost(110),
        name="back",
    )(ids, *saved)


def deliver_kernel(
    sel, ga, other, tokens, grads, total,
    outputs, input_grad, qkv_grad, attn_grad, router_grad, first, second, win_grad, wout_grad,
):
    outputs[...] = tokens[...]
    input_grad[...] = grads[...].astype(F32)
    count, rows, columns = sel.shape
    width = ga.shape[4]
    choice = sel[...].reshape(count * rows, columns)
    for kind, grad in ((0, win_grad), (1, wout_grad)):
        values = dot_tn(choice, ga[0, :, kind].reshape(count * rows, width))
        grad[...] = values + other[kind].astype(F32)

    @pl.when(pl.program_id(0) == 0)
    def _():
        planes, cut, _ = total.shape
        for z in range(planes):
            r = slice(z * cut, (z + 1) * cut)
            values = total[z].astype(F32)
            qkv_grad[r] = values[:, : 3 * width]
            attn_grad[r] = values[:, 3 * width : 4 * width]
            router_grad[r] = values[:, 4 * width : 4 * width + router_grad.shape[1]]
            first[r] = values[:, 4 * width + LANES : 4 * width + LANES + 1]
            second[r] = values[:, 4 * width + EXPERTS_AT : 4 * width + EXPERTS_AT + 1]


def deliver(sel, ga, other, tokens, grads, total, experts):
    chunks = ga.shape[0]
    planes, piece, width = tokens.shape
    dense_rows = total.shape[0] * total.shape[1]
    part = pl.BlockSpec((planes // chunks, piece, width), lambda i: (i, 0, 0))
    rows = other.shape[1] // chunks
    grad = pl.BlockSpec((rows, width), lambda i: (i, 0))
    S = lambda shape, t=F32: jax.ShapeDtypeStruct(shape, t)
    return pl.pallas_call(
        deliver_kernel,
        grid=(chunks,),
        in_specs=[
            whole(*sel.shape),
            pl.BlockSpec((1,) + ga.shape[1:], lambda i: (i, 0, 0, 0, 0)),
            pl.BlockSpec((2, rows, width), lambda i: (0, i, 0)),
            part,
            part,
            whole(*total.shape),
        ],
        out_specs=[
            part,
            part,
            whole(dense_rows, 3 * width),
            whole(dense_rows, width),
            whole(dense_rows, experts),
            whole(dense_rows, 1),
            whole(dense_rows, 1),
            grad,
            grad,
        ],
        out_shape=[
            S(tokens.shape, LOW),
            S(tokens.shape),
            S((dense_rows, 3 * width)),
            S((dense_rows, width)),
            S((dense_rows, experts)),
            S((dense_rows, 1)),
            S((dense_rows, 1)),
            S(other.shape[1:]),
            S(other.shape[1:]),
        ],
        compiler_params=pltpu.CompilerParams(vmem_limit_bytes=LARGE),
        cost_estimate=cost(5),
        name="deliver",
    )(sel, ga, other, tokens, grads, total)


def local(
    activations, qkv_weight, attn_weight, router_weight, gain_one, gain_two,
    expert_in, expert_out, segments, task_ids, task_experts, out_grad,
):
    packs, length, width = activations.shape
    planes = lax.axis_size("seq")
    groups = lax.axis_size("dp")
    cuts = 2 * packs
    assert cuts == planes == 4 and groups % 2 == 0
    piece = length // 2
    experts = router_weight.shape[1]
    hidden = expert_in.shape[0]
    assert experts + 2 <= TINY
    zeros = jnp.zeros((TINY - experts - 2, qkv_weight.shape[0]), LOW)
    tiny = jnp.concatenate([router_weight.T, gain_one[None], gain_two[None], zeros])
    ids, *saved = front(
        task_experts.T,
        activations.reshape(cuts, piece, width),
        segments,
        out_grad.reshape(cuts, piece, width),
        qkv_weight,
        attn_weight,
        tiny,
        task_ids,
        expert_in.reshape(hidden * experts, width),
        expert_out.reshape(hidden * experts, width),
        groups,
        planes,
        experts,
    )
    outputs, input_grad, total, grads, other = back(ids, saved, groups, planes)
    sel = saved[15]
    outputs, input_grad, qkv_grad, attn_grad, router_grad, first, second, win_grad, wout_grad = (
        deliver(sel, grads, other, outputs, input_grad, total, experts)
    )
    return (
        outputs.reshape(packs, length, width),
        input_grad.reshape(packs, length, width),
        qkv_grad,
        attn_grad,
        router_grad,
        first.reshape(-1),
        second.reshape(-1),
        win_grad.reshape(expert_in.shape),
        wout_grad.reshape(expert_in.shape),
    )


def solution(mesh):
    placed = (
        P("dp", "seq", None),
        P("dp", None),
        P("dp", None),
        P("dp", None),
        P("dp"),
        P("dp"),
        P(("dp", "seq"), None, None),
        P(("dp", "seq"), None, None),
        P("dp", "seq"),
        P("dp", "seq"),
        P(),
        P("dp", "seq", None),
    )
    return jax.shard_map(
        local,
        mesh=mesh,
        in_specs=placed,
        out_specs=(
            P("dp", "seq", None),
            P("dp", "seq", None),
            P("dp", None),
            P("dp", None),
            P("dp", None),
            P("dp"),
            P("dp"),
            P(("dp", "seq"), None, None),
            P(("dp", "seq"), None, None),
        ),
        check_vma=False,
    )
```

```python
import functools

import jax
import jax.numpy as jnp
from jax import lax
from jax.experimental import pallas as pl
from jax.experimental.pallas import tpu as pltpu
from jax.sharding import PartitionSpec as P

HEAD = 64
LANES = 128
SEG_COL = HEAD
LSE_COL = HEAD + 16
SEGMENTS = 16
FAR = 1e9
LARGE = 62 << 20
NT = (((1,), (1,)), ((), ()))
TN = (((0,), (0,)), ((), ()))
MESH = pl.DeviceIdType.MESH
EXPERTS_AT = LANES - 1
TINY = 16
F32 = jnp.float32
LOW = jnp.bfloat16


def dot(a, b):
    return jnp.dot(a, b, preferred_element_type=F32)


def dot_nt(a, b):
    return lax.dot_general(a, b, NT, preferred_element_type=F32)


def dot_tn(a, b):
    return lax.dot_general(a, b, TN, preferred_element_type=F32)


def thirds(values):
    high = values.astype(LOW).astype(F32)
    rest = values - high
    mid = rest.astype(LOW).astype(F32)
    return high, mid, rest - mid


def lanes_of(shape):
    return lax.broadcasted_iota(jnp.int32, shape, len(shape) - 1)


def put_thirds(base, values, column):
    lane = lanes_of(base.shape)
    high, mid, last = thirds(values)
    base = jnp.where(lane == column, high, base)
    base = jnp.where(lane == column + 1, mid, base)
    return jnp.where(lane == column + 2, last, base)


def normalize(values):
    center = values - jnp.mean(values, axis=-1, keepdims=True)
    inverse = lax.rsqrt(jnp.mean(center * center, axis=-1, keepdims=True) + 1e-05)
    return center * inverse, inverse


def norm_backward(upstream, scaled, inverse, gain_vec):
    direct = upstream * gain_vec
    return inverse * (
        direct
        - jnp.mean(direct, axis=-1, keepdims=True)
        - scaled * jnp.mean(direct * scaled, axis=-1, keepdims=True)
    )


def cost(micros):
    return pl.CostEstimate(flops=int(micros * 1e7), bytes_accessed=1 << 10, transcendentals=0)


def whole(*shape):
    return pl.BlockSpec(shape, lambda *_: (0,) * len(shape))


def remote(source, target, send, receive, device):
    return pltpu.make_async_remote_copy(
        src_ref=source,
        dst_ref=target,
        send_sem=send,
        recv_sem=receive,
        device_id=device,
        device_id_type=MESH,
    )


def each(count, body):
    def step(i, carry):
        body(i)
        return carry

    lax.fori_loop(0, count, step, 0)


def layer_kernel(
    groups, planes, experts, te, acts, seg, up_in, qkv_in, attn_in, tiny_in, task, win_in, wout_in,
    tokens_out, grads_out, total_out, other_got, ga_got, gb_got, sel_out,
    x, segx, up, res, stage, both, other, near_all, attn_all, tiny_all, small, sel, task_all, task_s,
    qa, ka, va, att, attf, normed, gates, slot, dv, send, got_a, got_b, out, dx, far_value, far_dx,
    far_gate, att_grad, att_send, attn_acc, router_acc, gain_acc, rest_part, rest_got, gb, key_t,
    dq_acc, qkv_acc, first_acc, qkv_part, qkv_got, part, heard, summed, sums,
    sem_x, sem_seg, sem_on, sem_seg_on, sem_up, sem_up_on, sem_near, sem_attn, sem_tiny, sem_task,
    sem_phase, sem_a, sem_b, sem_ga, sem_gb, sem_att, sem_far, sem_sums, sem_out, sem_att_back,
    sem_rest, sem_back, sem_qkv, sem_in, sem_part, sem_total, home, local,
):
    me = lax.axis_index("dp")
    place = lax.axis_index("seq")
    core = lax.rem(me, 2)
    base = me - core
    partner = (base + 1 - core, place)
    peer = (me, place + 2 - 4 * (place // 2))
    band = 2 * (place // 2)
    mine = me * 2 + lax.rem(place, 2)
    count = 2 * groups
    piece, width = x.shape[1], x.shape[2]
    tokens = 2 * planes * piece
    half = tokens // 2
    chunks, _, _, rows, _ = send.shape
    chunk_rows = rows * experts
    heads = qa.shape[0]
    pairs = heads // 2
    near_width = heads * HEAD
    near_cols = near_all.shape[2]
    dense_rows = tiny_all.shape[2]
    stays = (place // 2) == core
    spot = core + 2 * lax.rem(place, 2)
    kinds = range(3)
    used = [0]

    def copy_here(source, target):
        copy = pltpu.make_async_copy(source, target, local.at[used[0]])
        used[0] += 1
        return copy

    def rows_of(b, size):
        return pl.ds(pl.multiple_of(b * size, size), size)

    kind_rows = both.shape[0] // 2
    load_up = copy_here(up_in, res)
    load_both = [
        copy_here(source, both.at[pl.ds(kind * kind_rows, source.shape[0])])
        for kind, source in enumerate((win_in, wout_in))
    ]
    load_up.start()
    for copy in load_both:
        copy.start()
    greet_all(groups, planes)

    def goes(d):
        return jnp.logical_not(stays & (d == spot))

    def token_copies(piece_of, target, sem, sem_on):
        def give_piece(d):
            to = (base + lax.rem(d, 2), 2 * core + d // 2)
            return remote(piece_of(d), target.at[place], sem.at[0, d], sem.at[1, place], to)

        at_home = copy_here(piece_of(spot), target.at[place])

        def start():
            def one(d):
                @pl.when(goes(d))
                def _():
                    give_piece(d).start()

            each(planes, one)

            @pl.when(stays)
            def _():
                at_home.start()

        def onward(k):
            return remote(target.at[k], target.at[planes + k], sem_on.at[0, k], sem_on.at[1, k], partner)

        def receive(k):
            home = stays & (k == place)

            @pl.when(home)
            def _():
                at_home.wait()

            @pl.when(jnp.logical_not(home))
            def _():
                remote(piece_of(0), target.at[k], sem.at[0, 0], sem.at[1, k], partner).wait_recv()

            onward(k).start()

        def finish():
            def one(d):
                @pl.when(goes(d))
                def _():
                    give_piece(d).wait_send()

                onward(d).wait_send()

            each(planes, one)

        return start, receive, lambda k: onward(k).wait_recv(), finish

    def seg_piece(d):
        return seg.at[:, rows_of(lax.rem(d, 2), piece)]

    x_start, x_receive, x_far, x_finish = token_copies(lambda d: acts.at[d], x, sem_x, sem_on)
    seg_start, seg_receive, seg_far, seg_finish = token_copies(seg_piece, segx, sem_seg, sem_seg_on)
    up_start, up_receive, up_far, up_finish = token_copies(
        lambda d: stage.at[d], up, sem_up, sem_up_on
    )

    def way_back(source, target, sem):
        def give_piece(k):
            to = (base + place // 2, k)
            return remote(source.at[k], target.at[spot], sem.at[0, k], sem.at[1, spot], to)

        at_home = copy_here(source.at[place], target.at[spot])

        def start(k):
            home = stays & (k == place)

            @pl.when(jnp.logical_not(home))
            def _():
                give_piece(k).start()

            @pl.when(home)
            def _():
                at_home.start()

        def end(d):
            @pl.when(jnp.logical_not(stays & (d == place)))
            def _():
                give_piece(d).wait_send()

            @pl.when(goes(d))
            def _():
                remote(source.at[0], target.at[d], sem.at[0, 0], sem.at[1, d], partner).wait_recv()

            @pl.when(stays & (d == place))
            def _():
                at_home.wait()

        return start, lambda: each(planes, end)

    out_start, out_end = way_back(stage, tokens_out, sem_out)
    in_start, in_end = way_back(up, grads_out, sem_in)

    def others(body):
        each(groups - 1, lambda i: body(lax.rem(me + 1 + i, groups)))

    def give(source, target, sem, i):
        return remote(source, target.at[me], sem.at[0, i], sem.at[1, me], (i, place))

    def taken(source, target, sem, i):
        return remote(source, target.at[i], sem.at[0, i], sem.at[1, i], (i, place))

    def near_part(i, kind):
        at = 2 * kind * near_width + lax.rem(i, 2) * near_width
        return qkv_in.at[:, pl.ds(pl.multiple_of(at, near_width), near_width)]

    def near_copy(i, kind, to, of):
        return remote(
            near_part(to, kind),
            near_all.at[of, :, pl.ds(kind * near_width, near_width)],
            sem_near.at[0, i, kind],
            sem_near.at[1, of, kind],
            (i, place),
        )

    def part_of(kind, c):
        at = kind * kind_rows + c * chunk_rows
        return pl.ds(at if isinstance(c, int) else pl.multiple_of(at, chunk_rows), chunk_rows)

    def phase_copy(kind, c):
        source = (win_in, wout_in)[kind].at[rows_of(c, chunk_rows)]
        target = other.at[part_of(kind, c)]
        return remote(source, target, sem_phase.at[0, kind, c], sem_phase.at[1, kind, c], peer)

    def sums_copy(kind, c):
        r = part_of(kind, c)
        return remote(
            sums.at[r], other_got.at[r], sem_sums.at[0, kind, c], sem_sums.at[1, kind, c], peer
        )

    def band_device(m):
        return (m // 2, band + lax.rem(m, 2))

    def band_copies(source, target, sem, home_sem):
        def give_part(c, m):
            to = band_device(m)
            return remote(source(c, m), target(c, mine), sem.at[c, 0, m], sem.at[c, 1, mine], to)

        def at_home(c):
            return pltpu.make_async_copy(source(c, mine), target(c, mine), home_sem.at[c])

        def run(body):
            each(count - 1, lambda i: body(lax.rem(mine + 1 + i, count)))

        def start(c):
            run(lambda m: give_part(c, m).start())
            at_home(c).start()

        def sent(c):
            run(lambda m: give_part(c, m).wait_send())

        def received(c):
            run(
                lambda m: remote(
                    source(c, m), target(c, m), sem.at[c, 0, m], sem.at[c, 1, m], band_device(m)
                ).wait_recv()
            )
            at_home(c).wait()

        return start, sent, received

    def by_chunk(source, target, sem, home_sem):
        return band_copies(
            lambda c, m: source.at[c, m], lambda c, m: target.at[c, m], sem, home_sem
        )

    a_start, a_sent, a_received = band_copies(
        lambda c, m: send.at[:, m], lambda c, m: got_a.at[:, m], sem_a, home.at[0]
    )
    b_start, b_sent, b_received = by_chunk(send, got_b, sem_b, home.at[1])
    ga_start, ga_sent, ga_received = by_chunk(got_a, ga_got, sem_ga, home.at[2])
    gb_start, gb_sent, gb_received = by_chunk(got_b, gb_got, sem_gb, home.at[3])

    def load_gb(c):
        return pltpu.make_async_copy(gb_got.at[c], send.at[c], home.at[4, c])

    x_start()
    seg_start()
    task_part = task.at[:, pl.ds(0, LANES)]
    others(lambda i: give(task_part, task_all, sem_task, i).start())
    others(lambda i: give(tiny_in, tiny_all, sem_tiny, i).start())

    def start_near(i):
        for kind in kinds:
            near_copy(i, kind, i, me).start()

    others(start_near)
    own_task = copy_here(task_part, task_all.at[me])
    own_dense = [
        copy_here(tiny_in, tiny_all.at[me]),
        copy_here(attn_in, attn_all.at[me]),
    ] + [
        copy_here(near_part(me, kind), near_all.at[me, :, pl.ds(kind * near_width, near_width)])
        for kind in kinds
    ]
    for copy in [own_task] + own_dense:
        copy.start()
    load_up.wait()
    stage[...] = res[...].astype(LOW)
    others(lambda i: taken(task_part, task_all, sem_task, i).wait_recv())
    own_task.wait()
    to_scalars = copy_here(task_all, task_s)
    to_scalars.start()
    to_scalars.wait()

    def expert_of(dp, z):
        at = z // 2 + dp - lax.rem(dp, 2)
        return te[lax.rem(dp, 2), task_s[at, lax.rem(z, 2), 0]]

    mine_id = expert_of(me, place)
    other_id = expert_of(partner[0], place)

    sel_row = lax.broadcasted_iota(jnp.int32, (rows, chunk_rows), 0)
    sel_col = lax.broadcasted_iota(jnp.int32, (rows, chunk_rows), 1)

    def fill_sel(m):
        dp, z = band_device(m)
        hit = sel_col == sel_row * experts + expert_of(dp, z)
        sel[m] = jnp.where(hit, 1.0, 0.0).astype(LOW)

    each(count, fill_sel)
    save_sel = copy_here(sel, sel_out)
    save_sel.start()

    def choose(source, c):
        choice = sel[...].reshape(count * rows, chunk_rows)
        for kind in range(2):
            values = dot(choice, source[part_of(kind, c), :])
            send[c, :, kind] = values.astype(LOW).reshape(count, rows, width)

    for copy in load_both:
        copy.wait()
    for c in range(chunks):
        choose(both, c)

    def end_near(i):
        for kind in kinds:
            near_copy(i, kind, i, i).wait_recv()

    others(end_near)
    others(lambda i: taken(tiny_in, tiny_all, sem_tiny, i).wait_recv())
    for copy in own_dense:
        copy.wait()
    eye = lax.broadcasted_iota(jnp.int32, (TINY, LANES), 0) == lanes_of((TINY, LANES))
    eye = jnp.where(eye, 1.0, 0.0).astype(LOW)

    def turn(i):
        small[rows_of(i, dense_rows), :] = dot_tn(tiny_all[i], eye)

    each(groups, turn)

    turned = small[...].T
    first_gain = turned[experts : experts + 1]
    second_gain = turned[experts + 1 : experts + 2]
    lane = lanes_of((piece, LANES))

    def project(k):
        scaled, _ = normalize(x[k].astype(F32))
        low = (scaled * first_gain).astype(LOW)
        values = dot(low, near_all[...].reshape(width, near_cols))
        segment = segx[k, pl.ds(lax.rem(place, 2), 1)].astype(F32)
        segment = jnp.broadcast_to(segment, (LANES, piece)).T
        same = (lane - SEG_COL).astype(F32) == segment
        in_seg = (lane >= SEG_COL) & (lane < SEG_COL + SEGMENTS)
        q_more = jnp.where(same, 1.0, 0.0)
        k_more = jnp.where(in_seg & jnp.logical_not(same), -FAR, 0.0)
        k_more = jnp.where((lane >= LSE_COL) & (lane < LSE_COL + 3), 1.0, k_more)
        v_more = jnp.where((lane >= HEAD) & (lane < HEAD + 3), 1.0, 0.0)
        r = rows_of(k, piece)

        def head(kind, h, more):
            at = kind * near_width + h // 2 * LANES
            values_of = values[:, at : at + LANES]
            if h % 2:
                values_of = pltpu.roll(values_of, HEAD, 1)
            return jnp.where(lane < HEAD, values_of, more)

        for h in range(heads):
            query = head(0, h, 0.0).astype(LOW).astype(F32) * HEAD**-0.5
            qa[h, r, :] = (query + q_more).astype(LOW)
            ka[h, r, :] = head(1, h, k_more).astype(LOW)
            va[h, r, :] = head(2, h, v_more).astype(LOW)

    def by_distance(k):
        return lax.bitwise_xor(place, jnp.int32(k))

    def arrive(k):
        x_receive(k)
        seg_receive(k)

    def start_phase(c):
        for kind in range(2):
            phase_copy(kind, c).start()

    for k in range(planes):
        arrive(by_distance(k))
        if k < planes // 2:
            project(by_distance(k))
    up_start()
    a_start(0)
    start_phase(0)
    others(lambda i: give(attn_in, attn_all, sem_attn, i).start())
    for k in range(planes // 2, planes):
        project(by_distance(k))

    def far_piece(k):
        x_far(k)
        seg_far(k)
        project(planes + k)

    each(planes, far_piece)

    block = min(512, half)

    def att_copy(p):
        return remote(att.at[p], attf.at[p], sem_att.at[0, p], sem_att.at[1, p], partner)

    for p in range(pairs):

        def attend(i):
            r = rows_of(i, block)
            parts = []
            for h in (2 * p, 2 * p + 1):
                query = qa[h, r, :]
                scores = dot_nt(query, ka[h])
                top = jnp.max(scores, axis=1, keepdims=True)
                probs = jnp.exp(scores - top).astype(LOW)
                mixed = dot(probs, va[h])
                total = mixed[:, HEAD : HEAD + 1]
                parts.append(mixed[:, :HEAD] / total)
                lse = top + jnp.log(total)
                qa[h, r, :] = put_thirds(query.astype(F32), -lse, LSE_COL).astype(LOW)
            att[p, r, :] = jnp.concatenate(parts, axis=1).astype(LOW)

        each(tokens // block, attend)
        att_copy(p).start()
        if p == 0 and chunks > 1:
            start_phase(1)

    def other_weights(c):
        for kind in range(2):
            phase_copy(kind, c).wait_recv()
        choose(other, c)
        b_start(c)

    for c in range(2, chunks):
        start_phase(c)
    for k in range(planes):
        up_receive(by_distance(k))
    for p in range(pairs):
        att_copy(p).wait_recv()
    others(lambda i: taken(attn_in, attn_all, sem_attn, i).wait_recv())

    def weight_rows(which):
        values = attn_all[pl.ds(which * (groups // 2), groups // 2)]
        return values.reshape(width // 2, width)

    def middle(b):
        @pl.when(b >= planes)
        def _():
            up_far(b - planes)

        r = rows_of(b, piece)
        f = rows_of(lax.rem(b + planes, 2 * planes), piece)
        residual = x[b].astype(F32)
        near_att = jnp.concatenate([att[p, r, :] for p in range(pairs)], axis=1)
        far_att = jnp.concatenate([attf[p, f, :] for p in range(pairs)], axis=1)
        residual += dot(near_att, weight_rows(core)) + dot(far_att, weight_rows(1 - core))

        @pl.when(b < planes)
        def _():
            res[b] = residual

        scaled, _ = normalize(residual)
        low = (scaled * second_gain).astype(LOW)
        normed[r, :] = low
        logits = dot(low, small[...].astype(LOW))
        of_mine = jnp.sum(jnp.where(lane == mine_id, logits, 0.0), axis=1, keepdims=True)
        of_other = jnp.sum(jnp.where(lane == other_id, logits, 0.0), axis=1, keepdims=True)
        top = jnp.maximum(of_mine, of_other)
        of_mine = jnp.exp(of_mine - top)
        of_other = jnp.exp(of_other - top)
        total = of_mine + of_other
        gate = of_mine / total
        gates[r, :] = jnp.where(lane == 0, gate, jnp.where(lane == 1, of_other / total, 0.0))
        slot[r, :] = (gate * up[b].astype(F32)).astype(LOW)

    each(2 * planes, middle)

    def add_up_others(c):
        b_sent(c)
        gb_received(c)
        load_gb(c).start()
        load_gb(c).wait()
        choice = sel[...].reshape(count * rows, chunk_rows)
        for kind in range(2):
            values = send[c, :, kind].reshape(count * rows, width)
            sums[part_of(kind, c), :] = dot_tn(choice, values).astype(LOW)
            sums_copy(kind, c).start()

    out[...] = jnp.zeros_like(out)
    dx[...] = jnp.zeros_like(dx)
    per = max(1, 256 // rows)

    def expert(weights, c):
        def tile(t):
            at = pl.ds(t * per, per)
            win = weights[c, at, 0].reshape(per * rows, width)
            wout = weights[c, at, 1].reshape(per * rows, width)
            pre = dot_nt(normed[...], win)
            hidden_grad = dot_nt(slot[...], wout)
            cdf = 0.5 * (1.0 + lax.erf(pre * 0.7071067811865476))
            slope = cdf + pre * jnp.exp(-0.5 * pre * pre) * 0.3989422804014327
            hidden = (pre * cdf).astype(LOW)
            pre_grad = (hidden_grad * slope).astype(LOW)
            out[...] += dot(hidden, wout)
            dx[...] += dot(pre_grad, win)
            weights[c, at, 0] = dot_tn(pre_grad, normed[...]).astype(LOW).reshape(per, rows, width)
            weights[c, at, 1] = dot_tn(hidden, slot[...]).astype(LOW).reshape(per, rows, width)

        each(count // per, tile)

    def second(c):
        b_received(c)
        expert(got_b, c)
        gb_start(c)

    a_sent(0)
    a_received(0)
    if chunks > 1:
        other_weights(0)
        expert(got_a, 0)
        other_weights(1)
        expert(got_a, 1)
        second(0)
        other_weights(2)
        expert(got_a, 2)
        second(1)
        other_weights(3)
        expert(got_a, 3)
        add_up_others(0)
        second(2)
        add_up_others(1)
        second(3)
    else:
        expert(got_a, 0)
        other_weights(0)
        second(0)

    step = half // 2
    step_lane = lanes_of((step, LANES))
    for at in range(0, tokens, step):
        r = pl.ds(at, step)
        value = out[r, :]
        upstream = up[pl.ds(at // piece, step // piece)].reshape(step, width).astype(F32)
        gate_grad = jnp.sum(value * upstream, axis=1, keepdims=True)
        value = value * gates[r, 0:1]
        if at < half:
            out[r, :] = value
            gates[r, :] = jnp.where(step_lane == 2, gate_grad, gates[r, :])
        else:
            t = pl.ds(at - half, step)
            other[t, :] = value.astype(LOW)
            both[t, :] = dx[r, :].astype(LOW)
            gates[r, :] = jnp.broadcast_to(gate_grad, (step, LANES))
    far_copies = [
        remote(other.at[pl.ds(0, half)], far_value, sem_far.at[0, 0], sem_far.at[1, 0], partner),
        remote(both.at[pl.ds(0, half)], far_dx, sem_far.at[0, 1], sem_far.at[1, 1], partner),
        remote(gates.at[pl.ds(half, half)], far_gate, sem_far.at[0, 2], sem_far.at[1, 2], partner),
    ]
    for copy in far_copies:
        copy.start()
    up_finish()

    res_grad = out.at[pl.ds(half, half)]
    attn_acc[...] = jnp.zeros_like(attn_acc)
    router_acc[...] = jnp.zeros_like(router_acc)
    gain_acc[...] = jnp.zeros_like(gain_acc)
    for copy in far_copies:
        copy.wait()


    def post(b):
        r = rows_of(b, piece)
        residual = res[b]
        upstream = up[b].astype(F32)
        stage[b] = (residual + out[r, :] + far_value[r, :].astype(F32)).astype(LOW)
        out_start(b)
        gate = gates[r, :]
        gate_mine, gate_other, grad_mine = gate[:, 0:1], gate[:, 1:2], gate[:, 2:3]
        grad_other = far_gate[r, 0:1]
        mean = gate_mine * grad_mine + gate_other * grad_other
        logit_grad = jnp.where(lane == mine_id, gate_mine * (grad_mine - mean), 0.0)
        logit_grad += jnp.where(lane == other_id, gate_other * (grad_other - mean), 0.0)
        normed_grad = dx[r, :] + far_dx[r, :].astype(F32)
        router = small[...].astype(LOW)
        for third in thirds(logit_grad):
            third = third.astype(LOW)
            router_acc[...] += dot_tn(normed[r, :], third)
            normed_grad += dot_nt(third, router)
        scaled, inverse = normalize(residual)
        gain_acc[...] += jnp.sum(normed_grad * scaled, axis=0, keepdims=True)
        residual_grad = upstream + norm_backward(normed_grad, scaled, inverse, second_gain)
        res_grad[r, :] = residual_grad
        low = residual_grad.astype(LOW)
        f = pl.ds(pl.multiple_of(half + b * piece, piece), piece)
        both_att = [att[p, r, :] for p in range(pairs)] + [attf[p, f, :] for p in range(pairs)]
        for i, values in enumerate(both_att):
            attn_acc[i * LANES : (i + 1) * LANES] += dot_tn(values, low)
        near_back = dot_nt(low, weight_rows(core)).astype(LOW)
        far_back = dot_nt(low, weight_rows(1 - core)).astype(LOW)
        for p in range(pairs):
            att_grad[p, r, :] = near_back[:, p * LANES : (p + 1) * LANES]
            att_send[p, r, :] = far_back[:, p * LANES : (p + 1) * LANES]

    each(planes, post)

    def att_back_copy(p):
        target = att_grad.at[p, pl.ds(half, half)]
        return remote(att_send.at[p], target, sem_att_back.at[0, p], sem_att_back.at[1, p], partner)

    for p in range(pairs):
        att_back_copy(p).start()
    own_rows = near_width // dense_rows
    turned = jnp.broadcast_to(gain_acc[...], (LANES, width)).T
    tail = jnp.where(lanes_of(turned.shape) == EXPERTS_AT, turned, router_acc[...]).astype(LOW)
    rest_part[:, :, width:] = tail.reshape(groups, dense_rows, LANES)
    for side in range(2):
        values = attn_acc[side * near_width : (side + 1) * near_width].astype(LOW)
        at = core if side == 0 else 1 - core
        rest_part[pl.ds(at * own_rows, own_rows), :, :width] = values.reshape(
            own_rows, dense_rows, width
        )

    def rest_copy(i):
        return give(rest_part.at[i], rest_got, sem_rest, i)

    others(lambda i: rest_copy(i).start())

    if chunks > 1:
        add_up_others(2)

    all_lane = lanes_of((tokens, LANES))
    for p in range(pairs):
        att_back_copy(p).wait_recv()
        halves = []
        for side in range(2):
            h = 2 * p + side
            pair_grad = att_grad[p].astype(F32)
            inner = pair_grad * att[p].astype(F32)
            if side == 1:
                pair_grad = pltpu.roll(pair_grad, HEAD, 1)
                inner = pltpu.roll(inner, HEAD, 1)
            delta = jnp.sum(jnp.where(all_lane < HEAD, inner, 0.0), axis=1, keepdims=True)
            pair_grad = jnp.where(all_lane < HEAD, pair_grad, 0.0)
            gb[...] = put_thirds(pair_grad, -delta, HEAD).astype(LOW)
            key_t[...] = ka[h].T[:HEAD]
            dq_acc[...] = jnp.zeros_like(dq_acc)
            dk_cols = pl.ds((pairs + p) * LANES + side * HEAD, HEAD)
            dv_cols = pl.ds(p * LANES + side * HEAD, HEAD)

            def keys(i):
                r = rows_of(i, block)
                weights = jnp.exp(dot_nt(ka[h, r, :], qa[h]))
                centered = dot_nt(va[h, r, :], gb[...])
                score_grad = (weights * centered).astype(LOW)
                dv[r, dv_cols] = dot(weights.astype(LOW), gb[...])[:, :HEAD].astype(LOW)
                slot[r, dk_cols] = dot(score_grad, qa[h])[:, :HEAD].astype(LOW)
                dq_acc[...] += dot(key_t[:, r], score_grad)

            each(tokens // block, keys)
            halves.append(dq_acc[...].T * HEAD**-0.5)
            if h == 0:
                add_up_others(chunks - 1)
                each(chunks, ga_start)
        slot[:, p * LANES : (p + 1) * LANES] = jnp.concatenate(halves, axis=1).astype(LOW)

    qkv_acc[...] = jnp.zeros_like(qkv_acc)
    first_acc[...] = jnp.zeros_like(first_acc)
    back_near = dx.at[pl.ds(half, half)]
    back_send = normed.at[pl.ds(0, half)]
    back_got = normed.at[pl.ds(half, half)]

    def project_back(b):
        r = rows_of(b, piece)
        values = jnp.concatenate([slot[r, :], dv[r, :]], axis=1)
        scaled, _ = normalize(x[b].astype(F32))
        back = dot_nt(values, near_all[...].reshape(width, near_cols))
        qkv_acc[...] += dot_tn((scaled * first_gain).astype(LOW), values)
        first_acc[...] += jnp.sum(back * scaled, axis=0, keepdims=True)
        return back

    def far_block(i):
        back_send[rows_of(i, piece), :] = project_back(planes + i).astype(LOW)

    def near_block(i):
        back_near[rows_of(i, piece), :] = project_back(i)

    each(planes, far_block)
    back_copy = remote(back_send, back_got, sem_back.at[0], sem_back.at[1], partner)
    back_copy.start()
    each(planes, near_block)
    qkv_part[:, :, :near_cols] = qkv_acc[...].astype(LOW).reshape(groups, dense_rows, near_cols)
    turned = jnp.broadcast_to(first_acc[...], (LANES, width)).T.astype(LOW)
    qkv_part[:, :, near_cols:] = turned.reshape(groups, dense_rows, LANES)

    def qkv_copy(i):
        return give(qkv_part.at[i], qkv_got, sem_qkv, i)

    others(lambda i: qkv_copy(i).start())

    back_copy.wait_recv()

    def finish(b):
        r = rows_of(b, piece)
        scaled, inverse = normalize(x[b].astype(F32))
        grad = back_near[r, :] + back_got[r, :].astype(F32)
        first = norm_backward(grad, scaled, inverse, first_gain)
        up[b] = (res_grad[r, :] + first).astype(LOW)
        in_start(b)

    each(planes, finish)

    others(lambda i: taken(rest_part.at[i], rest_got, sem_rest, i).wait_recv())
    others(lambda i: taken(qkv_part.at[i], qkv_got, sem_qkv, i).wait_recv())

    def from_group(mine_part, got, i):
        return jnp.where(i == me, mine_part[i], got[i]).astype(F32)

    def add(j, sums_of):
        first, second, rest = sums_of
        first += from_group(qkv_part, qkv_got, 2 * j)
        second += from_group(qkv_part, qkv_got, 2 * j + 1)
        rest += from_group(rest_part, rest_got, 2 * j)
        rest += from_group(rest_part, rest_got, 2 * j + 1)
        return first, second, rest

    zero = jnp.zeros(qkv_part.shape[1:], F32)
    first, second, rest = lax.fori_loop(
        0, groups // 2, add, (zero, zero, jnp.zeros(rest_part.shape[1:], F32))
    )
    columns = []
    for kind in kinds:
        for side in (first, second):
            columns.append(side[:, kind * near_width : (kind + 1) * near_width])
    columns += [rest, first[:, near_cols:] + second[:, near_cols:]]
    share = jnp.concatenate(columns, axis=1).astype(LOW)
    cut = dense_rows // planes
    for z in range(planes):
        part[z] = share[z * cut : (z + 1) * cut]

    def over_planes(body):
        each(planes - 1, lambda i: body(lax.rem(place + 1 + i, planes)))

    def tell_part(z):
        return remote(part.at[z], heard.at[place], sem_part.at[0, z], sem_part.at[1, place], (me, z))

    def hear_part(z):
        return remote(part.at[z], heard.at[z], sem_part.at[0, z], sem_part.at[1, z], (me, z))

    def tell_sum(z):
        target = total_out.at[place]
        return remote(summed, target, sem_total.at[0, z], sem_total.at[1, place], (me, z))

    def hear_sum(z):
        return remote(summed, total_out.at[z], sem_total.at[0, z], sem_total.at[1, z], (me, z))

    over_planes(lambda z: tell_part(z).start())
    over_planes(lambda z: hear_part(z).wait_recv())
    sum_of = part[place].astype(F32)
    for k in range(1, planes):
        sum_of += heard[lax.rem(place + k, planes)].astype(F32)
    summed[...] = sum_of.astype(LOW)
    over_planes(lambda z: tell_sum(z).start())
    put = copy_here(summed, total_out.at[place])
    put.start()

    x_finish()
    seg_finish()

    def end_dense(i):
        give(task_part, task_all, sem_task, i).wait_send()
        give(tiny_in, tiny_all, sem_tiny, i).wait_send()
        give(attn_in, attn_all, sem_attn, i).wait_send()
        for kind in kinds:
            near_copy(i, kind, i, me).wait_send()
        rest_copy(i).wait_send()
        qkv_copy(i).wait_send()

    others(end_dense)
    save_sel.wait()
    for p in range(pairs):
        att_copy(p).wait_send()
        att_back_copy(p).wait_send()
    back_copy.wait_send()
    for c in range(chunks):
        ga_sent(c)
        ga_received(c)
        gb_sent(c)
        for kind in range(2):
            phase_copy(kind, c).wait_send()
            sums_copy(kind, c).wait()
    over_planes(lambda z: tell_part(z).wait_send())
    over_planes(lambda z: tell_sum(z).wait_send())
    over_planes(lambda z: hear_sum(z).wait_recv())
    put.wait()
    out_end()
    in_end()


def greet_all(groups, planes):
    me = lax.axis_index("dp")
    place = lax.axis_index("seq")
    base = me - lax.rem(me, 2)
    band = 2 * (place // 2)
    mine = me * 2 + lax.rem(place, 2)
    barrier = pltpu.get_barrier_semaphore()

    def signal(dp, z):
        pl.semaphore_signal(barrier, inc=1, device_id=(dp, z), device_id_type=MESH)

    def near_planes(i):
        m = lax.rem(mine + 1 + i, 2 * groups)
        signal(m // 2, band + lax.rem(m, 2))

    each(2 * groups - 1, near_planes)
    each(4, lambda i: signal(base + i // 2, 2 - band + lax.rem(i, 2)))
    pl.semaphore_wait(barrier, 2 * groups + 3)


def layer(te, acts, seg, up_in, qkv, attn, tiny, task, win, wout, groups, planes, experts):
    _, piece, width = acts.shape
    half = planes * piece
    tokens = 2 * half
    heads = width // HEAD // 2
    pairs = heads // 2
    hidden = win.shape[0] // experts
    chunks = 4 if hidden % 64 == 0 else 1
    rows = hidden // chunks
    count = 2 * groups
    dense_rows = qkv.shape[0]
    near_cols = 3 * heads * HEAD
    anywhere = pl.BlockSpec(memory_space=pl.ANY)
    dma = pltpu.SemaphoreType.DMA
    S = lambda shape, t=LOW: jax.ShapeDtypeStruct(shape, t)
    V = lambda shape, t=LOW: pltpu.VMEM(shape, t)
    pieces = (planes, piece, width)
    head_shape = (heads, tokens, LANES)
    pair_shape = (pairs, tokens, LANES)
    band_shape = (chunks, count, 2, rows, width)
    both_shape = (max(half, 2 * win.shape[0]), width)
    sel_shape = (count, rows, rows * experts)
    rest_shape = (groups, dense_rows, width + LANES)
    qkv_shape = (groups, dense_rows, near_cols + LANES)
    total = (planes, dense_rows // planes, 4 * width + 2 * LANES)
    return pl.pallas_call(
        functools.partial(layer_kernel, groups, planes, experts),
        in_specs=[pl.BlockSpec(memory_space=pltpu.SMEM)] + [anywhere] * 9,
        out_specs=[anywhere] * 7,
        out_shape=[
            S(pieces),
            S(pieces),
            S(total),
            S(both_shape),
            S(band_shape),
            S(band_shape),
            S(sel_shape),
        ],
        scratch_shapes=[
            V((2 * planes, piece, width)),
            V((2 * planes, 2, piece), jnp.int32),
            V((2 * planes, piece, width)),
            V(pieces, F32),
            V(pieces),
            V(both_shape),
            V(both_shape),
            V((groups, dense_rows, near_cols)),
            V((groups, dense_rows, width)),
            V((groups,) + tiny.shape),
            V((width, LANES), F32),
            V(sel_shape),
            V((groups, 2, LANES), jnp.int32),
            pltpu.SMEM((groups, 2, LANES), jnp.int32),
            V(head_shape),
            V(head_shape),
            V(head_shape),
            V(pair_shape),
            V(pair_shape),
            V((tokens, width)),
            V((tokens, LANES), F32),
            V((tokens, width)),
            V((tokens, heads * HEAD)),
            V(band_shape),
            V(band_shape),
            V(band_shape),
            V((tokens, width), F32),
            V((tokens, width), F32),
            V((half, width)),
            V((half, width)),
            V((half, LANES), F32),
            V(pair_shape),
            V((pairs, half, LANES)),
            V((width, width), F32),
            V((width, LANES), F32),
            V((1, width), F32),
            V(rest_shape),
            V(rest_shape),
            V((tokens, LANES)),
            V((HEAD, tokens)),
            V((HEAD, tokens), F32),
            V((width, near_cols), F32),
            V((1, width), F32),
            V(qkv_shape),
            V(qkv_shape),
            V(total),
            V(total),
            V(total[1:]),
            V(both_shape),
        ]
        + [dma((2, planes))] * 6
        + [dma((2, groups, 3))]
        + [dma((2, groups))] * 3
        + [dma((2, 2, chunks)), dma((1, 2, count))]
        + [dma((chunks, 2, count))] * 3
        + [dma((2, pairs)), dma((2, 3)), dma((2, 2, chunks)), dma((2, planes)), dma((2, pairs))]
        + [dma((2, groups)), dma((2,)), dma((2, groups))]
        + [dma((2, planes))] * 3
        + [dma((5, chunks)), dma((32,))],
        compiler_params=pltpu.CompilerParams(
            collective_id=0, has_side_effects=True, vmem_limit_bytes=LARGE
        ),
        cost_estimate=cost(250),
        name="layer",
    )(te, acts, seg, up_in, qkv, attn, tiny, task, win, wout)


def deliver_kernel(
    sel, ga, other, tokens, grads, total,
    outputs, input_grad, qkv_grad, attn_grad, router_grad, first, second, win_grad, wout_grad,
):
    outputs[...] = tokens[...]
    input_grad[...] = grads[...].astype(F32)
    count, rows, columns = sel.shape
    width = ga.shape[4]
    choice = sel[...].reshape(count * rows, columns)
    for kind, grad in ((0, win_grad), (1, wout_grad)):
        values = dot_tn(choice, ga[0, :, kind].reshape(count * rows, width))
        grad[...] = values + other[kind].astype(F32)

    @pl.when(pl.program_id(0) == 0)
    def _():
        planes, cut, _ = total.shape
        for z in range(planes):
            r = slice(z * cut, (z + 1) * cut)
            values = total[z].astype(F32)
            qkv_grad[r] = values[:, : 3 * width]
            attn_grad[r] = values[:, 3 * width : 4 * width]
        small = jnp.concatenate([total[z, :, 4 * width :].astype(F32) for z in range(planes)])
        turned = small[:, :LANES].T
        router_grad[...] = turned[: router_grad.shape[0]]
        second[...] = turned[EXPERTS_AT : EXPERTS_AT + 1]
        first[...] = small[:, LANES:].T[0:1]


def deliver(sel, ga, other, tokens, grads, total, experts):
    chunks = ga.shape[0]
    planes, piece, width = tokens.shape
    dense_rows = total.shape[0] * total.shape[1]
    part = pl.BlockSpec((planes // chunks, piece, width), lambda i: (i, 0, 0))
    rows = other.shape[1] // chunks
    grad = pl.BlockSpec((rows, width), lambda i: (i, 0))
    S = lambda shape, t=F32: jax.ShapeDtypeStruct(shape, t)
    return pl.pallas_call(
        deliver_kernel,
        grid=(chunks,),
        in_specs=[
            whole(*sel.shape),
            pl.BlockSpec((1,) + ga.shape[1:], lambda i: (i, 0, 0, 0, 0)),
            pl.BlockSpec((2, rows, width), lambda i: (0, i, 0)),
            part,
            part,
            whole(*total.shape),
        ],
        out_specs=[
            part,
            part,
            whole(dense_rows, 3 * width),
            whole(dense_rows, width),
            whole(experts, dense_rows),
            whole(1, dense_rows),
            whole(1, dense_rows),
            grad,
            grad,
        ],
        out_shape=[
            S(tokens.shape, LOW),
            S(tokens.shape),
            S((dense_rows, 3 * width)),
            S((dense_rows, width)),
            S((experts, dense_rows)),
            S((1, dense_rows)),
            S((1, dense_rows)),
            S(other.shape[1:]),
            S(other.shape[1:]),
        ],
        compiler_params=pltpu.CompilerParams(vmem_limit_bytes=LARGE),
        cost_estimate=cost(5),
        name="deliver",
    )(sel, ga, other, tokens, grads, total)


def local(
    activations, qkv_weight, attn_weight, router_weight, gain_one, gain_two,
    expert_in, expert_out, segments, task_ids, task_experts, out_grad,
):
    packs, length, width = activations.shape
    planes = lax.axis_size("seq")
    groups = lax.axis_size("dp")
    cuts = 2 * packs
    assert cuts == planes == 4 and groups % 2 == 0
    piece = length // 2
    experts = router_weight.shape[1]
    hidden = expert_in.shape[0]
    assert experts + 2 <= TINY
    zeros = jnp.zeros((TINY - experts - 2, qkv_weight.shape[0]), LOW)
    tiny = jnp.concatenate([router_weight.T, gain_one[None], gain_two[None], zeros])
    tokens, grads, total, other, expert_grads, _, sel = layer(
        task_experts.T,
        activations.reshape(cuts, piece, width),
        segments,
        out_grad.reshape(cuts, piece, width),
        qkv_weight,
        attn_weight,
        tiny,
        task_ids,
        expert_in.reshape(hidden * experts, width),
        expert_out.reshape(hidden * experts, width),
        groups,
        planes,
        experts,
    )
    outputs, input_grad, qkv_grad, attn_grad, router_grad, first, second, win_grad, wout_grad = (
        deliver(
            sel,
            expert_grads,
            other.reshape(2, -1, width)[:, : hidden * experts],
            tokens,
            grads,
            total,
            experts,
        )
    )
    return (
        outputs.reshape(packs, length, width),
        input_grad.reshape(packs, length, width),
        qkv_grad,
        attn_grad,
        router_grad.T,
        first.reshape(-1),
        second.reshape(-1),
        win_grad.reshape(expert_in.shape),
        wout_grad.reshape(expert_in.shape),
    )


def solution(mesh):
    placed = (
        P("dp", "seq", None),
        P("dp", None),
        P("dp", None),
        P("dp", None),
        P("dp"),
        P("dp"),
        P(("dp", "seq"), None, None),
        P(("dp", "seq"), None, None),
        P("dp", "seq"),
        P("dp", "seq"),
        P(),
        P("dp", "seq", None),
    )
    return jax.shard_map(
        local,
        mesh=mesh,
        in_specs=placed,
        out_specs=(
            P("dp", "seq", None),
            P("dp", "seq", None),
            P("dp", None),
            P("dp", None),
            P("dp", None),
            P("dp"),
            P("dp"),
            P(("dp", "seq"), None, None),
            P(("dp", "seq"), None, None),
        ),
        check_vma=False,
    )
```

```python
import functools

import jax
import jax.numpy as jnp
from jax import lax
from jax.experimental import pallas as pl
from jax.experimental.pallas import tpu as pltpu
from jax.sharding import PartitionSpec as P

HEAD = 64
LANES = 128
SEG_COL = HEAD
LSE_COL = HEAD + 16
SEGMENTS = 16
FAR = 1e9
LARGE = 62 << 20
NT = (((1,), (1,)), ((), ()))
TN = (((0,), (0,)), ((), ()))
MESH = pl.DeviceIdType.MESH
EXPERTS_AT = LANES - 1
TINY = 16
F32 = jnp.float32
LOW = jnp.bfloat16


def dot(a, b):
    return jnp.dot(a, b, preferred_element_type=F32)


def dot_nt(a, b):
    return lax.dot_general(a, b, NT, preferred_element_type=F32)


def dot_tn(a, b):
    return lax.dot_general(a, b, TN, preferred_element_type=F32)


def thirds(values):
    high = values.astype(LOW).astype(F32)
    rest = values - high
    mid = rest.astype(LOW).astype(F32)
    return high, mid, rest - mid


def lanes_of(shape):
    return lax.broadcasted_iota(jnp.int32, shape, len(shape) - 1)


def put_thirds(base, values, column):
    lane = lanes_of(base.shape)
    high, mid, last = thirds(values)
    base = jnp.where(lane == column, high, base)
    base = jnp.where(lane == column + 1, mid, base)
    return jnp.where(lane == column + 2, last, base)


def normalize(values):
    center = values - jnp.mean(values, axis=-1, keepdims=True)
    inverse = lax.rsqrt(jnp.mean(center * center, axis=-1, keepdims=True) + 1e-05)
    return center * inverse, inverse


def norm_backward(upstream, scaled, inverse, gain_vec):
    direct = upstream * gain_vec
    return inverse * (
        direct
        - jnp.mean(direct, axis=-1, keepdims=True)
        - scaled * jnp.mean(direct * scaled, axis=-1, keepdims=True)
    )


def cost(micros):
    return pl.CostEstimate(flops=int(micros * 1e7), bytes_accessed=1 << 10, transcendentals=0)


def whole(*shape):
    return pl.BlockSpec(shape, lambda *_: (0,) * len(shape))


def remote(source, target, send, receive, device):
    return pltpu.make_async_remote_copy(
        src_ref=source,
        dst_ref=target,
        send_sem=send,
        recv_sem=receive,
        device_id=device,
        device_id_type=MESH,
    )


def each(count, body):
    def step(i, carry):
        body(i)
        return carry

    lax.fori_loop(0, count, step, 0)


def layer_kernel(
    groups, planes, experts, te, acts, seg, up_in, qkv_in, attn_in, tiny_in, task, win_in, wout_in,
    tokens_out, grads_out, total_out, other_got, ga_got, gb_got, far_w, sel_out,
    x, segx, up, res, stage, both, other, near_all, attn_all, tiny_all, small, sel, task_all, task_s,
    qa, ka, va, att, attf, normed, gates, slot, dv, send, got_a, got_b, out, dx, far_value, far_dx,
    far_gate, att_grad, att_send, attn_acc, router_acc, gain_acc, rest_part, rest_got, gb, key_t,
    dq_acc, qkv_acc, first_acc, qkv_part, qkv_got, part, heard, summed, sums,
    sem_x, sem_seg, sem_on, sem_seg_on, sem_up, sem_up_on, sem_near, sem_attn, sem_tiny, sem_task,
    sem_phase, sem_a, sem_b, sem_ga, sem_gb, sem_att, sem_far, sem_sums, sem_out, sem_att_back,
    sem_rest, sem_back, sem_qkv, sem_in, sem_part, sem_total, home, local,
):
    me = lax.axis_index("dp")
    place = lax.axis_index("seq")
    core = lax.rem(me, 2)
    base = me - core
    partner = (base + 1 - core, place)
    band = 2 * (place // 2)
    hub = 1 + place // 2
    at_hub = place == hub
    mine = me * 2 + lax.rem(place, 2)
    count = 2 * groups
    piece, width = x.shape[1], x.shape[2]
    tokens = 2 * planes * piece
    half = tokens // 2
    slots = send.shape[0]
    chunks, _, _, rows, _ = got_a.shape
    chunk_rows = rows * experts
    heads = qa.shape[0]
    pairs = heads // 2
    near_width = heads * HEAD
    near_cols = near_all.shape[2]
    dense_rows = tiny_all.shape[2]
    stays = (place // 2) == core
    spot = core + 2 * lax.rem(place, 2)
    kinds = range(3)
    used = [0]

    def copy_here(source, target):
        copy = pltpu.make_async_copy(source, target, local.at[used[0]])
        used[0] += 1
        return copy

    def rows_of(b, size):
        return pl.ds(pl.multiple_of(b * size, size), size)

    kind_rows = both.shape[0] // 2
    load_up = copy_here(up_in, res)
    load_both = [
        copy_here(source, both.at[pl.ds(kind * kind_rows, source.shape[0])])
        for kind, source in enumerate((win_in, wout_in))
    ]
    load_up.start()
    for copy in load_both:
        copy.start()
    greet_all(groups, planes)

    def goes(d):
        return jnp.logical_not(stays & (d == spot))

    def token_copies(piece_of, target, sem, sem_on):
        def give_piece(d):
            to = (base + lax.rem(d, 2), 2 * core + d // 2)
            return remote(piece_of(d), target.at[place], sem.at[0, d], sem.at[1, place], to)

        at_home = copy_here(piece_of(spot), target.at[place])

        def start():
            def one(d):
                @pl.when(goes(d))
                def _():
                    give_piece(d).start()

            each(planes, one)

            @pl.when(stays)
            def _():
                at_home.start()

        def onward(k):
            return remote(target.at[k], target.at[planes + k], sem_on.at[0, k], sem_on.at[1, k], partner)

        def receive(k):
            home = stays & (k == place)

            @pl.when(home)
            def _():
                at_home.wait()

            @pl.when(jnp.logical_not(home))
            def _():
                remote(piece_of(0), target.at[k], sem.at[0, 0], sem.at[1, k], partner).wait_recv()

            onward(k).start()

        def finish():
            def one(d):
                @pl.when(goes(d))
                def _():
                    give_piece(d).wait_send()

                onward(d).wait_send()

            each(planes, one)

        return start, receive, lambda k: onward(k).wait_recv(), finish

    def seg_piece(d):
        return seg.at[:, rows_of(lax.rem(d, 2), piece)]

    x_start, x_receive, x_far, x_finish = token_copies(lambda d: acts.at[d], x, sem_x, sem_on)
    seg_start, seg_receive, seg_far, seg_finish = token_copies(seg_piece, segx, sem_seg, sem_seg_on)
    up_start, up_receive, up_far, up_finish = token_copies(
        lambda d: stage.at[d], up, sem_up, sem_up_on
    )

    def way_back(source, target, sem):
        def give_piece(k):
            to = (base + place // 2, k)
            return remote(source.at[k], target.at[spot], sem.at[0, k], sem.at[1, spot], to)

        at_home = copy_here(source.at[place], target.at[spot])

        def start(k):
            home = stays & (k == place)

            @pl.when(jnp.logical_not(home))
            def _():
                give_piece(k).start()

            @pl.when(home)
            def _():
                at_home.start()

        def end(d):
            @pl.when(jnp.logical_not(stays & (d == place)))
            def _():
                give_piece(d).wait_send()

            @pl.when(goes(d))
            def _():
                remote(source.at[0], target.at[d], sem.at[0, 0], sem.at[1, d], partner).wait_recv()

            @pl.when(stays & (d == place))
            def _():
                at_home.wait()

        return start, lambda: each(planes, end)

    out_start, out_end = way_back(stage, tokens_out, sem_out)
    in_start, in_end = way_back(up, grads_out, sem_in)

    def others(body):
        each(groups - 1, lambda i: body(lax.rem(me + 1 + i, groups)))

    def give(source, target, sem, i):
        return remote(source, target.at[me], sem.at[0, i], sem.at[1, me], (i, place))

    def taken(source, target, sem, i):
        return remote(source, target.at[i], sem.at[0, i], sem.at[1, i], (i, place))

    def near_part(i, kind):
        at = 2 * kind * near_width + lax.rem(i, 2) * near_width
        return qkv_in.at[:, pl.ds(pl.multiple_of(at, near_width), near_width)]

    def near_copy(i, kind, to, of):
        return remote(
            near_part(to, kind),
            near_all.at[of, :, pl.ds(kind * near_width, near_width)],
            sem_near.at[0, i, kind],
            sem_near.at[1, of, kind],
            (i, place),
        )

    def part_of(kind, c):
        at = kind * kind_rows + c * chunk_rows
        return pl.ds(at if isinstance(c, int) else pl.multiple_of(at, chunk_rows), chunk_rows)

    def phase_copy(kind, c):
        r = rows_of(c, chunk_rows)
        return remote(
            (win_in, wout_in)[kind].at[r],
            far_w.at[lax.rem(place, 2), kind, r],
            sem_phase.at[0, 0, kind, c],
            sem_phase.at[1, lax.rem(place, 2), kind, c],
            (me, 3 - hub),
        )

    def phase_got(b, kind, c):
        r = rows_of(c, chunk_rows)
        return remote(
            (win_in, wout_in)[kind].at[r],
            far_w.at[b, kind, r],
            sem_phase.at[0, 0, kind, c],
            sem_phase.at[1, b, kind, c],
            (me, 2 - band + b),
        )

    def ring(c, b):
        at = lax.rem(2 * c + b, 4) * 2 * chunk_rows
        return at if isinstance(at, int) else pl.multiple_of(at, chunk_rows)

    def sums_copy(kind, c, b):
        r = pl.ds(ring(c, b) + kind * chunk_rows, chunk_rows)
        return remote(
            sums.at[r],
            other_got.at[part_of(kind, c)],
            sem_sums.at[0, b, kind, c],
            sem_sums.at[1, 0, kind, c],
            (me, 2 - band + b),
        )

    def sums_got(kind, c):
        r = part_of(kind, c)
        return remote(
            sums.at[pl.ds(0, chunk_rows)],
            other_got.at[r],
            sem_sums.at[0, 0, kind, c],
            sem_sums.at[1, 0, kind, c],
            (me, 3 - hub),
        )

    def band_device(m):
        return (m // 2, band + lax.rem(m, 2))

    def band_copies(source, target, sem, home_sem):
        def give_part(c, m):
            to = band_device(m)
            return remote(source(c, m), target(c, mine), sem.at[c, 0, m], sem.at[c, 1, mine], to)

        def at_home(c):
            return pltpu.make_async_copy(source(c, mine), target(c, mine), home_sem.at[c])

        def run(body):
            each(count - 1, lambda i: body(lax.rem(mine + 1 + i, count)))

        def start(c):
            run(lambda m: give_part(c, m).start())
            at_home(c).start()

        def sent(c):
            run(lambda m: give_part(c, m).wait_send())

        def received(c):
            run(
                lambda m: remote(
                    source(c, m), target(c, m), sem.at[c, 0, m], sem.at[c, 1, m], band_device(m)
                ).wait_recv()
            )
            at_home(c).wait()

        return start, sent, received

    def by_chunk(source, target, sem, home_sem):
        return band_copies(
            lambda c, m: source.at[c, m], lambda c, m: target.at[c, m], sem, home_sem
        )

    a_start, a_sent, a_received = band_copies(
        lambda c, m: send.at[pl.ds(0, chunks), m], lambda c, m: got_a.at[:, m], sem_a, home.at[3]
    )
    ga_start, ga_sent, ga_received = by_chunk(got_a, ga_got, sem_ga, home.at[0])

    def far_rows(dp):
        return pl.ds(2 * dp, 2)

    def b_slots(c):
        return pl.ds(lax.rem(2 * c, slots), 2)

    def b_part(c, m):
        return remote(
            send.at[b_slots(c), m],
            got_b.at[c, far_rows(me)],
            sem_b.at[c, 0, m],
            sem_b.at[c, 1, me],
            band_device(m),
        )

    def b_home(c):
        return pltpu.make_async_copy(
            send.at[b_slots(c), mine], got_b.at[c, far_rows(me)], home.at[1, c]
        )

    def others_of_band(body):
        each(count - 1, lambda i: body(lax.rem(mine + 1 + i, count)))

    def b_start(c):
        b_home(c).start()
        others_of_band(lambda m: b_part(c, m).start())
        b_home(c).wait()

    def b_sent(c):
        others_of_band(lambda m: b_part(c, m).wait_send())

    def b_received(c):
        def one(dp):
            @pl.when(jnp.logical_not(at_hub & (dp == me)))
            def _():
                remote(
                    send.at[pl.ds(0, 2), 0],
                    got_b.at[c, far_rows(dp)],
                    sem_b.at[c, 0, dp],
                    sem_b.at[c, 1, dp],
                    (dp, hub),
                ).wait_recv()

        each(groups, one)

    def gb_part(c, dp):
        return remote(
            got_b.at[c, far_rows(dp)],
            gb_got.at[c, :, :, rows_of(mine, rows)],
            sem_gb.at[c, 0, dp],
            sem_gb.at[c, 1, mine],
            (dp, hub),
        )

    def gb_home(c):
        target = gb_got.at[c, :, :, rows_of(mine, rows)]
        return pltpu.make_async_copy(got_b.at[c, far_rows(me)], target, home.at[2, c])

    def gb_each(body):
        def one(j):
            dp = lax.rem(me + 1 + j, groups)

            @pl.when(jnp.logical_not(at_hub & (dp == me)))
            def _():
                body(dp)

        each(groups, one)

    def gb_start(c):
        gb_each(lambda dp: gb_part(c, dp).start())

        @pl.when(at_hub)
        def _():
            gb_home(c).start()

    def gb_sent(c):
        gb_each(lambda dp: gb_part(c, dp).wait_send())

    def gb_received(c):
        others_of_band(
            lambda m: remote(
                got_b.at[c, pl.ds(0, 2)],
                gb_got.at[c, :, :, rows_of(m, rows)],
                sem_gb.at[c, 0, 0],
                sem_gb.at[c, 1, m],
                band_device(m),
            ).wait_recv()
        )
        gb_home(c).wait()

    def staged(b, kind, size):
        at = (2 * b + kind) * size
        return pl.ds(at if 4 * size <= other.shape[0] else 0, size)

    def load_gb(c, b, kind):
        target = other.at[staged(b, kind, count * rows)]
        return pltpu.make_async_copy(gb_got.at[c, b, kind], target, home.at[5 + b, kind])

    x_start()
    seg_start()
    task_part = task.at[:, pl.ds(0, LANES)]
    others(lambda i: give(task_part, task_all, sem_task, i).start())
    others(lambda i: give(tiny_in, tiny_all, sem_tiny, i).start())

    def start_near(i):
        for kind in kinds:
            near_copy(i, kind, i, me).start()

    others(start_near)
    own_task = copy_here(task_part, task_all.at[me])
    own_dense = [
        copy_here(tiny_in, tiny_all.at[me]),
        copy_here(attn_in, attn_all.at[me]),
    ] + [
        copy_here(near_part(me, kind), near_all.at[me, :, pl.ds(kind * near_width, near_width)])
        for kind in kinds
    ]
    for copy in [own_task] + own_dense:
        copy.start()
    load_up.wait()
    stage[...] = res[...].astype(LOW)
    others(lambda i: taken(task_part, task_all, sem_task, i).wait_recv())
    own_task.wait()
    to_scalars = copy_here(task_all, task_s)
    to_scalars.start()
    to_scalars.wait()

    def expert_of(dp, z):
        at = z // 2 + dp - lax.rem(dp, 2)
        return te[lax.rem(dp, 2), task_s[at, lax.rem(z, 2), 0]]

    mine_id = expert_of(me, place)
    other_id = expert_of(partner[0], place)

    sel_row = lax.broadcasted_iota(jnp.int32, (rows, chunk_rows), 0)
    sel_col = lax.broadcasted_iota(jnp.int32, (rows, chunk_rows), 1)

    def fill_sel(m):
        dp, z = band_device(m)
        hit = sel_col == sel_row * experts + expert_of(dp, z)
        sel[m] = jnp.where(hit, 1.0, 0.0).astype(LOW)

    each(count, fill_sel)
    save_sel = copy_here(sel, sel_out)
    save_sel.start()

    def choose(source, target):
        choice = sel[...].reshape(count * rows, chunk_rows)
        for kind in range(2):
            values = dot(choice, source(kind))
            target[:, kind] = values.astype(LOW).reshape(count, rows, width)

    for copy in load_both:
        copy.wait()
    each(chunks, lambda c: choose(lambda kind: both[part_of(kind, c), :], send.at[c]))

    def end_near(i):
        for kind in kinds:
            near_copy(i, kind, i, i).wait_recv()

    others(end_near)
    others(lambda i: taken(tiny_in, tiny_all, sem_tiny, i).wait_recv())
    for copy in own_dense:
        copy.wait()
    eye = lax.broadcasted_iota(jnp.int32, (TINY, LANES), 0) == lanes_of((TINY, LANES))
    eye = jnp.where(eye, 1.0, 0.0).astype(LOW)

    def turn(i):
        small[rows_of(i, dense_rows), :] = dot_tn(tiny_all[i], eye)

    each(groups, turn)

    turned = small[...].T
    first_gain = turned[experts : experts + 1]
    second_gain = turned[experts + 1 : experts + 2]
    lane = lanes_of((piece, LANES))

    def project(k):
        scaled, _ = normalize(x[k].astype(F32))
        low = (scaled * first_gain).astype(LOW)
        values = dot(low, near_all[...].reshape(width, near_cols))
        segment = segx[k, pl.ds(lax.rem(place, 2), 1)].astype(F32)
        segment = jnp.broadcast_to(segment, (LANES, piece)).T
        same = (lane - SEG_COL).astype(F32) == segment
        in_seg = (lane >= SEG_COL) & (lane < SEG_COL + SEGMENTS)
        q_more = jnp.where(same, 1.0, 0.0)
        k_more = jnp.where(in_seg & jnp.logical_not(same), -FAR, 0.0)
        k_more = jnp.where((lane >= LSE_COL) & (lane < LSE_COL + 3), 1.0, k_more)
        v_more = jnp.where((lane >= HEAD) & (lane < HEAD + 3), 1.0, 0.0)
        r = rows_of(k, piece)

        def head(kind, h, more):
            at = kind * near_width + h // 2 * LANES
            values_of = values[:, at : at + LANES]
            if h % 2:
                values_of = pltpu.roll(values_of, HEAD, 1)
            return jnp.where(lane < HEAD, values_of, more)

        for h in range(heads):
            query = head(0, h, 0.0).astype(LOW).astype(F32) * HEAD**-0.5
            qa[h, r, :] = (query + q_more).astype(LOW)
            ka[h, r, :] = head(1, h, k_more).astype(LOW)
            va[h, r, :] = head(2, h, v_more).astype(LOW)

    def by_distance(k):
        return lax.bitwise_xor(place, jnp.int32(k))

    def arrive(k):
        x_receive(k)
        seg_receive(k)

    def start_phase(c):
        for kind in range(2):
            phase_copy(kind, c).start()

    def far_piece(k):
        x_far(k)
        seg_far(k)
        project(planes + k)

    near_order = [by_distance(k) for k in range(planes)]
    arrive(near_order[0])
    project(near_order[0])
    arrive(near_order[1])
    project(near_order[1])
    far_piece(near_order[0])
    for k in near_order[2:]:
        arrive(k)
    up_start()
    a_start(0)
    for c in range(min(2, chunks)):
        start_phase(c)
    others(lambda i: give(attn_in, attn_all, sem_attn, i).start())
    far_piece(near_order[1])
    for k in near_order[2:]:
        project(k)
    for k in near_order[2:]:
        far_piece(k)

    block = min(512, half)

    def att_copy(p):
        return remote(att.at[p], attf.at[p], sem_att.at[0, p], sem_att.at[1, p], partner)

    for p in range(pairs):

        def attend(i):
            r = rows_of(i, block)
            parts = []
            for h in (2 * p, 2 * p + 1):
                query = qa[h, r, :]
                scores = dot_nt(query, ka[h])
                top = jnp.max(scores, axis=1, keepdims=True)
                probs = jnp.exp(scores - top).astype(LOW)
                mixed = dot(probs, va[h])
                total = mixed[:, HEAD : HEAD + 1]
                parts.append(mixed[:, :HEAD] / total)
                lse = top + jnp.log(total)
                qa[h, r, :] = put_thirds(query.astype(F32), -lse, LSE_COL).astype(LOW)
            att[p, r, :] = jnp.concatenate(parts, axis=1).astype(LOW)

        each(tokens // block, attend)
        att_copy(p).start()
        if p == 0:
            for c in range(2, chunks):
                start_phase(c)

    def other_weights(c):
        @pl.when(at_hub)
        def _():
            loads = []
            for b in range(2):
                for kind in range(2):
                    phase_got(b, kind, c).wait_recv()
                    source = far_w.at[b, kind, rows_of(c, chunk_rows)]
                    target = other.at[staged(b, kind, chunk_rows)]
                    loads.append(pltpu.make_async_copy(source, target, home.at[7 + b, kind]))
                    loads[-1].start()

            @pl.when(2 * c >= slots)
            def _():
                b_sent(c - slots // 2)

            for b in range(2):
                for kind in range(2):
                    loads[2 * b + kind].wait()
                choose(
                    lambda kind: other[staged(b, kind, chunk_rows), :],
                    send.at[lax.rem(2 * c, slots) + b],
                )
            b_start(c)

    for k in range(planes):
        up_receive(by_distance(k))
    for p in range(pairs):
        att_copy(p).wait_recv()
    others(lambda i: taken(attn_in, attn_all, sem_attn, i).wait_recv())

    def weight_rows(which):
        values = attn_all[pl.ds(which * (groups // 2), groups // 2)]
        return values.reshape(width // 2, width)

    def middle(b):
        @pl.when(b >= planes)
        def _():
            up_far(b - planes)

        r = rows_of(b, piece)
        f = rows_of(lax.rem(b + planes, 2 * planes), piece)
        residual = x[b].astype(F32)
        near_att = jnp.concatenate([att[p, r, :] for p in range(pairs)], axis=1)
        far_att = jnp.concatenate([attf[p, f, :] for p in range(pairs)], axis=1)
        residual += dot(near_att, weight_rows(core)) + dot(far_att, weight_rows(1 - core))

        @pl.when(b < planes)
        def _():
            res[b] = residual

        scaled, _ = normalize(residual)
        low = (scaled * second_gain).astype(LOW)
        normed[r, :] = low
        logits = dot(low, small[...].astype(LOW))
        of_mine = jnp.sum(jnp.where(lane == mine_id, logits, 0.0), axis=1, keepdims=True)
        of_other = jnp.sum(jnp.where(lane == other_id, logits, 0.0), axis=1, keepdims=True)
        top = jnp.maximum(of_mine, of_other)
        of_mine = jnp.exp(of_mine - top)
        of_other = jnp.exp(of_other - top)
        total = of_mine + of_other
        gate = of_mine / total
        gates[r, :] = jnp.where(lane == 0, gate, jnp.where(lane == 1, of_other / total, 0.0))
        slot[r, :] = (gate * up[b].astype(F32)).astype(LOW)

    each(2 * planes, middle)

    def add_up_others(c):
        @pl.when(at_hub)
        def _():
            together = 4 * count * rows <= other.shape[0]
            choice = sel[...].reshape(count * rows, chunk_rows)
            gb_received(c)
            if together:
                for b in range(2):
                    for kind in range(2):
                        load_gb(c, b, kind).start()
            for b in range(2):

                @pl.when(2 * c + b >= 4)
                def _():
                    for kind in range(2):
                        sums_copy(kind, c - 2, b).wait_send()

                for kind in range(2):
                    if not together:
                        load_gb(c, b, kind).start()
                    load_gb(c, b, kind).wait()
                    r = pl.ds(ring(c, b) + kind * chunk_rows, chunk_rows)
                    values = other[staged(b, kind, count * rows), :]
                    sums[r, :] = dot_tn(choice, values).astype(LOW)
                    sums_copy(kind, c, b).start()

    out[...] = jnp.zeros_like(out)
    dx[...] = jnp.zeros_like(dx)
    per = max(1, 256 // rows)

    def expert(weights, c):
        def tile(t):
            at = pl.ds(t * per, per)
            win = weights[c, at, 0].reshape(per * rows, width)
            wout = weights[c, at, 1].reshape(per * rows, width)
            pre = dot_nt(normed[...], win)
            hidden_grad = dot_nt(slot[...], wout)
            cdf = 0.5 * (1.0 + lax.erf(pre * 0.7071067811865476))
            slope = cdf + pre * jnp.exp(-0.5 * pre * pre) * 0.3989422804014327
            hidden = (pre * cdf).astype(LOW)
            pre_grad = (hidden_grad * slope).astype(LOW)
            out[...] += dot(hidden, wout)
            dx[...] += dot(pre_grad, win)
            weights[c, at, 0] = dot_tn(pre_grad, normed[...]).astype(LOW).reshape(per, rows, width)
            weights[c, at, 1] = dot_tn(hidden, slot[...]).astype(LOW).reshape(per, rows, width)

        each(count // per, tile)

    a_sent(0)
    a_received(0)
    other_weights(0)

    def step_of(j):
        @pl.when(j < chunks)
        def _():
            expert(got_a, j)

        @pl.when(j + 1 < chunks)
        def _():
            other_weights(j + 1)

        @pl.when(j > 0)
        def _():
            b_received(j - 1)
            expert(got_b, j - 1)
            gb_start(j - 1)

        if chunks > 1:

            @pl.when(j == chunks)
            def _():
                add_up_others(0)

    each(chunks + 1, step_of)

    @pl.when(at_hub)
    def _():
        for c in range(chunks - slots // 2, chunks):
            b_sent(c)

    step = half // 2
    step_lane = lanes_of((step, LANES))
    for at in range(0, tokens, step):
        r = pl.ds(at, step)
        value = out[r, :]
        upstream = up[pl.ds(at // piece, step // piece)].reshape(step, width).astype(F32)
        gate_grad = jnp.sum(value * upstream, axis=1, keepdims=True)
        value = value * gates[r, 0:1]
        if at < half:
            out[r, :] = value
            gates[r, :] = jnp.where(step_lane == 2, gate_grad, gates[r, :])
        else:
            t = pl.ds(at - half, step)
            other[t, :] = value.astype(LOW)
            both[t, :] = dx[r, :].astype(LOW)
            gates[r, :] = jnp.broadcast_to(gate_grad, (step, LANES))
    far_copies = [
        remote(other.at[pl.ds(0, half)], far_value, sem_far.at[0, 0], sem_far.at[1, 0], partner),
        remote(both.at[pl.ds(0, half)], far_dx, sem_far.at[0, 1], sem_far.at[1, 1], partner),
        remote(gates.at[pl.ds(half, half)], far_gate, sem_far.at[0, 2], sem_far.at[1, 2], partner),
    ]
    for copy in far_copies:
        copy.start()
    up_finish()
    res_grad = out.at[pl.ds(half, half)]
    attn_acc[...] = jnp.zeros_like(attn_acc)
    router_acc[...] = jnp.zeros_like(router_acc)
    gain_acc[...] = jnp.zeros_like(gain_acc)
    for copy in far_copies:
        copy.wait()
    if chunks > 1:
        add_up_others(1)


    def post(b):
        r = rows_of(b, piece)
        residual = res[b]
        upstream = up[b].astype(F32)
        stage[b] = (residual + out[r, :] + far_value[r, :].astype(F32)).astype(LOW)
        out_start(b)
        gate = gates[r, :]
        gate_mine, gate_other, grad_mine = gate[:, 0:1], gate[:, 1:2], gate[:, 2:3]
        grad_other = far_gate[r, 0:1]
        mean = gate_mine * grad_mine + gate_other * grad_other
        logit_grad = jnp.where(lane == mine_id, gate_mine * (grad_mine - mean), 0.0)
        logit_grad += jnp.where(lane == other_id, gate_other * (grad_other - mean), 0.0)
        normed_grad = dx[r, :] + far_dx[r, :].astype(F32)
        router = small[...].astype(LOW)
        for third in thirds(logit_grad):
            third = third.astype(LOW)
            router_acc[...] += dot_tn(normed[r, :], third)
            normed_grad += dot_nt(third, router)
        scaled, inverse = normalize(residual)
        gain_acc[...] += jnp.sum(normed_grad * scaled, axis=0, keepdims=True)
        residual_grad = upstream + norm_backward(normed_grad, scaled, inverse, second_gain)
        res_grad[r, :] = residual_grad
        low = residual_grad.astype(LOW)
        f = pl.ds(pl.multiple_of(half + b * piece, piece), piece)
        both_att = [att[p, r, :] for p in range(pairs)] + [attf[p, f, :] for p in range(pairs)]
        for i, values in enumerate(both_att):
            attn_acc[i * LANES : (i + 1) * LANES] += dot_tn(values, low)
        near_back = dot_nt(low, weight_rows(core)).astype(LOW)
        far_back = dot_nt(low, weight_rows(1 - core)).astype(LOW)
        for p in range(pairs):
            att_grad[p, r, :] = near_back[:, p * LANES : (p + 1) * LANES]
            att_send[p, r, :] = far_back[:, p * LANES : (p + 1) * LANES]

    each(planes, post)

    def att_back_copy(p):
        target = att_grad.at[p, pl.ds(half, half)]
        return remote(att_send.at[p], target, sem_att_back.at[0, p], sem_att_back.at[1, p], partner)

    for p in range(pairs):
        att_back_copy(p).start()
    own_rows = near_width // dense_rows
    turned = jnp.broadcast_to(gain_acc[...], (LANES, width)).T
    tail = jnp.where(lanes_of(turned.shape) == EXPERTS_AT, turned, router_acc[...]).astype(LOW)
    rest_part[:, :, width:] = tail.reshape(groups, dense_rows, LANES)
    for side in range(2):
        values = attn_acc[side * near_width : (side + 1) * near_width].astype(LOW)
        at = core if side == 0 else 1 - core
        rest_part[pl.ds(at * own_rows, own_rows), :, :width] = values.reshape(
            own_rows, dense_rows, width
        )

    def rest_copy(i):
        return give(rest_part.at[i], rest_got, sem_rest, i)

    others(lambda i: rest_copy(i).start())

    for c in range(2, chunks - 1):
        add_up_others(c)

    all_lane = lanes_of((tokens, LANES))
    for p in range(pairs):
        att_back_copy(p).wait_recv()
        halves = []
        for side in range(2):
            h = 2 * p + side
            pair_grad = att_grad[p].astype(F32)
            inner = pair_grad * att[p].astype(F32)
            if side == 1:
                pair_grad = pltpu.roll(pair_grad, HEAD, 1)
                inner = pltpu.roll(inner, HEAD, 1)
            delta = jnp.sum(jnp.where(all_lane < HEAD, inner, 0.0), axis=1, keepdims=True)
            pair_grad = jnp.where(all_lane < HEAD, pair_grad, 0.0)
            gb[...] = put_thirds(pair_grad, -delta, HEAD).astype(LOW)
            key_t[...] = ka[h].T[:HEAD]
            dq_acc[...] = jnp.zeros_like(dq_acc)
            dk_cols = pl.ds((pairs + p) * LANES + side * HEAD, HEAD)
            dv_cols = pl.ds(p * LANES + side * HEAD, HEAD)

            def keys(i):
                r = rows_of(i, block)
                weights = jnp.exp(dot_nt(ka[h, r, :], qa[h]))
                centered = dot_nt(va[h, r, :], gb[...])
                score_grad = (weights * centered).astype(LOW)
                dv[r, dv_cols] = dot(weights.astype(LOW), gb[...])[:, :HEAD].astype(LOW)
                slot[r, dk_cols] = dot(score_grad, qa[h])[:, :HEAD].astype(LOW)
                dq_acc[...] += dot(key_t[:, r], score_grad)

            each(tokens // block, keys)
            halves.append(dq_acc[...].T * HEAD**-0.5)
            if h == 0:
                add_up_others(chunks - 1)
                each(chunks, ga_start)
        slot[:, p * LANES : (p + 1) * LANES] = jnp.concatenate(halves, axis=1).astype(LOW)

    qkv_acc[...] = jnp.zeros_like(qkv_acc)
    first_acc[...] = jnp.zeros_like(first_acc)
    back_near = dx.at[pl.ds(half, half)]
    back_send = normed.at[pl.ds(0, half)]
    back_got = normed.at[pl.ds(half, half)]

    def project_back(b):
        r = rows_of(b, piece)
        values = jnp.concatenate([slot[r, :], dv[r, :]], axis=1)
        scaled, _ = normalize(x[b].astype(F32))
        back = dot_nt(values, near_all[...].reshape(width, near_cols))
        qkv_acc[...] += dot_tn((scaled * first_gain).astype(LOW), values)
        first_acc[...] += jnp.sum(back * scaled, axis=0, keepdims=True)
        return back

    def far_block(i):
        back_send[rows_of(i, piece), :] = project_back(planes + i).astype(LOW)

    def near_block(i):
        back_near[rows_of(i, piece), :] = project_back(i)

    each(planes, far_block)
    back_copy = remote(back_send, back_got, sem_back.at[0], sem_back.at[1], partner)
    back_copy.start()
    each(planes, near_block)
    qkv_part[:, :, :near_cols] = qkv_acc[...].astype(LOW).reshape(groups, dense_rows, near_cols)
    turned = jnp.broadcast_to(first_acc[...], (LANES, width)).T.astype(LOW)
    qkv_part[:, :, near_cols:] = turned.reshape(groups, dense_rows, LANES)

    def qkv_copy(i):
        return give(qkv_part.at[i], qkv_got, sem_qkv, i)

    others(lambda i: qkv_copy(i).start())

    back_copy.wait_recv()

    def finish(b):
        r = rows_of(b, piece)
        scaled, inverse = normalize(x[b].astype(F32))
        grad = back_near[r, :] + back_got[r, :].astype(F32)
        first = norm_backward(grad, scaled, inverse, first_gain)
        up[b] = (res_grad[r, :] + first).astype(LOW)
        in_start(b)

    each(planes, finish)

    others(lambda i: taken(rest_part.at[i], rest_got, sem_rest, i).wait_recv())
    others(lambda i: taken(qkv_part.at[i], qkv_got, sem_qkv, i).wait_recv())

    def from_group(mine_part, got, i):
        return jnp.where(i == me, mine_part[i], got[i]).astype(F32)

    def add(j, sums_of):
        first, second, rest = sums_of
        first += from_group(qkv_part, qkv_got, 2 * j)
        second += from_group(qkv_part, qkv_got, 2 * j + 1)
        rest += from_group(rest_part, rest_got, 2 * j)
        rest += from_group(rest_part, rest_got, 2 * j + 1)
        return first, second, rest

    zero = jnp.zeros(qkv_part.shape[1:], F32)
    first, second, rest = lax.fori_loop(
        0, groups // 2, add, (zero, zero, jnp.zeros(rest_part.shape[1:], F32))
    )
    columns = []
    for kind in kinds:
        for side in (first, second):
            columns.append(side[:, kind * near_width : (kind + 1) * near_width])
    columns += [rest, first[:, near_cols:] + second[:, near_cols:]]
    share = jnp.concatenate(columns, axis=1).astype(LOW)
    cut = dense_rows // planes
    for z in range(planes):
        part[z] = share[z * cut : (z + 1) * cut]

    def over_planes(body):
        each(planes - 1, lambda i: body(lax.rem(place + 1 + i, planes)))

    def tell_part(z):
        return remote(part.at[z], heard.at[place], sem_part.at[0, z], sem_part.at[1, place], (me, z))

    def hear_part(z):
        return remote(part.at[z], heard.at[z], sem_part.at[0, z], sem_part.at[1, z], (me, z))

    def tell_sum(z):
        target = total_out.at[place]
        return remote(summed, target, sem_total.at[0, z], sem_total.at[1, place], (me, z))

    def hear_sum(z):
        return remote(summed, total_out.at[z], sem_total.at[0, z], sem_total.at[1, z], (me, z))

    over_planes(lambda z: tell_part(z).start())
    over_planes(lambda z: hear_part(z).wait_recv())
    sum_of = part[place].astype(F32)
    for k in range(1, planes):
        sum_of += heard[lax.rem(place + k, planes)].astype(F32)
    summed[...] = sum_of.astype(LOW)
    over_planes(lambda z: tell_sum(z).start())
    put = copy_here(summed, total_out.at[place])
    put.start()

    x_finish()
    seg_finish()

    def end_dense(i):
        give(task_part, task_all, sem_task, i).wait_send()
        give(tiny_in, tiny_all, sem_tiny, i).wait_send()
        give(attn_in, attn_all, sem_attn, i).wait_send()
        for kind in kinds:
            near_copy(i, kind, i, me).wait_send()
        rest_copy(i).wait_send()
        qkv_copy(i).wait_send()

    others(end_dense)
    save_sel.wait()
    for p in range(pairs):
        att_copy(p).wait_send()
        att_back_copy(p).wait_send()
    back_copy.wait_send()
    for c in range(chunks):
        ga_sent(c)
        ga_received(c)
        gb_sent(c)
        for kind in range(2):
            phase_copy(kind, c).wait_send()
            sums_got(kind, c).wait_recv()

    @pl.when(at_hub)
    def _():
        for k in range(max(0, 2 * chunks - 4), 2 * chunks):
            for kind in range(2):
                sums_copy(kind, k // 2, k % 2).wait_send()

    over_planes(lambda z: tell_part(z).wait_send())
    over_planes(lambda z: tell_sum(z).wait_send())
    over_planes(lambda z: hear_sum(z).wait_recv())
    put.wait()
    out_end()
    in_end()


def greet_all(groups, planes):
    me = lax.axis_index("dp")
    place = lax.axis_index("seq")
    base = me - lax.rem(me, 2)
    band = 2 * (place // 2)
    mine = me * 2 + lax.rem(place, 2)
    barrier = pltpu.get_barrier_semaphore()

    def signal(dp, z):
        pl.semaphore_signal(barrier, inc=1, device_id=(dp, z), device_id_type=MESH)

    def near_planes(i):
        m = lax.rem(mine + 1 + i, 2 * groups)
        signal(m // 2, band + lax.rem(m, 2))

    each(2 * groups - 1, near_planes)
    each(4, lambda i: signal(base + i // 2, 2 - band + lax.rem(i, 2)))
    pl.semaphore_wait(barrier, 2 * groups + 3)


def layer(te, acts, seg, up_in, qkv, attn, tiny, task, win, wout, groups, planes, experts):
    _, piece, width = acts.shape
    half = planes * piece
    tokens = 2 * half
    heads = width // HEAD // 2
    pairs = heads // 2
    hidden = win.shape[0] // experts
    chunks = 4 if hidden % 64 == 0 else 1
    rows = hidden // chunks
    count = 2 * groups
    dense_rows = qkv.shape[0]
    near_cols = 3 * heads * HEAD
    anywhere = pl.BlockSpec(memory_space=pl.ANY)
    dma = pltpu.SemaphoreType.DMA
    S = lambda shape, t=LOW: jax.ShapeDtypeStruct(shape, t)
    V = lambda shape, t=LOW: pltpu.VMEM(shape, t)
    pieces = (planes, piece, width)
    head_shape = (heads, tokens, LANES)
    pair_shape = (pairs, tokens, LANES)
    band_shape = (chunks, count, 2, rows, width)
    both_shape = (max(half, 2 * win.shape[0]), width)
    sel_shape = (count, rows, rows * experts)
    rest_shape = (groups, dense_rows, width + LANES)
    qkv_shape = (groups, dense_rows, near_cols + LANES)
    total = (planes, dense_rows // planes, 4 * width + 2 * LANES)
    return pl.pallas_call(
        functools.partial(layer_kernel, groups, planes, experts),
        in_specs=[pl.BlockSpec(memory_space=pltpu.SMEM)] + [anywhere] * 9,
        out_specs=[anywhere] * 8,
        out_shape=[
            S(pieces),
            S(pieces),
            S(total),
            S(both_shape),
            S(band_shape),
            S((chunks, 2, 2, count * rows, width)),
            S((2, 2) + win.shape),
            S(sel_shape),
        ],
        scratch_shapes=[
            V((2 * planes, piece, width)),
            V((2 * planes, 2, piece), jnp.int32),
            V((2 * planes, piece, width)),
            V(pieces, F32),
            V(pieces),
            V(both_shape),
            V(both_shape),
            V((groups, dense_rows, near_cols)),
            V((groups, dense_rows, width)),
            V((groups,) + tiny.shape),
            V((width, LANES), F32),
            V(sel_shape),
            V((groups, 2, LANES), jnp.int32),
            pltpu.SMEM((groups, 2, LANES), jnp.int32),
            V(head_shape),
            V(head_shape),
            V(head_shape),
            V(pair_shape),
            V(pair_shape),
            V((tokens, width)),
            V((tokens, LANES), F32),
            V((tokens, width)),
            V((tokens, heads * HEAD)),
            V((max(2, chunks),) + band_shape[1:]),
            V(band_shape),
            V(band_shape),
            V((tokens, width), F32),
            V((tokens, width), F32),
            V((half, width)),
            V((half, width)),
            V((half, LANES), F32),
            V(pair_shape),
            V((pairs, half, LANES)),
            V((width, width), F32),
            V((width, LANES), F32),
            V((1, width), F32),
            V(rest_shape),
            V(rest_shape),
            V((tokens, LANES)),
            V((HEAD, tokens)),
            V((HEAD, tokens), F32),
            V((width, near_cols), F32),
            V((1, width), F32),
            V(qkv_shape),
            V(qkv_shape),
            V(total),
            V(total),
            V(total[1:]),
            V(both_shape),
        ]
        + [dma((2, planes))] * 6
        + [dma((2, groups, 3))]
        + [dma((2, groups))] * 3
        + [dma((2, 2, 2, chunks)), dma((1, 2, count))]
        + [dma((chunks, 2, count))] * 3
        + [dma((2, pairs)), dma((2, 3)), dma((2, 2, 2, chunks)), dma((2, planes)), dma((2, pairs))]
        + [dma((2, groups)), dma((2,)), dma((2, groups))]
        + [dma((2, planes))] * 3
        + [dma((9, max(2, chunks))), dma((32,))],
        compiler_params=pltpu.CompilerParams(
            collective_id=0, has_side_effects=True, vmem_limit_bytes=LARGE
        ),
        cost_estimate=cost(250),
        name="layer",
    )(te, acts, seg, up_in, qkv, attn, tiny, task, win, wout)


def deliver_kernel(
    sel, ga, other, tokens, grads, total,
    outputs, input_grad, qkv_grad, attn_grad, router_grad, first, second, win_grad, wout_grad,
):
    outputs[...] = tokens[...]
    input_grad[...] = grads[...].astype(F32)
    count, rows, columns = sel.shape
    width = ga.shape[4]
    choice = sel[...].reshape(count * rows, columns)
    for kind, grad in ((0, win_grad), (1, wout_grad)):
        for c in range(ga.shape[0]):
            r = slice(c * columns, (c + 1) * columns)
            values = dot_tn(choice, ga[c, :, kind].reshape(count * rows, width))
            grad[r] = values + other[kind, r].astype(F32)

    @pl.when(pl.program_id(0) == 0)
    def _():
        planes, cut, _ = total.shape
        for z in range(planes):
            r = slice(z * cut, (z + 1) * cut)
            values = total[z].astype(F32)
            qkv_grad[r] = values[:, : 3 * width]
            attn_grad[r] = values[:, 3 * width : 4 * width]
        small = jnp.concatenate([total[z, :, 4 * width :].astype(F32) for z in range(planes)])
        turned = small[:, :LANES].T
        router_grad[...] = turned[: router_grad.shape[0]]
        second[...] = turned[EXPERTS_AT : EXPERTS_AT + 1]
        first[...] = small[:, LANES:].T[0:1]


def deliver(sel, ga, other, tokens, grads, total, experts):
    chunks = ga.shape[0]
    steps = min(2, chunks)
    per = chunks // steps
    planes, piece, width = tokens.shape
    dense_rows = total.shape[0] * total.shape[1]
    part = pl.BlockSpec((planes // steps, piece, width), lambda i: (i, 0, 0))
    rows = other.shape[1] // steps
    grad = pl.BlockSpec((rows, width), lambda i: (i, 0))
    S = lambda shape, t=F32: jax.ShapeDtypeStruct(shape, t)
    return pl.pallas_call(
        deliver_kernel,
        grid=(steps,),
        in_specs=[
            whole(*sel.shape),
            pl.BlockSpec((per,) + ga.shape[1:], lambda i: (i, 0, 0, 0, 0)),
            pl.BlockSpec((2, rows, width), lambda i: (0, i, 0)),
            part,
            part,
            whole(*total.shape),
        ],
        out_specs=[
            part,
            part,
            whole(dense_rows, 3 * width),
            whole(dense_rows, width),
            whole(experts, dense_rows),
            whole(1, dense_rows),
            whole(1, dense_rows),
            grad,
            grad,
        ],
        out_shape=[
            S(tokens.shape, LOW),
            S(tokens.shape),
            S((dense_rows, 3 * width)),
            S((dense_rows, width)),
            S((experts, dense_rows)),
            S((1, dense_rows)),
            S((1, dense_rows)),
            S(other.shape[1:]),
            S(other.shape[1:]),
        ],
        compiler_params=pltpu.CompilerParams(vmem_limit_bytes=LARGE),
        cost_estimate=cost(5),
        name="deliver",
    )(sel, ga, other, tokens, grads, total)


def local(
    activations, qkv_weight, attn_weight, router_weight, gain_one, gain_two,
    expert_in, expert_out, segments, task_ids, task_experts, out_grad,
):
    packs, length, width = activations.shape
    planes = lax.axis_size("seq")
    groups = lax.axis_size("dp")
    cuts = 2 * packs
    assert cuts == planes == 4 and groups % 2 == 0
    piece = length // 2
    experts = router_weight.shape[1]
    hidden = expert_in.shape[0]
    assert experts + 2 <= TINY
    zeros = jnp.zeros((TINY - experts - 2, qkv_weight.shape[0]), LOW)
    tiny = jnp.concatenate([router_weight.T, gain_one[None], gain_two[None], zeros])
    tokens, grads, total, other, expert_grads, _, _, sel = layer(
        task_experts.T,
        activations.reshape(cuts, piece, width),
        segments,
        out_grad.reshape(cuts, piece, width),
        qkv_weight,
        attn_weight,
        tiny,
        task_ids,
        expert_in.reshape(hidden * experts, width),
        expert_out.reshape(hidden * experts, width),
        groups,
        planes,
        experts,
    )
    outputs, input_grad, qkv_grad, attn_grad, router_grad, first, second, win_grad, wout_grad = (
        deliver(
            sel,
            expert_grads,
            other.reshape(2, -1, width)[:, : hidden * experts],
            tokens,
            grads,
            total,
            experts,
        )
    )
    return (
        outputs.reshape(packs, length, width),
        input_grad.reshape(packs, length, width),
        qkv_grad,
        attn_grad,
        router_grad.T,
        first.reshape(-1),
        second.reshape(-1),
        win_grad.reshape(expert_in.shape),
        wout_grad.reshape(expert_in.shape),
    )


def solution(mesh):
    placed = (
        P("dp", "seq", None),
        P("dp", None),
        P("dp", None),
        P("dp", None),
        P("dp"),
        P("dp"),
        P(("dp", "seq"), None, None),
        P(("dp", "seq"), None, None),
        P("dp", "seq"),
        P("dp", "seq"),
        P(),
        P("dp", "seq", None),
    )
    return jax.shard_map(
        local,
        mesh=mesh,
        in_specs=placed,
        out_specs=(
            P("dp", "seq", None),
            P("dp", "seq", None),
            P("dp", None),
            P("dp", None),
            P("dp", None),
            P("dp"),
            P("dp"),
            P(("dp", "seq"), None, None),
            P(("dp", "seq"), None, None),
        ),
        check_vma=False,
    )
```

```python
import functools

import jax
import jax.numpy as jnp
from jax import lax
from jax.experimental import pallas as pl
from jax.experimental.pallas import tpu as pltpu
from jax.sharding import PartitionSpec as P

HEAD = 64
LANES = 128
SEG_COL = HEAD
LSE_COL = HEAD + 16
SEGMENTS = 16
FAR = 1e9
LARGE = 62 << 20
NT = (((1,), (1,)), ((), ()))
TN = (((0,), (0,)), ((), ()))
MESH = pl.DeviceIdType.MESH
EXPERTS_AT = LANES - 1
TINY = 16
F32 = jnp.float32
LOW = jnp.bfloat16


def dot(a, b):
    return jnp.dot(a, b, preferred_element_type=F32)


def dot_nt(a, b):
    return lax.dot_general(a, b, NT, preferred_element_type=F32)


def dot_tn(a, b):
    return lax.dot_general(a, b, TN, preferred_element_type=F32)


def thirds(values):
    high = values.astype(LOW).astype(F32)
    rest = values - high
    mid = rest.astype(LOW).astype(F32)
    return high, mid, rest - mid


def lanes_of(shape):
    return lax.broadcasted_iota(jnp.int32, shape, len(shape) - 1)


def put_thirds(base, values, column):
    lane = lanes_of(base.shape)
    high, mid, last = thirds(values)
    base = jnp.where(lane == column, high, base)
    base = jnp.where(lane == column + 1, mid, base)
    return jnp.where(lane == column + 2, last, base)


def normalize(values):
    center = values - jnp.mean(values, axis=-1, keepdims=True)
    inverse = lax.rsqrt(jnp.mean(center * center, axis=-1, keepdims=True) + 1e-05)
    return center * inverse, inverse


def norm_backward(upstream, scaled, inverse, gain_vec):
    direct = upstream * gain_vec
    return inverse * (
        direct
        - jnp.mean(direct, axis=-1, keepdims=True)
        - scaled * jnp.mean(direct * scaled, axis=-1, keepdims=True)
    )


def cost(micros):
    return pl.CostEstimate(flops=int(micros * 1e7), bytes_accessed=1 << 10, transcendentals=0)


def whole(*shape):
    return pl.BlockSpec(shape, lambda *_: (0,) * len(shape))


def remote(source, target, send, receive, device):
    return pltpu.make_async_remote_copy(
        src_ref=source,
        dst_ref=target,
        send_sem=send,
        recv_sem=receive,
        device_id=device,
        device_id_type=MESH,
    )


def each(count, body):
    def step(i, carry):
        body(i)
        return carry

    lax.fori_loop(0, count, step, 0)


def layer_kernel(
    groups, planes, experts, te, acts, seg, up_in, qkv_in, attn_in, tiny_in, task, win_in, wout_in,
    tokens_out, grads_out, total_out, other_got, ga_got, gb_got, far_w, sel_out,
    x, segx, up, res, stage, both, other, near_all, attn_all, tiny_all, small, sel, task_all, task_s,
    qa, ka, va, att, attf, normed, gates, slot, dv, send, got_a, got_b, out, dx, far_value, far_dx,
    far_gate, att_grad, att_send, attn_acc, router_acc, gain_acc, rest_part, rest_got, gb, key_t,
    dq_acc, qkv_acc, first_acc, qkv_part, qkv_got, part, heard, summed, sums,
    sem_x, sem_seg, sem_on, sem_seg_on, sem_up, sem_up_on, sem_near, sem_attn, sem_tiny, sem_task,
    sem_phase, sem_a, sem_b, sem_ga, sem_gb, sem_att, sem_far, sem_sums, sem_out, sem_att_back,
    sem_rest, sem_back, sem_qkv, sem_in, sem_part, sem_total, home, local,
):
    me = lax.axis_index("dp")
    place = lax.axis_index("seq")
    core = lax.rem(me, 2)
    base = me - core
    partner = (base + 1 - core, place)
    band = 2 * (place // 2)
    hub = 1 + place // 2
    at_hub = place == hub
    mine = me * 2 + lax.rem(place, 2)
    count = 2 * groups
    piece, width = x.shape[1], x.shape[2]
    tokens = 2 * planes * piece
    half = tokens // 2
    slots = send.shape[0]
    chunks, _, _, rows, _ = got_a.shape
    chunk_rows = rows * experts
    heads = qa.shape[0]
    pairs = heads // 2
    near_width = heads * HEAD
    near_cols = near_all.shape[2]
    dense_rows = tiny_all.shape[2]
    stays = (place // 2) == core
    spot = core + 2 * lax.rem(place, 2)
    kinds = range(3)
    used = [0]

    def copy_here(source, target):
        copy = pltpu.make_async_copy(source, target, local.at[used[0]])
        used[0] += 1
        return copy

    def rows_of(b, size):
        return pl.ds(pl.multiple_of(b * size, size), size)

    kind_rows = both.shape[0] // 2
    load_up = copy_here(up_in, res)
    load_both = [
        copy_here(source, both.at[pl.ds(kind * kind_rows, source.shape[0])])
        for kind, source in enumerate((win_in, wout_in))
    ]
    load_up.start()
    for copy in load_both:
        copy.start()
    greet_all(groups, planes)

    def goes(d):
        return jnp.logical_not(stays & (d == spot))

    def token_copies(piece_of, target, sem, sem_on):
        def give_piece(d):
            to = (base + lax.rem(d, 2), 2 * core + d // 2)
            return remote(piece_of(d), target.at[place], sem.at[0, d], sem.at[1, place], to)

        at_home = copy_here(piece_of(spot), target.at[place])

        def start():
            def one(d):
                @pl.when(goes(d))
                def _():
                    give_piece(d).start()

            each(planes, one)

            @pl.when(stays)
            def _():
                at_home.start()

        def onward(k):
            return remote(target.at[k], target.at[planes + k], sem_on.at[0, k], sem_on.at[1, k], partner)

        def receive(k):
            home = stays & (k == place)

            @pl.when(home)
            def _():
                at_home.wait()

            @pl.when(jnp.logical_not(home))
            def _():
                remote(piece_of(0), target.at[k], sem.at[0, 0], sem.at[1, k], partner).wait_recv()

            onward(k).start()

        def finish():
            def one(d):
                @pl.when(goes(d))
                def _():
                    give_piece(d).wait_send()

                onward(d).wait_send()

            each(planes, one)

        return start, receive, lambda k: onward(k).wait_recv(), finish

    def seg_piece(d):
        return seg.at[:, rows_of(lax.rem(d, 2), piece)]

    x_start, x_receive, x_far, x_finish = token_copies(lambda d: acts.at[d], x, sem_x, sem_on)
    seg_start, seg_receive, seg_far, seg_finish = token_copies(seg_piece, segx, sem_seg, sem_seg_on)
    up_start, up_receive, up_far, up_finish = token_copies(
        lambda d: stage.at[d], up, sem_up, sem_up_on
    )

    def way_back(source, target, sem):
        def give_piece(k):
            to = (base + place // 2, k)
            return remote(source.at[k], target.at[spot], sem.at[0, k], sem.at[1, spot], to)

        at_home = copy_here(source.at[place], target.at[spot])

        def start(k):
            home = stays & (k == place)

            @pl.when(jnp.logical_not(home))
            def _():
                give_piece(k).start()

            @pl.when(home)
            def _():
                at_home.start()

        def end(d):
            @pl.when(jnp.logical_not(stays & (d == place)))
            def _():
                give_piece(d).wait_send()

            @pl.when(goes(d))
            def _():
                remote(source.at[0], target.at[d], sem.at[0, 0], sem.at[1, d], partner).wait_recv()

            @pl.when(stays & (d == place))
            def _():
                at_home.wait()

        return start, lambda: each(planes, end)

    out_start, out_end = way_back(stage, tokens_out, sem_out)
    in_start, in_end = way_back(up, grads_out, sem_in)

    def others(body):
        each(groups - 1, lambda i: body(lax.rem(me + 1 + i, groups)))

    def give(source, target, sem, i):
        return remote(source, target.at[me], sem.at[0, i], sem.at[1, me], (i, place))

    def taken(source, target, sem, i):
        return remote(source, target.at[i], sem.at[0, i], sem.at[1, i], (i, place))

    def near_part(i, kind):
        at = 2 * kind * near_width + lax.rem(i, 2) * near_width
        return qkv_in.at[:, pl.ds(pl.multiple_of(at, near_width), near_width)]

    def near_copy(i, kind, to, of):
        return remote(
            near_part(to, kind),
            near_all.at[of, :, pl.ds(kind * near_width, near_width)],
            sem_near.at[0, i, kind],
            sem_near.at[1, of, kind],
            (i, place),
        )

    def part_of(kind, c):
        at = kind * kind_rows + c * chunk_rows
        return pl.ds(at if isinstance(c, int) else pl.multiple_of(at, chunk_rows), chunk_rows)

    def phase_copy(kind, c):
        r = rows_of(c, chunk_rows)
        return remote(
            (win_in, wout_in)[kind].at[r],
            far_w.at[lax.rem(place, 2), kind, r],
            sem_phase.at[0, 0, kind, c],
            sem_phase.at[1, lax.rem(place, 2), kind, c],
            (me, 3 - hub),
        )

    def phase_got(b, kind, c):
        r = rows_of(c, chunk_rows)
        return remote(
            (win_in, wout_in)[kind].at[r],
            far_w.at[b, kind, r],
            sem_phase.at[0, 0, kind, c],
            sem_phase.at[1, b, kind, c],
            (me, 2 - band + b),
        )

    def ring(c, b):
        at = lax.rem(2 * c + b, 4) * 2 * chunk_rows
        return at if isinstance(at, int) else pl.multiple_of(at, chunk_rows)

    def sums_copy(kind, c, b):
        r = pl.ds(ring(c, b) + kind * chunk_rows, chunk_rows)
        return remote(
            sums.at[r],
            other_got.at[part_of(kind, c)],
            sem_sums.at[0, b, kind, c],
            sem_sums.at[1, 0, kind, c],
            (me, 2 - band + b),
        )

    def sums_got(kind, c):
        r = part_of(kind, c)
        return remote(
            sums.at[pl.ds(0, chunk_rows)],
            other_got.at[r],
            sem_sums.at[0, 0, kind, c],
            sem_sums.at[1, 0, kind, c],
            (me, 3 - hub),
        )

    def band_device(m):
        return (m // 2, band + lax.rem(m, 2))

    def band_copies(source, target, sem, home_sem):
        def give_part(c, m):
            to = band_device(m)
            return remote(source(c, m), target(c, mine), sem.at[c, 0, m], sem.at[c, 1, mine], to)

        def at_home(c):
            return pltpu.make_async_copy(source(c, mine), target(c, mine), home_sem.at[c])

        def run(body):
            each(count - 1, lambda i: body(lax.rem(mine + 1 + i, count)))

        def start(c):
            run(lambda m: give_part(c, m).start())
            at_home(c).start()

        def sent(c):
            run(lambda m: give_part(c, m).wait_send())

        def received(c):
            run(
                lambda m: remote(
                    source(c, m), target(c, m), sem.at[c, 0, m], sem.at[c, 1, m], band_device(m)
                ).wait_recv()
            )
            at_home(c).wait()

        return start, sent, received

    def by_chunk(source, target, sem, home_sem):
        return band_copies(
            lambda c, m: source.at[c, m], lambda c, m: target.at[c, m], sem, home_sem
        )

    a_start, a_sent, a_received = band_copies(
        lambda c, m: send.at[pl.ds(0, chunks), m], lambda c, m: got_a.at[:, m], sem_a, home.at[3]
    )
    ga_start, ga_sent, ga_received = by_chunk(got_a, ga_got, sem_ga, home.at[0])

    def far_rows(dp):
        return pl.ds(2 * dp, 2)

    def b_slots(c):
        return pl.ds(lax.rem(2 * c, slots), 2)

    def b_part(c, m):
        return remote(
            send.at[b_slots(c), m],
            got_b.at[c, far_rows(me)],
            sem_b.at[c, 0, m],
            sem_b.at[c, 1, me],
            band_device(m),
        )

    def b_home(c):
        return pltpu.make_async_copy(
            send.at[b_slots(c), mine], got_b.at[c, far_rows(me)], home.at[1, c]
        )

    def others_of_band(body):
        each(count - 1, lambda i: body(lax.rem(mine + 1 + i, count)))

    def b_start(c):
        b_home(c).start()
        others_of_band(lambda m: b_part(c, m).start())
        b_home(c).wait()

    def b_sent(c):
        others_of_band(lambda m: b_part(c, m).wait_send())

    def b_received(c):
        def one(dp):
            @pl.when(jnp.logical_not(at_hub & (dp == me)))
            def _():
                remote(
                    send.at[pl.ds(0, 2), 0],
                    got_b.at[c, far_rows(dp)],
                    sem_b.at[c, 0, dp],
                    sem_b.at[c, 1, dp],
                    (dp, hub),
                ).wait_recv()

        each(groups, one)

    def gb_part(c, dp):
        return remote(
            got_b.at[c, far_rows(dp)],
            gb_got.at[c, :, :, rows_of(mine, rows)],
            sem_gb.at[c, 0, dp],
            sem_gb.at[c, 1, mine],
            (dp, hub),
        )

    def gb_home(c):
        target = gb_got.at[c, :, :, rows_of(mine, rows)]
        return pltpu.make_async_copy(got_b.at[c, far_rows(me)], target, home.at[2, c])

    def gb_each(body):
        def one(j):
            dp = lax.rem(me + 1 + j, groups)

            @pl.when(jnp.logical_not(at_hub & (dp == me)))
            def _():
                body(dp)

        each(groups, one)

    def gb_start(c):
        gb_each(lambda dp: gb_part(c, dp).start())

        @pl.when(at_hub)
        def _():
            gb_home(c).start()

    def gb_sent(c):
        gb_each(lambda dp: gb_part(c, dp).wait_send())

    def gb_received(c):
        others_of_band(
            lambda m: remote(
                got_b.at[c, pl.ds(0, 2)],
                gb_got.at[c, :, :, rows_of(m, rows)],
                sem_gb.at[c, 0, 0],
                sem_gb.at[c, 1, m],
                band_device(m),
            ).wait_recv()
        )
        gb_home(c).wait()

    def staged(b, kind, size):
        at = (2 * b + kind) * size
        return pl.ds(at if 4 * size <= other.shape[0] else 0, size)

    def load_gb(c, b, kind):
        target = other.at[staged(b, kind, count * rows)]
        return pltpu.make_async_copy(gb_got.at[c, b, kind], target, home.at[5 + b, kind])

    x_start()
    seg_start()
    task_part = task.at[:, pl.ds(0, LANES)]
    others(lambda i: give(task_part, task_all, sem_task, i).start())
    others(lambda i: give(tiny_in, tiny_all, sem_tiny, i).start())

    def start_near(i):
        for kind in kinds:
            near_copy(i, kind, i, me).start()

    others(start_near)
    own_task = copy_here(task_part, task_all.at[me])
    own_dense = [
        copy_here(tiny_in, tiny_all.at[me]),
        copy_here(attn_in, attn_all.at[me]),
    ] + [
        copy_here(near_part(me, kind), near_all.at[me, :, pl.ds(kind * near_width, near_width)])
        for kind in kinds
    ]
    for copy in [own_task] + own_dense:
        copy.start()
    load_up.wait()
    stage[...] = res[...].astype(LOW)
    others(lambda i: taken(task_part, task_all, sem_task, i).wait_recv())
    own_task.wait()
    to_scalars = copy_here(task_all, task_s)
    to_scalars.start()
    to_scalars.wait()

    def expert_of(dp, z):
        at = z // 2 + dp - lax.rem(dp, 2)
        return te[lax.rem(dp, 2), task_s[at, lax.rem(z, 2), 0]]

    mine_id = expert_of(me, place)
    other_id = expert_of(partner[0], place)

    sel_row = lax.broadcasted_iota(jnp.int32, (rows, chunk_rows), 0)
    sel_col = lax.broadcasted_iota(jnp.int32, (rows, chunk_rows), 1)

    def fill_sel(m):
        dp, z = band_device(m)
        hit = sel_col == sel_row * experts + expert_of(dp, z)
        sel[m] = jnp.where(hit, 1.0, 0.0).astype(LOW)

    each(count, fill_sel)
    save_sel = copy_here(sel, sel_out)
    save_sel.start()

    def choose(source, target):
        choice = sel[...].reshape(count * rows, chunk_rows)
        for kind in range(2):
            values = dot(choice, source(kind))
            target[:, kind] = values.astype(LOW).reshape(count, rows, width)

    for copy in load_both:
        copy.wait()
    each(chunks, lambda c: choose(lambda kind: both[part_of(kind, c), :], send.at[c]))

    def end_near(i):
        for kind in kinds:
            near_copy(i, kind, i, i).wait_recv()

    others(end_near)
    others(lambda i: taken(tiny_in, tiny_all, sem_tiny, i).wait_recv())
    for copy in own_dense:
        copy.wait()
    eye = lax.broadcasted_iota(jnp.int32, (TINY, LANES), 0) == lanes_of((TINY, LANES))
    eye = jnp.where(eye, 1.0, 0.0).astype(LOW)

    def turn(i):
        small[rows_of(i, dense_rows), :] = dot_tn(tiny_all[i], eye)

    each(groups, turn)

    turned = small[...].T
    first_gain = turned[experts : experts + 1]
    second_gain = turned[experts + 1 : experts + 2]
    lane = lanes_of((piece, LANES))

    def project(k):
        scaled, _ = normalize(x[k].astype(F32))
        low = (scaled * first_gain).astype(LOW)
        values = dot(low, near_all[...].reshape(width, near_cols))
        segment = segx[k, pl.ds(lax.rem(place, 2), 1)].astype(F32)
        segment = jnp.broadcast_to(segment, (LANES, piece)).T
        same = (lane - SEG_COL).astype(F32) == segment
        in_seg = (lane >= SEG_COL) & (lane < SEG_COL + SEGMENTS)
        q_more = jnp.where(same, 1.0, 0.0)
        k_more = jnp.where(in_seg & jnp.logical_not(same), -FAR, 0.0)
        k_more = jnp.where((lane >= LSE_COL) & (lane < LSE_COL + 3), 1.0, k_more)
        v_more = jnp.where((lane >= HEAD) & (lane < HEAD + 3), 1.0, 0.0)
        r = rows_of(k, piece)

        def head(kind, h, more):
            at = kind * near_width + h // 2 * LANES
            values_of = values[:, at : at + LANES]
            if h % 2:
                values_of = pltpu.roll(values_of, HEAD, 1)
            return jnp.where(lane < HEAD, values_of, more)

        for h in range(heads):
            query = head(0, h, 0.0).astype(LOW).astype(F32) * HEAD**-0.5
            qa[h, r, :] = (query + q_more).astype(LOW)
            ka[h, r, :] = head(1, h, k_more).astype(LOW)
            va[h, r, :] = head(2, h, v_more).astype(LOW)

    def by_distance(k):
        return lax.bitwise_xor(place, jnp.int32(k))

    def arrive(k):
        x_receive(k)
        seg_receive(k)

    def start_phase(c):
        for kind in range(2):
            phase_copy(kind, c).start()

    def far_piece(k):
        x_far(k)
        seg_far(k)
        project(planes + k)

    near_order = [by_distance(k) for k in range(planes)]
    arrive(near_order[0])
    project(near_order[0])
    arrive(near_order[1])
    project(near_order[1])
    far_piece(near_order[0])
    for k in near_order[2:]:
        arrive(k)
    up_start()
    a_start(0)
    for c in range(min(2, chunks)):
        start_phase(c)
    others(lambda i: give(attn_in, attn_all, sem_attn, i).start())
    far_piece(near_order[1])
    for k in near_order[2:]:
        project(k)
    for k in near_order[2:]:
        far_piece(k)

    block = min(512, half)

    def att_copy(p):
        return remote(att.at[p], attf.at[p], sem_att.at[0, p], sem_att.at[1, p], partner)

    for p in range(pairs):

        def attend(i):
            r = rows_of(i, block)
            parts = []
            for h in (2 * p, 2 * p + 1):
                query = qa[h, r, :]
                scores = dot_nt(query, ka[h])
                top = jnp.max(scores, axis=1, keepdims=True)
                probs = jnp.exp(scores - top).astype(LOW)
                mixed = dot(probs, va[h])
                total = mixed[:, HEAD : HEAD + 1]
                parts.append(mixed[:, :HEAD] / total)
                lse = top + jnp.log(total)
                qa[h, r, :] = put_thirds(query.astype(F32), -lse, LSE_COL).astype(LOW)
            att[p, r, :] = jnp.concatenate(parts, axis=1).astype(LOW)

        each(tokens // block, attend)
        att_copy(p).start()
        if p == 0:
            for c in range(2, chunks):
                start_phase(c)

    def other_weights(c):
        @pl.when(at_hub)
        def _():
            loads = []
            for b in range(2):
                for kind in range(2):
                    phase_got(b, kind, c).wait_recv()
                    source = far_w.at[b, kind, rows_of(c, chunk_rows)]
                    target = other.at[staged(b, kind, chunk_rows)]
                    loads.append(pltpu.make_async_copy(source, target, home.at[7 + b, kind]))
                    loads[-1].start()

            @pl.when(2 * c >= slots)
            def _():
                b_sent(c - slots // 2)

            for b in range(2):
                for kind in range(2):
                    loads[2 * b + kind].wait()
                choose(
                    lambda kind: other[staged(b, kind, chunk_rows), :],
                    send.at[lax.rem(2 * c, slots) + b],
                )
            b_start(c)

    for k in range(planes):
        up_receive(by_distance(k))
    for p in range(pairs):
        att_copy(p).wait_recv()
    others(lambda i: taken(attn_in, attn_all, sem_attn, i).wait_recv())

    def weight_rows(which):
        values = attn_all[pl.ds(which * (groups // 2), groups // 2)]
        return values.reshape(width // 2, width)

    def middle(b):
        @pl.when(b >= planes)
        def _():
            up_far(b - planes)

        r = rows_of(b, piece)
        f = rows_of(lax.rem(b + planes, 2 * planes), piece)
        residual = x[b].astype(F32)
        near_att = jnp.concatenate([att[p, r, :] for p in range(pairs)], axis=1)
        far_att = jnp.concatenate([attf[p, f, :] for p in range(pairs)], axis=1)
        residual += dot(near_att, weight_rows(core)) + dot(far_att, weight_rows(1 - core))

        @pl.when(b < planes)
        def _():
            res[b] = residual

        scaled, _ = normalize(residual)
        low = (scaled * second_gain).astype(LOW)
        normed[r, :] = low
        logits = dot(low, small[...].astype(LOW))
        of_mine = jnp.sum(jnp.where(lane == mine_id, logits, 0.0), axis=1, keepdims=True)
        of_other = jnp.sum(jnp.where(lane == other_id, logits, 0.0), axis=1, keepdims=True)
        top = jnp.maximum(of_mine, of_other)
        of_mine = jnp.exp(of_mine - top)
        of_other = jnp.exp(of_other - top)
        total = of_mine + of_other
        gate = of_mine / total
        gates[r, :] = jnp.where(lane == 0, gate, jnp.where(lane == 1, of_other / total, 0.0))
        slot[r, :] = (gate * up[b].astype(F32)).astype(LOW)

    each(2 * planes, middle)

    def add_up_others(c):
        @pl.when(at_hub)
        def _():
            together = 4 * count * rows <= other.shape[0]
            choice = sel[...].reshape(count * rows, chunk_rows)
            gb_received(c)
            if together:
                for b in range(2):
                    for kind in range(2):
                        load_gb(c, b, kind).start()
            for b in range(2):

                @pl.when(2 * c + b >= 4)
                def _():
                    for kind in range(2):
                        sums_copy(kind, c - 2, b).wait_send()

                for kind in range(2):
                    if not together:
                        load_gb(c, b, kind).start()
                    load_gb(c, b, kind).wait()
                    r = pl.ds(ring(c, b) + kind * chunk_rows, chunk_rows)
                    values = other[staged(b, kind, count * rows), :]
                    sums[r, :] = dot_tn(choice, values).astype(LOW)
                    sums_copy(kind, c, b).start()

    out[...] = jnp.zeros_like(out)
    dx[...] = jnp.zeros_like(dx)
    per = max(1, 256 // rows)

    def expert(weights, c):
        def tile(t):
            at = pl.ds(t * per, per)
            win = weights[c, at, 0].reshape(per * rows, width)
            wout = weights[c, at, 1].reshape(per * rows, width)
            pre = dot_nt(normed[...], win)
            hidden_grad = dot_nt(slot[...], wout)
            cdf = 0.5 * (1.0 + lax.erf(pre * 0.7071067811865476))
            slope = cdf + pre * jnp.exp(-0.5 * pre * pre) * 0.3989422804014327
            hidden = (pre * cdf).astype(LOW)
            pre_grad = (hidden_grad * slope).astype(LOW)
            out[...] += dot(hidden, wout)
            dx[...] += dot(pre_grad, win)
            weights[c, at, 0] = dot_tn(pre_grad, normed[...]).astype(LOW).reshape(per, rows, width)
            weights[c, at, 1] = dot_tn(hidden, slot[...]).astype(LOW).reshape(per, rows, width)

        each(count // per, tile)

    a_sent(0)
    a_received(0)
    other_weights(0)

    def step_of(j):
        @pl.when(j < chunks)
        def _():
            expert(got_a, j)

        @pl.when(j + 1 < chunks)
        def _():
            other_weights(j + 1)

        @pl.when(j > 0)
        def _():
            b_received(j - 1)
            expert(got_b, j - 1)
            gb_start(j - 1)

        if chunks > 1:

            @pl.when(j == chunks)
            def _():
                add_up_others(0)

    each(chunks + 1, step_of)

    @pl.when(at_hub)
    def _():
        for c in range(chunks - slots // 2, chunks):
            b_sent(c)

    step = half // 2
    step_lane = lanes_of((step, LANES))
    for at in range(0, tokens, step):
        r = pl.ds(at, step)
        value = out[r, :]
        upstream = up[pl.ds(at // piece, step // piece)].reshape(step, width).astype(F32)
        gate_grad = jnp.sum(value * upstream, axis=1, keepdims=True)
        value = value * gates[r, 0:1]
        if at < half:
            out[r, :] = value
            gates[r, :] = jnp.where(step_lane == 2, gate_grad, gates[r, :])
        else:
            t = pl.ds(at - half, step)
            other[t, :] = value.astype(LOW)
            both[t, :] = dx[r, :].astype(LOW)
            gates[r, :] = jnp.broadcast_to(gate_grad, (step, LANES))
    far_copies = [
        remote(other.at[pl.ds(0, half)], far_value, sem_far.at[0, 0], sem_far.at[1, 0], partner),
        remote(both.at[pl.ds(0, half)], far_dx, sem_far.at[0, 1], sem_far.at[1, 1], partner),
        remote(gates.at[pl.ds(half, half)], far_gate, sem_far.at[0, 2], sem_far.at[1, 2], partner),
    ]
    for copy in far_copies:
        copy.start()
    up_finish()
    res_grad = out.at[pl.ds(half, half)]
    attn_acc[...] = jnp.zeros_like(attn_acc)
    router_acc[...] = jnp.zeros_like(router_acc)
    gain_acc[...] = jnp.zeros_like(gain_acc)
    for copy in far_copies:
        copy.wait()
    if chunks > 1:
        add_up_others(1)


    def post(b):
        r = rows_of(b, piece)
        residual = res[b]
        upstream = up[b].astype(F32)
        stage[b] = (residual + out[r, :] + far_value[r, :].astype(F32)).astype(LOW)
        out_start(b)
        gate = gates[r, :]
        gate_mine, gate_other, grad_mine = gate[:, 0:1], gate[:, 1:2], gate[:, 2:3]
        grad_other = far_gate[r, 0:1]
        mean = gate_mine * grad_mine + gate_other * grad_other
        logit_grad = jnp.where(lane == mine_id, gate_mine * (grad_mine - mean), 0.0)
        logit_grad += jnp.where(lane == other_id, gate_other * (grad_other - mean), 0.0)
        normed_grad = dx[r, :] + far_dx[r, :].astype(F32)
        router = small[...].astype(LOW)
        for third in thirds(logit_grad):
            third = third.astype(LOW)
            router_acc[...] += dot_tn(normed[r, :], third)
            normed_grad += dot_nt(third, router)
        scaled, inverse = normalize(residual)
        gain_acc[...] += jnp.sum(normed_grad * scaled, axis=0, keepdims=True)
        residual_grad = upstream + norm_backward(normed_grad, scaled, inverse, second_gain)
        res_grad[r, :] = residual_grad
        low = residual_grad.astype(LOW)
        f = pl.ds(pl.multiple_of(half + b * piece, piece), piece)
        both_att = [att[p, r, :] for p in range(pairs)] + [attf[p, f, :] for p in range(pairs)]
        for i, values in enumerate(both_att):
            attn_acc[i * LANES : (i + 1) * LANES] += dot_tn(values, low)
        near_back = dot_nt(low, weight_rows(core)).astype(LOW)
        far_back = dot_nt(low, weight_rows(1 - core)).astype(LOW)
        for p in range(pairs):
            att_grad[p, r, :] = near_back[:, p * LANES : (p + 1) * LANES]
            att_send[p, r, :] = far_back[:, p * LANES : (p + 1) * LANES]

    each(planes, post)

    def att_back_copy(p):
        target = att_grad.at[p, pl.ds(half, half)]
        return remote(att_send.at[p], target, sem_att_back.at[0, p], sem_att_back.at[1, p], partner)

    for p in range(pairs):
        att_back_copy(p).start()
    own_rows = near_width // dense_rows
    turned = jnp.broadcast_to(gain_acc[...], (LANES, width)).T
    tail = jnp.where(lanes_of(turned.shape) == EXPERTS_AT, turned, router_acc[...]).astype(LOW)
    rest_part[:, :, width:] = tail.reshape(groups, dense_rows, LANES)
    for side in range(2):
        values = attn_acc[side * near_width : (side + 1) * near_width].astype(LOW)
        at = core if side == 0 else 1 - core
        rest_part[pl.ds(at * own_rows, own_rows), :, :width] = values.reshape(
            own_rows, dense_rows, width
        )

    def rest_copy(i):
        return give(rest_part.at[i], rest_got, sem_rest, i)

    others(lambda i: rest_copy(i).start())

    for c in range(2, chunks - 1):
        add_up_others(c)

    each(chunks, ga_start)

    all_lane = lanes_of((tokens, LANES))
    for p in range(pairs):
        att_back_copy(p).wait_recv()
        halves = []
        for side in range(2):
            h = 2 * p + side
            pair_grad = att_grad[p].astype(F32)
            inner = pair_grad * att[p].astype(F32)
            if side == 1:
                pair_grad = pltpu.roll(pair_grad, HEAD, 1)
                inner = pltpu.roll(inner, HEAD, 1)
            delta = jnp.sum(jnp.where(all_lane < HEAD, inner, 0.0), axis=1, keepdims=True)
            pair_grad = jnp.where(all_lane < HEAD, pair_grad, 0.0)
            gb[...] = put_thirds(pair_grad, -delta, HEAD).astype(LOW)
            key_t[...] = ka[h].T[:HEAD]
            dq_acc[...] = jnp.zeros_like(dq_acc)
            dk_cols = pl.ds((pairs + p) * LANES + side * HEAD, HEAD)
            dv_cols = pl.ds(p * LANES + side * HEAD, HEAD)

            def keys(i):
                r = rows_of(i, block)
                weights = jnp.exp(dot_nt(ka[h, r, :], qa[h]))
                centered = dot_nt(va[h, r, :], gb[...])
                score_grad = (weights * centered).astype(LOW)
                dv[r, dv_cols] = dot(weights.astype(LOW), gb[...])[:, :HEAD].astype(LOW)
                slot[r, dk_cols] = dot(score_grad, qa[h])[:, :HEAD].astype(LOW)
                dq_acc[...] += dot(key_t[:, r], score_grad)

            each(tokens // block, keys)
            halves.append(dq_acc[...].T * HEAD**-0.5)
            if h == 0:
                add_up_others(chunks - 1)
        slot[:, p * LANES : (p + 1) * LANES] = jnp.concatenate(halves, axis=1).astype(LOW)

    qkv_acc[...] = jnp.zeros_like(qkv_acc)
    first_acc[...] = jnp.zeros_like(first_acc)
    back_near = dx.at[pl.ds(half, half)]
    back_send = normed.at[pl.ds(0, half)]
    back_got = normed.at[pl.ds(half, half)]

    def project_back(b):
        r = rows_of(b, piece)
        values = jnp.concatenate([slot[r, :], dv[r, :]], axis=1)
        scaled, _ = normalize(x[b].astype(F32))
        back = dot_nt(values, near_all[...].reshape(width, near_cols))
        qkv_acc[...] += dot_tn((scaled * first_gain).astype(LOW), values)
        first_acc[...] += jnp.sum(back * scaled, axis=0, keepdims=True)
        return back

    def far_block(i):
        back_send[rows_of(i, piece), :] = project_back(planes + i).astype(LOW)

    def near_block(i):
        back_near[rows_of(i, piece), :] = project_back(i)

    each(planes, far_block)
    back_copy = remote(back_send, back_got, sem_back.at[0], sem_back.at[1], partner)
    back_copy.start()
    each(planes, near_block)
    qkv_part[:, :, :near_cols] = qkv_acc[...].astype(LOW).reshape(groups, dense_rows, near_cols)
    turned = jnp.broadcast_to(first_acc[...], (LANES, width)).T.astype(LOW)
    qkv_part[:, :, near_cols:] = turned.reshape(groups, dense_rows, LANES)

    def qkv_copy(i):
        return give(qkv_part.at[i], qkv_got, sem_qkv, i)

    others(lambda i: qkv_copy(i).start())

    back_copy.wait_recv()

    def finish(b):
        r = rows_of(b, piece)
        scaled, inverse = normalize(x[b].astype(F32))
        grad = back_near[r, :] + back_got[r, :].astype(F32)
        first = norm_backward(grad, scaled, inverse, first_gain)
        up[b] = (res_grad[r, :] + first).astype(LOW)
        in_start(b)

    each(planes, finish)

    others(lambda i: taken(rest_part.at[i], rest_got, sem_rest, i).wait_recv())
    others(lambda i: taken(qkv_part.at[i], qkv_got, sem_qkv, i).wait_recv())

    def from_group(mine_part, got, i):
        return jnp.where(i == me, mine_part[i], got[i]).astype(F32)

    def add(j, sums_of):
        first, second, rest = sums_of
        first += from_group(qkv_part, qkv_got, 2 * j)
        second += from_group(qkv_part, qkv_got, 2 * j + 1)
        rest += from_group(rest_part, rest_got, 2 * j)
        rest += from_group(rest_part, rest_got, 2 * j + 1)
        return first, second, rest

    zero = jnp.zeros(qkv_part.shape[1:], F32)
    first, second, rest = lax.fori_loop(
        0, groups // 2, add, (zero, zero, jnp.zeros(rest_part.shape[1:], F32))
    )
    columns = []
    for kind in kinds:
        for side in (first, second):
            columns.append(side[:, kind * near_width : (kind + 1) * near_width])
    columns += [rest, first[:, near_cols:] + second[:, near_cols:]]
    share = jnp.concatenate(columns, axis=1).astype(LOW)
    cut = dense_rows // planes
    for z in range(planes):
        part[z] = share[z * cut : (z + 1) * cut]

    def over_planes(body):
        each(planes - 1, lambda i: body(lax.rem(place + 1 + i, planes)))

    def tell_part(z):
        return remote(part.at[z], heard.at[place], sem_part.at[0, z], sem_part.at[1, place], (me, z))

    def hear_part(z):
        return remote(part.at[z], heard.at[z], sem_part.at[0, z], sem_part.at[1, z], (me, z))

    def tell_sum(z):
        target = total_out.at[place]
        return remote(summed, target, sem_total.at[0, z], sem_total.at[1, place], (me, z))

    def hear_sum(z):
        return remote(summed, total_out.at[z], sem_total.at[0, z], sem_total.at[1, z], (me, z))

    over_planes(lambda z: tell_part(z).start())
    over_planes(lambda z: hear_part(z).wait_recv())
    sum_of = part[place].astype(F32)
    for k in range(1, planes):
        sum_of += heard[lax.rem(place + k, planes)].astype(F32)
    summed[...] = sum_of.astype(LOW)
    over_planes(lambda z: tell_sum(z).start())
    put = copy_here(summed, total_out.at[place])
    put.start()

    x_finish()
    seg_finish()

    def end_dense(i):
        give(task_part, task_all, sem_task, i).wait_send()
        give(tiny_in, tiny_all, sem_tiny, i).wait_send()
        give(attn_in, attn_all, sem_attn, i).wait_send()
        for kind in kinds:
            near_copy(i, kind, i, me).wait_send()
        rest_copy(i).wait_send()
        qkv_copy(i).wait_send()

    others(end_dense)
    save_sel.wait()
    for p in range(pairs):
        att_copy(p).wait_send()
        att_back_copy(p).wait_send()
    back_copy.wait_send()
    for c in range(chunks):
        ga_sent(c)
        ga_received(c)
        gb_sent(c)
        for kind in range(2):
            phase_copy(kind, c).wait_send()
            sums_got(kind, c).wait_recv()

    @pl.when(at_hub)
    def _():
        for k in range(max(0, 2 * chunks - 4), 2 * chunks):
            for kind in range(2):
                sums_copy(kind, k // 2, k % 2).wait_send()

    over_planes(lambda z: tell_part(z).wait_send())
    over_planes(lambda z: tell_sum(z).wait_send())
    over_planes(lambda z: hear_sum(z).wait_recv())
    put.wait()
    out_end()
    in_end()


def greet_all(groups, planes):
    me = lax.axis_index("dp")
    place = lax.axis_index("seq")
    base = me - lax.rem(me, 2)
    band = 2 * (place // 2)
    mine = me * 2 + lax.rem(place, 2)
    barrier = pltpu.get_barrier_semaphore()

    def signal(dp, z):
        pl.semaphore_signal(barrier, inc=1, device_id=(dp, z), device_id_type=MESH)

    def near_planes(i):
        m = lax.rem(mine + 1 + i, 2 * groups)
        signal(m // 2, band + lax.rem(m, 2))

    each(2 * groups - 1, near_planes)
    each(4, lambda i: signal(base + i // 2, 2 - band + lax.rem(i, 2)))
    pl.semaphore_wait(barrier, 2 * groups + 3)


def layer(te, acts, seg, up_in, qkv, attn, tiny, task, win, wout, groups, planes, experts):
    _, piece, width = acts.shape
    half = planes * piece
    tokens = 2 * half
    heads = width // HEAD // 2
    pairs = heads // 2
    hidden = win.shape[0] // experts
    chunks = 4 if hidden % 64 == 0 else 1
    rows = hidden // chunks
    count = 2 * groups
    dense_rows = qkv.shape[0]
    near_cols = 3 * heads * HEAD
    anywhere = pl.BlockSpec(memory_space=pl.ANY)
    dma = pltpu.SemaphoreType.DMA
    S = lambda shape, t=LOW: jax.ShapeDtypeStruct(shape, t)
    V = lambda shape, t=LOW: pltpu.VMEM(shape, t)
    pieces = (planes, piece, width)
    head_shape = (heads, tokens, LANES)
    pair_shape = (pairs, tokens, LANES)
    band_shape = (chunks, count, 2, rows, width)
    both_shape = (max(half, 2 * win.shape[0]), width)
    sel_shape = (count, rows, rows * experts)
    rest_shape = (groups, dense_rows, width + LANES)
    qkv_shape = (groups, dense_rows, near_cols + LANES)
    total = (planes, dense_rows // planes, 4 * width + 2 * LANES)
    return pl.pallas_call(
        functools.partial(layer_kernel, groups, planes, experts),
        in_specs=[pl.BlockSpec(memory_space=pltpu.SMEM)] + [anywhere] * 9,
        out_specs=[anywhere] * 8,
        out_shape=[
            S(pieces),
            S(pieces),
            S(total),
            S(both_shape),
            S(band_shape),
            S((chunks, 2, 2, count * rows, width)),
            S((2, 2) + win.shape),
            S(sel_shape),
        ],
        scratch_shapes=[
            V((2 * planes, piece, width)),
            V((2 * planes, 2, piece), jnp.int32),
            V((2 * planes, piece, width)),
            V(pieces, F32),
            V(pieces),
            V(both_shape),
            V(both_shape),
            V((groups, dense_rows, near_cols)),
            V((groups, dense_rows, width)),
            V((groups,) + tiny.shape),
            V((width, LANES), F32),
            V(sel_shape),
            V((groups, 2, LANES), jnp.int32),
            pltpu.SMEM((groups, 2, LANES), jnp.int32),
            V(head_shape),
            V(head_shape),
            V(head_shape),
            V(pair_shape),
            V(pair_shape),
            V((tokens, width)),
            V((tokens, LANES), F32),
            V((tokens, width)),
            V((tokens, heads * HEAD)),
            V((max(2, chunks),) + band_shape[1:]),
            V(band_shape),
            V(band_shape),
            V((tokens, width), F32),
            V((tokens, width), F32),
            V((half, width)),
            V((half, width)),
            V((half, LANES), F32),
            V(pair_shape),
            V((pairs, half, LANES)),
            V((width, width), F32),
            V((width, LANES), F32),
            V((1, width), F32),
            V(rest_shape),
            V(rest_shape),
            V((tokens, LANES)),
            V((HEAD, tokens)),
            V((HEAD, tokens), F32),
            V((width, near_cols), F32),
            V((1, width), F32),
            V(qkv_shape),
            V(qkv_shape),
            V(total),
            V(total),
            V(total[1:]),
            V(both_shape),
        ]
        + [dma((2, planes))] * 6
        + [dma((2, groups, 3))]
        + [dma((2, groups))] * 3
        + [dma((2, 2, 2, chunks)), dma((1, 2, count))]
        + [dma((chunks, 2, count))] * 3
        + [dma((2, pairs)), dma((2, 3)), dma((2, 2, 2, chunks)), dma((2, planes)), dma((2, pairs))]
        + [dma((2, groups)), dma((2,)), dma((2, groups))]
        + [dma((2, planes))] * 3
        + [dma((9, max(2, chunks))), dma((32,))],
        compiler_params=pltpu.CompilerParams(
            collective_id=0, has_side_effects=True, vmem_limit_bytes=LARGE
        ),
        cost_estimate=cost(250),
        name="layer",
    )(te, acts, seg, up_in, qkv, attn, tiny, task, win, wout)


def deliver_kernel(
    sel, ga, other, tokens, grads, total,
    outputs, input_grad, qkv_grad, attn_grad, router_grad, first, second, win_grad, wout_grad,
):
    outputs[...] = tokens[...]
    input_grad[...] = grads[...].astype(F32)
    count, rows, columns = sel.shape
    width = ga.shape[4]
    choice = sel[...].reshape(count * rows, columns)
    for kind, grad in ((0, win_grad), (1, wout_grad)):
        for c in range(ga.shape[0]):
            r = slice(c * columns, (c + 1) * columns)
            values = dot_tn(choice, ga[c, :, kind].reshape(count * rows, width))
            grad[r] = values + other[kind, r].astype(F32)

    @pl.when(pl.program_id(0) == 0)
    def _():
        planes, cut, _ = total.shape
        for z in range(planes):
            r = slice(z * cut, (z + 1) * cut)
            values = total[z].astype(F32)
            qkv_grad[r] = values[:, : 3 * width]
            attn_grad[r] = values[:, 3 * width : 4 * width]
        small = jnp.concatenate([total[z, :, 4 * width :].astype(F32) for z in range(planes)])
        turned = small[:, :LANES].T
        router_grad[...] = turned[: router_grad.shape[0]]
        second[...] = turned[EXPERTS_AT : EXPERTS_AT + 1]
        first[...] = small[:, LANES:].T[0:1]


def deliver(sel, ga, other, tokens, grads, total, experts):
    chunks = ga.shape[0]
    steps = min(2, chunks)
    per = chunks // steps
    planes, piece, width = tokens.shape
    dense_rows = total.shape[0] * total.shape[1]
    part = pl.BlockSpec((planes // steps, piece, width), lambda i: (i, 0, 0))
    rows = other.shape[1] // steps
    grad = pl.BlockSpec((rows, width), lambda i: (i, 0))
    S = lambda shape, t=F32: jax.ShapeDtypeStruct(shape, t)
    return pl.pallas_call(
        deliver_kernel,
        grid=(steps,),
        in_specs=[
            whole(*sel.shape),
            pl.BlockSpec((per,) + ga.shape[1:], lambda i: (i, 0, 0, 0, 0)),
            pl.BlockSpec((2, rows, width), lambda i: (0, i, 0)),
            part,
            part,
            whole(*total.shape),
        ],
        out_specs=[
            part,
            part,
            whole(dense_rows, 3 * width),
            whole(dense_rows, width),
            whole(experts, dense_rows),
            whole(1, dense_rows),
            whole(1, dense_rows),
            grad,
            grad,
        ],
        out_shape=[
            S(tokens.shape, LOW),
            S(tokens.shape),
            S((dense_rows, 3 * width)),
            S((dense_rows, width)),
            S((experts, dense_rows)),
            S((1, dense_rows)),
            S((1, dense_rows)),
            S(other.shape[1:]),
            S(other.shape[1:]),
        ],
        compiler_params=pltpu.CompilerParams(vmem_limit_bytes=LARGE),
        cost_estimate=cost(5),
        name="deliver",
    )(sel, ga, other, tokens, grads, total)


def local(
    activations, qkv_weight, attn_weight, router_weight, gain_one, gain_two,
    expert_in, expert_out, segments, task_ids, task_experts, out_grad,
):
    packs, length, width = activations.shape
    planes = lax.axis_size("seq")
    groups = lax.axis_size("dp")
    cuts = 2 * packs
    assert cuts == planes == 4 and groups % 2 == 0
    piece = length // 2
    experts = router_weight.shape[1]
    hidden = expert_in.shape[0]
    assert experts + 2 <= TINY
    zeros = jnp.zeros((TINY - experts - 2, qkv_weight.shape[0]), LOW)
    tiny = jnp.concatenate([router_weight.T, gain_one[None], gain_two[None], zeros])
    tokens, grads, total, other, expert_grads, _, _, sel = layer(
        task_experts.T,
        activations.reshape(cuts, piece, width),
        segments,
        out_grad.reshape(cuts, piece, width),
        qkv_weight,
        attn_weight,
        tiny,
        task_ids,
        expert_in.reshape(hidden * experts, width),
        expert_out.reshape(hidden * experts, width),
        groups,
        planes,
        experts,
    )
    outputs, input_grad, qkv_grad, attn_grad, router_grad, first, second, win_grad, wout_grad = (
        deliver(
            sel,
            expert_grads,
            other.reshape(2, -1, width)[:, : hidden * experts],
            tokens,
            grads,
            total,
            experts,
        )
    )
    return (
        outputs.reshape(packs, length, width),
        input_grad.reshape(packs, length, width),
        qkv_grad,
        attn_grad,
        router_grad.T,
        first.reshape(-1),
        second.reshape(-1),
        win_grad.reshape(expert_in.shape),
        wout_grad.reshape(expert_in.shape),
    )


def solution(mesh):
    placed = (
        P("dp", "seq", None),
        P("dp", None),
        P("dp", None),
        P("dp", None),
        P("dp"),
        P("dp"),
        P(("dp", "seq"), None, None),
        P(("dp", "seq"), None, None),
        P("dp", "seq"),
        P("dp", "seq"),
        P(),
        P("dp", "seq", None),
    )
    return jax.shard_map(
        local,
        mesh=mesh,
        in_specs=placed,
        out_specs=(
            P("dp", "seq", None),
            P("dp", "seq", None),
            P("dp", None),
            P("dp", None),
            P("dp", None),
            P("dp"),
            P("dp"),
            P(("dp", "seq"), None, None),
            P(("dp", "seq"), None, None),
        ),
        check_vma=False,
    )
```
